512 devices in a mesh: dp: 4 (over y_lo), tile: 128 (over y_hi, x, z, core).
Axes of the slice: x: 4, y: 8 (y_hi: 2, y_lo: 4; y = y_hi * 4 + y_lo), z: 8, core: 2. Of those that a mesh axis runs over, the one named last changes fastest.
Arguments:
- features: bfloat16 [8, 256, 8, 64, 64], P('dp', 'tile'), may hold values from -6 to 6
- occupancy: int32 [8, 256, 8, 64], P('dp', 'tile'), may hold values 0 or 1
- brick_slots: int32 [8, 256], P('dp', 'tile'), may hold values from 0 to 3, as said below
- conv1_weight: bfloat16 [64, 1728], replicated, may hold values from -0.3125 to 0.3125
- down_weight: bfloat16 [128, 512], replicated, may hold values from -0.5 to 0.5
- conv2_weight: bfloat16 [128, 3456], replicated, may hold values from -0.109375 to 0.109375
- upstream: bfloat16 [8, 256, 4, 16, 128], P('dp', 'tile'), may hold values from -6 to 6
Outputs:
- section_output: bfloat16 [8, 256, 4, 16, 128], P('dp', 'tile')
- conv1_grad: float32 [64, 1728], replicated
- down_grad: float32 [128, 512], replicated
- conv2_grad: float32 [128, 3456], replicated
The draws below stay inside these ranges and needn't reach their ends.
Inputs may be any that keep to these rules, and one draw needn't show every extreme that they name: `brick_slots`: the k-th brick of each tile lies in brick column k of the tile: its slot is k * 2 plus its brick row.
All inputs are finite; a program needn't handle non-finite values. No bound on the sum of `occupancy` on one device may be relied on, other than what follows from the above.
Results may differ from the reference program's by a relative error of at most 0.0075.
Values may be sent and summed in bfloat16 or wider, within the bound.
A program may use at most 64 MiB of HBM per device.

```python
import jax
import jax.numpy as jnp
from jax import lax

FINE_CH = 64
COARSE_CH = 128
BRICK = 8
TILE_X = 2
TILE_BRICK_ROWS = 2
HALF_BRICK = 4
PLANE = 64
COARSE_PLANE = 16
BRICKS = 256
SCENES = 8
N_TILE = 128


def draw_brick_slots(key, part):
    key = jax.random.fold_in(key, 7)
    rows = jax.random.randint(key, (SCENES, N_TILE, TILE_X), 0, TILE_BRICK_ROWS, dtype=jnp.int32)
    columns = jnp.arange(TILE_X, dtype=jnp.int32) * TILE_BRICK_ROWS
    return (rows + columns[None, None, :]).reshape(SCENES, N_TILE * TILE_X)


def plant(entries, own_key, least, top_value):
    spot = [jax.random.randint(jax.random.fold_in(own_key, axis), (), 0, length) for axis, length in enumerate(entries.shape)]
    longest = entries.shape.index(max(entries.shape))
    next_to = spot[:longest] + [(spot[longest] + 1) % entries.shape[longest]] + spot[longest + 1:]
    return entries.at[tuple(spot)].set(least).at[tuple(next_to)].set(top_value)


def shard_levels(stream_key, extent, cuts, low, high):
    factor_of, own = 1.0, jax.random.fold_in(stream_key, 6)
    for axis_at, shards_of in cuts:
        draws = jnp.exp(jax.random.uniform(jax.random.fold_in(own, axis_at), (shards_of,), jnp.float32, low / len(cuts), high / len(cuts)))
        factor_of = factor_of * jnp.repeat(draws, extent[axis_at] // shards_of).reshape([-1 if axis == axis_at else 1 for axis in range(len(extent))])
    return factor_of


def centred(stream_key, dims, deviation, bound, shards=(), kind=jnp.bfloat16):
    entries = deviation * jax.random.normal(stream_key, dims, jnp.float32)
    if shards:
        entries = entries * shard_levels(stream_key, dims, shards, -0.22, 0.18)
    return jnp.clip(entries, -bound, bound).astype(kind)


def setup_inputs(seed: int = 0) -> dict:
    key_of = jax.random.split(jax.random.key(seed), 8)
    return {
        "features": centred(key_of[0], (SCENES, BRICKS, BRICK, FINE_CH, PLANE), 1.0, 6.0, ((0, 4), (1, 128))),
        "occupancy": plant((jax.random.randint(key_of[1], (SCENES, BRICKS, BRICK, PLANE), 0, 4) < 1).astype(jnp.int32), jax.random.fold_in(key_of[1], 1), 0, 1),
        "brick_slots": draw_brick_slots(jax.random.fold_in(key_of[7], 71), 0),
        "conv1_weight": centred(key_of[3], (FINE_CH, 27 * FINE_CH), (27 * FINE_CH // 4) ** -0.5, 0.3125),
        "down_weight": centred(key_of[4], (COARSE_CH, 8 * FINE_CH), (2 * FINE_CH) ** -0.5, 0.5),
        "conv2_weight": centred(key_of[5], (COARSE_CH, 27 * COARSE_CH), (27 * COARSE_CH) ** -0.5, 0.109375),
        "upstream": centred(key_of[6], (SCENES, BRICKS, HALF_BRICK, COARSE_PLANE, COARSE_CH), 1.0, 6.0, ((0, 4), (1, 128))),
    }


def build_grid(bricks, slots, tile_x, tile_y, channels_last):
    scenes, active, side = bricks.shape[0], bricks.shape[1], bricks.shape[2]
    slot_ids = jnp.arange(tile_x * tile_y, dtype=jnp.int32)
    picks = (slots[:, :, None] == slot_ids[None, None, :]).astype(bricks.dtype)
    layout = (scenes, tile_x * tile_y) + (1,) * (bricks.ndim - 2)
    dense = None
    for index in range(active):
        term = picks[:, index].reshape(layout) * bricks[:, index][:, None]
        dense = term if dense is None else dense + term
    if channels_last:
        dense = dense.reshape(scenes, tile_x, tile_y, side, side, side, dense.shape[-1])
        dense = jnp.transpose(dense, (0, 1, 3, 2, 4, 5, 6))
        return dense.reshape(scenes, tile_x * side, tile_y * side, side, dense.shape[-1])
    channels = dense.shape[3]
    dense = dense.reshape(scenes, tile_x, tile_y, side, channels, side, side)
    dense = jnp.transpose(dense, (0, 1, 3, 4, 2, 5, 6))
    return dense.reshape(scenes, tile_x * side, channels, tile_y * side, side)


def extract_bricks(padded, slots, tile_y, side, channels_last):
    y_axis = 2 if channels_last else 3
    widths = [(0, 0)] * padded.ndim
    widths[y_axis] = (1, 1)
    padded = jnp.pad(padded, widths)

    def single(grid, slot):
        starts = [jnp.zeros((), jnp.int32)] * grid.ndim
        starts[0] = (slot // tile_y) * side
        starts[y_axis - 1] = (slot % tile_y) * side
        sizes = list(grid.shape)
        sizes[0] = side + 2
        sizes[y_axis - 1] = side + 2
        return lax.dynamic_slice(grid, starts, sizes)

    pieces = [jax.vmap(single)(padded, slots[:, index]) for index in range(slots.shape[1])]
    joined = jnp.stack(pieces, axis=1)
    count = joined.shape[0] * joined.shape[1]
    if channels_last:
        return joined.reshape(count, side + 2, (side + 2) * side, joined.shape[-1])
    return joined.reshape(count, side + 2, joined.shape[3], (side + 2) * side)


def stack_depth(values, flattened_axis, join_axis, side):
    length = values.shape[flattened_axis]
    depth = jnp.arange(length, dtype=jnp.int32) % side
    layout = [1] * values.ndim
    layout[flattened_axis] = length
    lower_boundary = (depth >= 1).astype(values.dtype).reshape(layout)
    upper_edge = (depth <= side - 2).astype(values.dtype).reshape(layout)
    widths = [(0, 0)] * values.ndim
    widths[flattened_axis] = (1, 1)
    padded = jnp.pad(values, widths)
    below = lax.slice_in_dim(padded, 0, length, axis=flattened_axis) * lower_boundary
    above = lax.slice_in_dim(padded, 2, length + 2, axis=flattened_axis) * upper_edge
    return jnp.concatenate([below, values, above], axis=join_axis)


def apply_taps(stacked, weight, side, flattened_axis, form):
    shaped = weight.astype(jnp.float32).reshape(weight.shape[0], 3, 3, -1)
    stacked = stacked.astype(jnp.float32)
    summed = None
    for step_x in range(3):
        rows = lax.slice_in_dim(stacked, step_x, step_x + side, axis=1)
        for step_y in range(3):
            window = lax.slice_in_dim(rows, step_y * side, step_y * side + side * side, axis=flattened_axis)
            contrib = jnp.einsum(form, window, shaped[:, step_x, step_y])
            summed = contrib if summed is None else summed + contrib
    return summed


def tap_gradient(grad_out, stacked, side, flattened_axis, form):
    grad_wide = grad_out.astype(jnp.float32)
    stacked = stacked.astype(jnp.float32)
    blocks = []
    for step_x in range(3):
        rows = lax.slice_in_dim(stacked, step_x, step_x + side, axis=1)
        for step_y in range(3):
            window = lax.slice_in_dim(rows, step_y * side, step_y * side + side * side, axis=flattened_axis)
            blocks.append(jnp.einsum(form, grad_wide, window))
    joined = jnp.stack(blocks, axis=1)
    return joined.reshape(joined.shape[0], -1)


def flip_weight(weight, in_channels):
    shaped = weight.reshape(weight.shape[0], 27, in_channels)[:, ::-1, :]
    return jnp.transpose(shaped, (2, 1, 0)).reshape(in_channels, 27 * weight.shape[0])


def silu_slope(pre_act):
    sig_gate = jax.nn.sigmoid(pre_act)
    return sig_gate * (1.0 + pre_act * (1.0 - sig_gate))


def child_selections(grid_side):
    half_side = grid_side // 2
    fine_index = jnp.arange(grid_side * grid_side, dtype=jnp.int32)
    coarse_index = jnp.arange(half_side * half_side, dtype=jnp.int32)
    lookup_tables = []
    for step_y in range(2):
        for step_z in range(2):
            target = (2 * (coarse_index // half_side) + step_y) * grid_side + 2 * (coarse_index % half_side) + step_z
            lookup_tables.append((fine_index[:, None] == target[None, :]).astype(jnp.bfloat16))
    return lookup_tables


def gather_child_voxels(fine_activation, lookup_tables):
    pieces = []
    for step_x in range(2):
        x_rows = fine_activation[:, step_x::2].astype(jnp.float32)
        for picker in lookup_tables:
            pieces.append(jnp.einsum("bxcv,vw->bxwc", x_rows, picker.astype(jnp.float32)).astype(jnp.bfloat16))
    return jnp.concatenate(pieces, axis=3)


def coarse_occupancy(fine_mask, lookup_tables):
    largest = None
    for step_x in range(2):
        for picker in lookup_tables:
            chosen = jnp.einsum("bxv,vw->bxw", fine_mask[:, step_x::2], picker.astype(jnp.float32), precision=lax.Precision.HIGHEST)
            largest = chosen if largest is None else jnp.maximum(largest, chosen)
    return largest


def spread_gradient(coarse_grad, down_weight, lookup_tables, fine_channels):
    shaped = down_weight.astype(jnp.float32).reshape(down_weight.shape[0], 8, fine_channels)
    spreads = [jnp.einsum("bxwo,vw->bxov", coarse_grad.astype(jnp.float32), picker.astype(jnp.float32)).astype(jnp.bfloat16) for picker in lookup_tables]
    rows_out = []
    for step_x in range(2):
        summed = None
        for index_yz in range(4):
            contrib = jnp.einsum("bxov,oc->bxcv", spreads[index_yz].astype(jnp.float32), shaped[:, step_x * 4 + index_yz])
            summed = contrib if summed is None else summed + contrib
        rows_out.append(summed)
    joined = jnp.stack(rows_out, axis=2)
    return joined.reshape(joined.shape[0], -1, joined.shape[3], joined.shape[4])


def tile_rows(whole, index):
    clamped = jnp.clip(index, 0, N_TILE - 1).astype(jnp.int32)
    return lax.dynamic_slice_in_dim(whole, clamped * TILE_X, TILE_X, axis=1)


def padded_grid(make_rows, brick_slots, index, channels_last):
    def grid_at(position):
        inside = jnp.logical_and(position >= 0, position < N_TILE).astype(jnp.bfloat16)
        return build_grid(make_rows(position), tile_rows(brick_slots, position), TILE_X, TILE_BRICK_ROWS, channels_last) * inside

    own = grid_at(index)
    left = grid_at(index - 1)
    right = grid_at(index + 1)
    return jnp.concatenate([left[:, -1:], own, right[:, :1]], axis=1)


def coarse_stack_of(whole, brick_slots, index):
    half_side = BRICK // 2

    def make_rows(position):
        return tile_rows(whole, position)

    padded = padded_grid(make_rows, brick_slots, index, True)
    return stack_depth(extract_bricks(padded, tile_rows(brick_slots, index), TILE_BRICK_ROWS, half_side, True), 2, 3, half_side)


def fine_forward(features, occupancy, brick_slots, conv1_weight, down_weight, index):
    side = BRICK

    def make_masked(position):
        gate = tile_rows(occupancy, position).astype(jnp.float32)[:, :, :, None, :]
        return (tile_rows(features, position).astype(jnp.float32) * gate).astype(jnp.bfloat16)

    padded = padded_grid(make_masked, brick_slots, index, False)
    fine_stack = stack_depth(extract_bricks(padded, tile_rows(brick_slots, index), TILE_BRICK_ROWS, side, False), 3, 2, side)
    fine_pre = apply_taps(fine_stack, conv1_weight, side, 3, "bxkv,ok->bxov")
    fine_mask = tile_rows(occupancy, index).astype(jnp.float32).reshape(-1, side, side * side)
    fine_activation = (jax.nn.silu(fine_pre) * fine_mask[:, :, None, :]).astype(jnp.bfloat16)
    lookup_tables = child_selections(side)
    child_voxels = gather_child_voxels(fine_activation, lookup_tables)
    coarse_gate = coarse_occupancy(fine_mask, lookup_tables)[..., None]
    down_pre = jnp.einsum("bxwk,ok->bxwo", child_voxels.astype(jnp.float32), down_weight.astype(jnp.float32))
    coarse_act = (jax.nn.silu(down_pre) * coarse_gate).astype(jnp.bfloat16)
    return fine_stack, fine_pre, fine_mask, child_voxels, coarse_gate, down_pre, coarse_act


def join_tiles(mapped):
    moved = jnp.moveaxis(mapped, 0, 1)
    return moved.reshape((moved.shape[0], moved.shape[1] * moved.shape[2]) + moved.shape[3:])


def reference(features, occupancy, brick_slots, conv1_weight, down_weight, conv2_weight, upstream):
    half_side = BRICK // 2
    scenes = features.shape[0]
    tile_ids = jnp.arange(N_TILE, dtype=jnp.int32)
    tile_shape = (scenes, TILE_X, half_side, half_side * half_side, COARSE_CH)
    lookup_tables = child_selections(BRICK)

    def forward_tile(index):
        return fine_forward(features, occupancy, brick_slots, conv1_weight, down_weight, index)[-1].reshape(tile_shape)

    coarse_all = join_tiles(lax.map(forward_tile, tile_ids))

    def coarse_tile(index):
        stack = coarse_stack_of(coarse_all, brick_slots, index)
        coarse_pre = apply_taps(stack, conv2_weight, half_side, 2, "bxvk,ok->bxvo")
        fine_mask = tile_rows(occupancy, index).astype(jnp.float32).reshape(-1, BRICK, BRICK * BRICK)
        coarse_gate = coarse_occupancy(fine_mask, lookup_tables)[..., None]
        out_rows = (jax.nn.silu(coarse_pre) * coarse_gate).astype(jnp.bfloat16)
        up_rows = tile_rows(upstream, index).reshape((-1,) + upstream.shape[2:]).astype(jnp.float32)
        grad_rows = (up_rows * coarse_gate * silu_slope(coarse_pre)).astype(jnp.bfloat16)
        return out_rows.reshape(tile_shape), grad_rows.reshape(tile_shape)

    out_tiles, grad_tiles = lax.map(coarse_tile, tile_ids)
    section_output = join_tiles(out_tiles)
    grad_all = join_tiles(grad_tiles)
    flipped = flip_weight(conv2_weight, COARSE_CH)

    def backward_tile(carry, index):
        fine_stack, fine_pre, fine_mask, child_voxels, coarse_gate, down_pre, coarse_act = fine_forward(features, occupancy, brick_slots, conv1_weight, down_weight, index)
        act_stack = coarse_stack_of(coarse_all, brick_slots, index)
        grad_rows = tile_rows(grad_all, index).reshape((-1,) + grad_all.shape[2:])
        conv2_term = tap_gradient(grad_rows, act_stack, half_side, 2, "bxvo,bxvk->ok")
        grad_stack = coarse_stack_of(grad_all, brick_slots, index)
        down_back = apply_taps(grad_stack, flipped, half_side, 2, "bxvk,ok->bxvo")
        down_grad_in = (down_back * coarse_gate * silu_slope(down_pre)).astype(jnp.bfloat16)
        down_term = jnp.einsum("bxwo,bxwk->ok", down_grad_in.astype(jnp.float32), child_voxels.astype(jnp.float32))
        fine_back = spread_gradient(down_grad_in, down_weight, lookup_tables, FINE_CH)
        fine_grad = (fine_back * fine_mask[:, :, None, :] * silu_slope(fine_pre)).astype(jnp.bfloat16)
        conv1_term = tap_gradient(fine_grad, fine_stack, BRICK, 3, "bxov,bxkv->ok")
        return (carry[0] + conv1_term, carry[1] + down_term, carry[2] + conv2_term), None

    start = (jnp.zeros(conv1_weight.shape, jnp.float32), jnp.zeros(down_weight.shape, jnp.float32), jnp.zeros(conv2_weight.shape, jnp.float32))
    totals, unused = lax.scan(backward_tile, start, tile_ids)
    scale = 1.0 / (scenes * N_TILE * TILE_X)
    return section_output, totals[0] * scale, totals[1] * scale, totals[2] * scale
```

```python
import jax
import jax.numpy as jnp
from jax import lax
from jax.experimental import pallas as pl
from jax.experimental.pallas import tpu as pltpu
from jax.sharding import PartitionSpec as P

FINE_CH = 64
COARSE_CH = 128
TILE_X = 2
TILE_BRICK_ROWS = 2


AXES = {"c": 2, "x": 4, "y": 8, "z": 8}
STAGES = {
    "x": (("rs", "c"), ("rs", "x"), ("rs", "y"), ("ar", "z"), ("ag", "y"), ("ag", "x"), ("ag", "c")),
    "y": (("rs", "c"), ("rs", "y"), ("rs", "x"), ("ar", "z"), ("ag", "x"), ("ag", "y"), ("ag", "c")),
    "z": (("rs", "c"), ("rs", "z"), ("rs", "x"), ("ar", "y"), ("ag", "x"), ("ag", "z"), ("ag", "c")),
}


Y_LOW = 4


def place():
    dp, tile = lax.axis_index("dp"), lax.axis_index("tile")
    c, x, z = AXES["c"], AXES["x"], AXES["z"]
    return {
        "c": lax.rem(tile, c),
        "z": lax.rem(lax.div(tile, c), z),
        "x": lax.rem(lax.div(tile, c * z), x),
        "y": lax.div(tile, c * z * x) * Y_LOW + dp,
    }


def device(at):
    c, x, z = AXES["c"], AXES["x"], AXES["z"]
    tile = ((lax.div(at["y"], Y_LOW) * x + at["x"]) * z + at["z"]) * c + at["c"]
    return {"dp": lax.rem(at["y"], Y_LOW), "tile": tile}


def peer(at, axis, step):
    moved = dict(at)
    moved[axis] = lax.rem(at[axis] + step, AXES[axis])
    return device(moved)


class Chain:
    def __init__(self, order, own, result, landing, held, send, recv, at):
        self.stages, self.at = STAGES[order], at
        self.own, self.result, self.landing, self.held = own, result, landing, held
        self.send, self.recv = send, recv
        self.copies = {}

    @staticmethod
    def sizes(order, tiles):
        landing, held = [], []
        for kind, axis in STAGES[order]:
            if kind == "rs":
                tiles //= AXES[axis]
                landing.append((AXES[axis] - 1, tiles))
                held.append(tiles)
            elif kind == "ar":
                landing.append((AXES[axis], tiles))
        return landing, held

    def source(self, stage):
        return self.own if stage == 0 else self.held[stage - 1]

    def offset(self, stages):
        first = 0
        for stage in range(stages):
            first = first + self.at[self.stages[stage][1]] * self.held[stage].shape[0]
        return first

    def start(self, stage):
        kind, axis = self.stages[stage]
        count = AXES[axis]
        for step in range(1, count):
            if kind == "rs":
                part = self.held[stage].shape[0]
                to = lax.rem(self.at[axis] + step, count)
                src = self.source(stage).at[pl.ds(to * part, part)]
                dst = self.landing[stage].at[step - 1]
            elif kind == "ar":
                src = self.source(stage)
                dst = self.landing[stage].at[self.at[axis]]
            else:
                back = len(self.stages) - 1 - stage
                part = self.held[back].shape[0]
                where = pl.ds(self.offset(back + 1), part)
                src = dst = self.result.at[where]
            copy = pltpu.make_async_remote_copy(
                src_ref=src, dst_ref=dst,
                send_sem=self.send.at[stage, step - 1], recv_sem=self.recv.at[stage, step - 1],
                device_id=peer(self.at, axis, step), device_id_type=pl.DeviceIdType.MESH,
            )
            copy.start()
            self.copies[stage, step] = copy

    def finish(self, stage):
        kind, axis = self.stages[stage]
        count = AXES[axis]
        for step in range(1, count):
            if kind == "ag":
                back = len(self.stages) - 1 - stage
                part = self.held[back].shape[0]
                origin = dict(self.at)
                origin[axis] = lax.rem(self.at[axis] + count - step, count)
                first = 0
                for earlier in range(back + 1):
                    first = first + origin[self.stages[earlier][1]] * self.held[earlier].shape[0]
                dst = self.result.at[pl.ds(first, part)]
            elif kind == "rs":
                dst = self.landing[stage].at[step - 1]
            else:
                dst = self.landing[stage].at[lax.rem(self.at[axis] + count - step, count)]
            pltpu.make_async_remote_copy(
                src_ref=dst, dst_ref=dst,
                send_sem=self.send.at[stage, step - 1], recv_sem=self.recv.at[stage, step - 1],
                device_id=peer(self.at, axis, step), device_id_type=pl.DeviceIdType.MESH,
            ).wait_recv()
        if kind == "rs":
            part = self.held[stage].shape[0]
            mine = self.source(stage)[pl.ds(self.at[axis] * part, part)]
            total = mine.astype(jnp.float32)
            for step in range(1, count):
                total = total + self.landing[stage][step - 1].astype(jnp.float32)
            self.held[stage][...] = total.astype(jnp.bfloat16)
        elif kind == "ar":
            self.landing[stage][self.at[axis]] = self.source(stage)[...]
            total = self.landing[stage][0].astype(jnp.float32)
            for index in range(1, count):
                total = total + self.landing[stage][index].astype(jnp.float32)
            self.result[pl.ds(self.offset(stage), total.shape[0])] = total.astype(jnp.bfloat16)

    def close(self):
        for copy in self.copies.values():
            copy.wait_send()


CHAINS = (("x", 0, 128), ("y", 128, 64), ("z", 192, 64), ("x", 256, 64))


def greet(at):
    barrier = pltpu.get_barrier_semaphore()
    met = 0
    for axis, count in AXES.items():
        for step in range(1, count):
            pl.semaphore_signal(barrier, inc=1, device_id=peer(at, axis, step), device_id_type=pl.DeviceIdType.MESH)
            met += 1
    pl.semaphore_wait(barrier, met)


def reduce_kernel(parts_ref, total_ref, *scratch):
    at = place()
    chains, scratch = [], list(scratch)
    send, recv = scratch.pop(), scratch.pop()
    for index, (order, first, tiles) in enumerate(CHAINS):
        landing = [scratch.pop(0) for _ in range(4)]
        held = [scratch.pop(0) for _ in range(3)]
        where = pl.ds(first, tiles)
        chains.append(Chain(order, parts_ref.at[where], total_ref.at[where], landing, held, send.at[index], recv.at[index], at))
    greet(at)
    stages = len(STAGES["x"])
    for stage in range(stages):
        for chain in chains:
            if stage:
                chain.finish(stage - 1)
            chain.start(stage)
    for chain in chains:
        chain.finish(stages - 1)
    for chain in chains:
        chain.close()


def reduce_all(parts):
    tile = parts.shape[1:]
    scratch = []
    for order, first, tiles in CHAINS:
        landing, held = Chain.sizes(order, tiles)
        scratch += [pltpu.VMEM(size + tile, jnp.bfloat16) for size in landing]
        scratch += [pltpu.VMEM((size,) + tile, jnp.bfloat16) for size in held]
    scratch += [pltpu.SemaphoreType.DMA((len(CHAINS), 7, 7))] * 2
    return pl.pallas_call(
        reduce_kernel,
        out_shape=jax.ShapeDtypeStruct(parts.shape, jnp.bfloat16),
        in_specs=[pl.BlockSpec(memory_space=pltpu.VMEM)],
        out_specs=pl.BlockSpec(memory_space=pltpu.VMEM),
        scratch_shapes=scratch,
        compiler_params=pltpu.CompilerParams(collective_id=0, has_side_effects=True, vmem_limit_bytes=40 * 2**20),
    )(parts)


def to_tiles(matrix):
    rows, columns = matrix.shape
    return matrix.reshape(rows // 16, 16, columns // 128, 128).transpose(0, 2, 1, 3).reshape(-1, 16, 128)


def from_tiles(tiles, rows):
    columns = tiles.shape[0] // (rows // 16)
    return tiles.reshape(rows // 16, columns, 16, 128).transpose(0, 2, 1, 3).reshape(rows, columns * 128)


def padded_2(cells, sides, width):
    for axis, dim in sides:
        count = lax.axis_size(axis)
        ends = count - 1
        head = lax.slice_in_dim(cells, 0, width, axis=dim)
        tail = lax.slice_in_dim(cells, cells.shape[dim] - width, cells.shape[dim], axis=dim)
        cells = jnp.concatenate(
            [
                lax.ppermute(tail, axis, [(i, (i + 1) % count) for i in range(ends)]),
                cells,
                lax.ppermute(head, axis, [((i + 1) % count, i) for i in range(ends)]),
            ],
            axis=dim,
        )
    return cells


def build_grid(bricks, slots, tile_x, tile_y, channels_last):
    scenes, active, side = (bricks.shape[0], bricks.shape[1], bricks.shape[2])
    slot_ids = jnp.arange(tile_x * tile_y, dtype=jnp.int32)
    picks = (slots[:, :, None] == slot_ids[None, None, :]).astype(bricks.dtype)
    layout = (scenes, tile_x * tile_y) + (1,) * (bricks.ndim - 2)
    dense = None
    for index in range(active):
        term = picks[:, index].reshape(layout) * bricks[:, index][:, None]
        dense = term if dense is None else dense + term
    if channels_last:
        dense = dense.reshape(scenes, tile_x, tile_y, side, side, side, dense.shape[-1])
        dense = jnp.transpose(dense, (0, 1, 3, 2, 4, 5, 6))
        return dense.reshape(scenes, tile_x * side, tile_y * side, side, dense.shape[-1])
    channels = dense.shape[3]
    dense = dense.reshape(scenes, tile_x, tile_y, side, channels, side, side)
    dense = jnp.transpose(dense, (0, 1, 3, 4, 2, 5, 6))
    return dense.reshape(scenes, tile_x * side, channels, tile_y * side, side)


def extract_bricks(padded, slots, tile_y, side, channels_last):
    y_axis = 2 if channels_last else 3
    widths = [(0, 0)] * padded.ndim
    widths[y_axis] = (1, 1)
    padded = jnp.pad(padded, widths)

    def single(grid, slot):
        starts = [jnp.zeros((), jnp.int32)] * grid.ndim
        starts[0] = slot // tile_y * side
        starts[y_axis - 1] = slot % tile_y * side
        sizes = list(grid.shape)
        sizes[0] = side + 2
        sizes[y_axis - 1] = side + 2
        return lax.dynamic_slice(grid, starts, sizes)

    pieces = [jax.vmap(single)(padded, slots[:, index]) for index in range(slots.shape[1])]
    joined = jnp.stack(pieces, axis=1)
    count = joined.shape[0] * joined.shape[1]
    if channels_last:
        return joined.reshape(count, side + 2, (side + 2) * side, joined.shape[-1])
    return joined.reshape(count, side + 2, joined.shape[3], (side + 2) * side)


def stack_depth(values, flattened_axis, join_axis, side):
    length = values.shape[flattened_axis]
    depth = jnp.arange(length, dtype=jnp.int32) % side
    layout = [1] * values.ndim
    layout[flattened_axis] = length
    lower_boundary = (depth >= 1).astype(values.dtype).reshape(layout)
    upper_edge = (depth <= side - 2).astype(values.dtype).reshape(layout)
    widths = [(0, 0)] * values.ndim
    widths[flattened_axis] = (1, 1)
    padded = jnp.pad(values, widths)
    below = lax.slice_in_dim(padded, 0, length, axis=flattened_axis) * lower_boundary
    above = lax.slice_in_dim(padded, 2, length + 2, axis=flattened_axis) * upper_edge
    return jnp.concatenate([below, values, above], axis=join_axis)


def apply_taps(stacked, weight, side, flattened_axis, form):
    shaped = weight.reshape(weight.shape[0], 3, 3, -1)
    summed = None
    for step_x in range(3):
        rows = lax.slice_in_dim(stacked, step_x, step_x + side, axis=1)
        for step_y in range(3):
            window = lax.slice_in_dim(
                rows, step_y * side, step_y * side + side * side, axis=flattened_axis
            )
            contrib = jnp.einsum(
                form, window, shaped[:, step_x, step_y], preferred_element_type=jnp.float32
            )
            summed = contrib if summed is None else summed + contrib
    return summed


def tap_gradient(grad_out, stacked, side, flattened_axis, form):
    blocks = []
    for step_x in range(3):
        rows = lax.slice_in_dim(stacked, step_x, step_x + side, axis=1)
        for step_y in range(3):
            window = lax.slice_in_dim(
                rows, step_y * side, step_y * side + side * side, axis=flattened_axis
            )
            blocks.append(jnp.einsum(form, grad_out, window, preferred_element_type=jnp.float32))
    joined = jnp.stack(blocks, axis=1)
    return joined.reshape(joined.shape[0], -1)


def flip_weight(weight, in_channels):
    shaped = weight.reshape(weight.shape[0], 27, in_channels)[:, ::-1, :]
    return jnp.transpose(shaped, (2, 1, 0)).reshape(in_channels, 27 * weight.shape[0])


def silu_slope(pre_act):
    sig_gate = jax.nn.sigmoid(pre_act)
    return sig_gate * (1.0 + pre_act * (1.0 - sig_gate))


def child_selections(grid_side):
    half_side = grid_side // 2
    fine_index = jnp.arange(grid_side * grid_side, dtype=jnp.int32)
    coarse_index = jnp.arange(half_side * half_side, dtype=jnp.int32)
    lookup_tables = []
    for step_y in range(2):
        for step_z in range(2):
            target = (
                (2 * (coarse_index // half_side) + step_y) * grid_side
                + 2 * (coarse_index % half_side)
                + step_z
            )
            lookup_tables.append((fine_index[:, None] == target[None, :]).astype(jnp.bfloat16))
    return lookup_tables


def gather_child_voxels(fine_activation, lookup_tables):
    pieces = []
    for step_x in range(2):
        x_rows = fine_activation[:, step_x::2]
        for picker in lookup_tables:
            pieces.append(
                jnp.einsum(
                    "bxcv,vw->bxwc", x_rows, picker, preferred_element_type=jnp.float32
                ).astype(jnp.bfloat16)
            )
    return jnp.concatenate(pieces, axis=3)


def coarse_occupancy(fine_mask, lookup_tables):
    largest = None
    for step_x in range(2):
        for picker in lookup_tables:
            chosen = jnp.einsum(
                "bxv,vw->bxw",
                fine_mask[:, step_x::2],
                picker.astype(jnp.float32),
                precision=lax.Precision.HIGHEST,
            )
            largest = chosen if largest is None else jnp.maximum(largest, chosen)
    return largest


def spread_gradient(coarse_grad, down_weight, lookup_tables, fine_channels):
    shaped = down_weight.reshape(down_weight.shape[0], 8, fine_channels)
    spreads = [
        jnp.einsum("bxwo,vw->bxov", coarse_grad, picker, preferred_element_type=jnp.float32).astype(
            jnp.bfloat16
        )
        for picker in lookup_tables
    ]
    rows_out = []
    for step_x in range(2):
        summed = None
        for index_yz in range(4):
            contrib = jnp.einsum(
                "bxov,oc->bxcv",
                spreads[index_yz],
                shaped[:, step_x * 4 + index_yz],
                preferred_element_type=jnp.float32,
            )
            summed = contrib if summed is None else summed + contrib
        rows_out.append(summed)
    joined = jnp.stack(rows_out, axis=2)
    return joined.reshape(joined.shape[0], -1, joined.shape[3], joined.shape[4])


def per_device(features, occupancy, brick_slots, conv1_weight, down_weight, conv2_weight, upstream):
    scenes, active, side = (features.shape[0], features.shape[1], features.shape[2])
    half_side = side // 2
    count = scenes * active
    coarse_shape = (scenes, active, half_side, half_side * half_side, upstream.shape[-1])
    masked = (features * occupancy.astype(jnp.float32)[:, :, :, None, :]).astype(jnp.bfloat16)
    fine_grid = build_grid(masked, brick_slots, TILE_X, TILE_BRICK_ROWS, False)
    fine_pad = padded_2(fine_grid, (("tile", 1),), 1)
    fine_stack = stack_depth(
        extract_bricks(fine_pad, brick_slots, TILE_BRICK_ROWS, side, False), 3, 2, side
    )
    fine_pre = apply_taps(fine_stack, conv1_weight, side, 3, "bxkv,ok->bxov")
    fine_mask = occupancy.astype(jnp.float32).reshape(count, side, side * side)
    fine_gate = fine_mask[:, :, None, :]
    fine_activation = (jax.nn.silu(fine_pre) * fine_gate).astype(jnp.bfloat16)
    lookup_tables = child_selections(side)
    child_voxels = gather_child_voxels(fine_activation, lookup_tables)
    coarse_gate = coarse_occupancy(fine_mask, lookup_tables)[..., None]
    down_pre = jnp.einsum(
        "bxwk,ok->bxwo", child_voxels, down_weight, preferred_element_type=jnp.float32
    )
    coarse_act = (jax.nn.silu(down_pre) * coarse_gate).astype(jnp.bfloat16)
    coarse_grid = build_grid(
        coarse_act.reshape(coarse_shape), brick_slots, TILE_X, TILE_BRICK_ROWS, True
    )
    coarse_pad = padded_2(coarse_grid, (("tile", 1),), 1)
    coarse_stack = stack_depth(
        extract_bricks(coarse_pad, brick_slots, TILE_BRICK_ROWS, half_side, True), 2, 3, half_side
    )
    coarse_pre = apply_taps(coarse_stack, conv2_weight, half_side, 2, "bxvk,ok->bxvo")
    section_output = (jax.nn.silu(coarse_pre) * coarse_gate).astype(jnp.bfloat16)
    up_rows = upstream.reshape((count,) + upstream.shape[2:])
    coarse_grad = (up_rows * coarse_gate * silu_slope(coarse_pre)).astype(jnp.bfloat16)
    scale = 1.0 / (scenes * lax.axis_size("dp") * lax.axis_size("tile") * active)
    conv2_term = tap_gradient(coarse_grad, coarse_stack, half_side, 2, "bxvo,bxvk->ok")
    grad_grid = build_grid(
        coarse_grad.reshape(coarse_shape), brick_slots, TILE_X, TILE_BRICK_ROWS, True
    )
    grad_pad = padded_2(grad_grid, (("tile", 1),), 1)
    grad_stack = stack_depth(
        extract_bricks(grad_pad, brick_slots, TILE_BRICK_ROWS, half_side, True), 2, 3, half_side
    )
    down_back = apply_taps(
        grad_stack, flip_weight(conv2_weight, COARSE_CH), half_side, 2, "bxvk,ok->bxvo"
    )
    down_grad_in = (down_back * coarse_gate * silu_slope(down_pre)).astype(jnp.bfloat16)
    down_term = jnp.einsum(
        "bxwo,bxwk->ok", down_grad_in, child_voxels, preferred_element_type=jnp.float32
    )
    fine_back = spread_gradient(down_grad_in, down_weight, lookup_tables, FINE_CH)
    fine_grad = (fine_back * fine_gate * silu_slope(fine_pre)).astype(jnp.bfloat16)
    conv1_term = tap_gradient(fine_grad, fine_stack, side, 3, "bxov,bxkv->ok")
    wide = jnp.concatenate([conv2_term, down_term], axis=1).astype(jnp.bfloat16)
    wide = jnp.pad(wide, ((0, 0), (0, 4096 - wide.shape[1])))
    narrow = jnp.pad(conv1_term.astype(jnp.bfloat16), ((0, 0), (0, 2048 - conv1_term.shape[1])))
    totals = reduce_all(jnp.concatenate([to_tiles(wide), to_tiles(narrow)], axis=0))
    wide = from_tiles(totals[:256], 128).astype(jnp.float32)
    narrow = from_tiles(totals[256:], 64).astype(jnp.float32)
    conv2_total, down_total, conv1_total = wide[:, :3456], wide[:, 3456:3968], narrow[:, :1728]
    return (
        section_output.reshape(coarse_shape),
        conv1_total * scale,
        down_total * scale,
        conv2_total * scale,
    )


def solution(mesh):
    return jax.shard_map(
        per_device,
        mesh=mesh,
        in_specs=(
            P("dp", "tile", None, None, None),
            P("dp", "tile", None, None),
            P("dp", "tile"),
            P(),
            P(),
            P(),
            P("dp", "tile", None, None, None),
        ),
        out_specs=(P("dp", "tile", None, None, None), P(), P(), P()),
        check_vma=False,
    )
```

```python
import functools

import jax
import jax.numpy as jnp
import numpy as np
from jax import lax
from jax.experimental import pallas as pl
from jax.experimental.pallas import tpu as pltpu
from jax.sharding import PartitionSpec as P

FINE = 64
COARSE = 128
MESH = pl.DeviceIdType.MESH

AXES = {"c": 2, "x": 4, "y": 8, "z": 8}
STAGES = {
    "x": (("rs", "c"), ("rs", "x"), ("rs", "y"), ("ar", "z"), ("ag", "y"), ("ag", "x"), ("ag", "c")),
    "y": (("rs", "c"), ("rs", "y"), ("rs", "x"), ("ar", "z"), ("ag", "x"), ("ag", "y"), ("ag", "c")),
    "z": (("rs", "c"), ("rs", "z"), ("rs", "x"), ("ar", "y"), ("ag", "x"), ("ag", "z"), ("ag", "c")),
}


Y_LOW = 4


def place():
    dp, tile = lax.axis_index("dp"), lax.axis_index("tile")
    c, x, z = AXES["c"], AXES["x"], AXES["z"]
    return {
        "c": lax.rem(tile, c),
        "z": lax.rem(lax.div(tile, c), z),
        "x": lax.rem(lax.div(tile, c * z), x),
        "y": lax.div(tile, c * z * x) * Y_LOW + dp,
    }


def device(at):
    c, x, z = AXES["c"], AXES["x"], AXES["z"]
    tile = ((lax.div(at["y"], Y_LOW) * x + at["x"]) * z + at["z"]) * c + at["c"]
    return {"dp": lax.rem(at["y"], Y_LOW), "tile": tile}


def peer(at, axis, step):
    moved = dict(at)
    moved[axis] = lax.rem(at[axis] + step, AXES[axis])
    return device(moved)


class Chain:
    def __init__(self, order, own, result, landing, held, send, recv, at):
        self.stages, self.at = STAGES[order], at
        self.own, self.result, self.landing, self.held = own, result, landing, held
        self.send, self.recv = send, recv
        self.copies = {}

    @staticmethod
    def sizes(order, tiles):
        landing, held = [], []
        for kind, axis in STAGES[order]:
            if kind == "rs":
                tiles //= AXES[axis]
                landing.append((AXES[axis] - 1, tiles))
                held.append(tiles)
            elif kind == "ar":
                landing.append((AXES[axis], tiles))
        return landing, held

    def source(self, stage):
        return self.own if stage == 0 else self.held[stage - 1]

    def offset(self, stages):
        first = 0
        for stage in range(stages):
            first = first + self.at[self.stages[stage][1]] * self.held[stage].shape[0]
        return first

    def start(self, stage):
        kind, axis = self.stages[stage]
        count = AXES[axis]
        for step in range(1, count):
            if kind == "rs":
                part = self.held[stage].shape[0]
                to = lax.rem(self.at[axis] + step, count)
                src = self.source(stage).at[pl.ds(to * part, part)]
                dst = self.landing[stage].at[step - 1]
            elif kind == "ar":
                src = self.source(stage)
                dst = self.landing[stage].at[self.at[axis]]
            else:
                back = len(self.stages) - 1 - stage
                part = self.held[back].shape[0]
                where = pl.ds(self.offset(back + 1), part)
                src = dst = self.result.at[where]
            copy = pltpu.make_async_remote_copy(
                src_ref=src, dst_ref=dst,
                send_sem=self.send.at[stage, step - 1], recv_sem=self.recv.at[stage, step - 1],
                device_id=peer(self.at, axis, step), device_id_type=MESH,
            )
            copy.start()
            self.copies[stage, step] = copy

    def finish(self, stage):
        kind, axis = self.stages[stage]
        count = AXES[axis]
        for step in range(1, count):
            if kind == "ag":
                back = len(self.stages) - 1 - stage
                part = self.held[back].shape[0]
                origin = dict(self.at)
                origin[axis] = lax.rem(self.at[axis] + count - step, count)
                first = 0
                for earlier in range(back + 1):
                    first = first + origin[self.stages[earlier][1]] * self.held[earlier].shape[0]
                dst = self.result.at[pl.ds(first, part)]
            elif kind == "rs":
                dst = self.landing[stage].at[step - 1]
            else:
                dst = self.landing[stage].at[lax.rem(self.at[axis] + count - step, count)]
            pltpu.make_async_remote_copy(
                src_ref=dst, dst_ref=dst,
                send_sem=self.send.at[stage, step - 1], recv_sem=self.recv.at[stage, step - 1],
                device_id=peer(self.at, axis, step), device_id_type=MESH,
            ).wait_recv()
        if kind == "rs":
            part = self.held[stage].shape[0]
            mine = self.source(stage)[pl.ds(self.at[axis] * part, part)]
            total = mine.astype(jnp.float32)
            for step in range(1, count):
                total = total + self.landing[stage][step - 1].astype(jnp.float32)
            self.held[stage][...] = total.astype(jnp.bfloat16)
        elif kind == "ar":
            self.landing[stage][self.at[axis]] = self.source(stage)[...]
            total = self.landing[stage][0].astype(jnp.float32)
            for index in range(1, count):
                total = total + self.landing[stage][index].astype(jnp.float32)
            self.result[pl.ds(self.offset(stage), total.shape[0])] = total.astype(jnp.bfloat16)

    def close(self):
        for copy in self.copies.values():
            copy.wait_send()

CHAINS = (("x", 0, 128), ("y", 128, 64), ("z", 192, 64), ("x", 256, 64))


def fine_selections():
    kept, after, before = np.zeros((3, 5, 64, 2, 64), np.float32)
    order = np.zeros((64, 64), np.float32)
    for y in range(8):
        for z in range(8):
            row = (y % 2) * 32 + (z % 2) * 16 + (y // 2) * 4 + z // 2
            order[row, y * 8 + z] = 1
            for tap in range(9):
                from_y, from_z = y + tap // 3 - 1, z + tap % 3 - 1
                if 0 <= from_z < 8:
                    into = kept if 0 <= from_y < 8 else after if from_y == 8 else before
                    into[tap // 2, row, tap % 2, (from_y % 8) * 8 + from_z] = 1
    return [np.asarray(table, jnp.bfloat16) for table in (kept.reshape(320, 128), after.reshape(320, 128), before.reshape(320, 128), order)]


def coarse_selections(planes):
    kept, after, before = np.zeros((3, 9, planes, 16, planes, 16), np.float32)
    for y in range(4):
        for z in range(4):
            for tap in range(9):
                from_y, from_z = y + tap // 3 - 1, z + tap % 3 - 1
                if 0 <= from_z < 4:
                    into = kept if 0 <= from_y < 4 else after if from_y == 4 else before
                    for plane in range(planes):
                        into[tap, plane, y * 4 + z, plane, (from_y % 4) * 4 + from_z] = 1
    return [np.asarray(table.reshape(9 * planes * 16, planes * 16), jnp.bfloat16) for table in (kept, after, before)]


def gate_slope(value):
    gate = jax.nn.sigmoid(value)
    return value * gate, gate * (1.0 + value * (1.0 - gate))


def dot(left, right, left_dim, right_dim):
    return lax.dot_general(left, right, (((left_dim,), (right_dim,)), ((), ())), preferred_element_type=jnp.float32)


def section_kernel(
    tiles_in_row,
    slots_ref, features_ref, occupancy_ref, w1_ref, wd_ref, w2_ref, upstream_ref,
    kept1_ref, after1_ref, before1_ref, order_ref, kept2_ref, kept8_ref, after8_ref, before8_ref,
    section_ref, total_ref,
    parts, halo1, halo2, halo3, out1, out2, out3,
    xs, w1p, w2f, mk, slope1, child, grad1, gate2, slope2, act2, edge2, im2, img, grad2,
    halo_send, halo_recv, *scratch,
):
    at = place()
    tile = lax.axis_index("tile")
    left, right = lax.rem(tile + tiles_in_row - 1, tiles_in_row), lax.rem(tile + 1, tiles_in_row)
    scratch = list(scratch)
    send, recv = scratch.pop(), scratch.pop()
    chains = []
    for index, (order, first, tiles) in enumerate(CHAINS):
        landing = [scratch.pop(0) for _ in range(4)]
        held = [scratch.pop(0) for _ in range(3)]
        where = pl.ds(first, tiles)
        chains.append(Chain(order, parts.at[where], total_ref.at[where], landing, held, send.at[index], recv.at[index], at))

    barrier = pltpu.get_barrier_semaphore()
    met = 0
    for near in (left, right):
        pl.semaphore_signal(barrier, inc=1, device_id={"tile": near}, device_id_type=MESH)
        met += 1
    for axis, count in AXES.items():
        for step in range(1, count):
            pl.semaphore_signal(barrier, inc=1, device_id=peer(at, axis, step), device_id_type=MESH)
            met += 1

    def exchange(which, source, target):
        copies = []
        for side, near in enumerate((right, left)):
            copy = pltpu.make_async_remote_copy(
                src_ref=source.at[side], dst_ref=target.at[side],
                send_sem=halo_send.at[which, side], recv_sem=halo_recv.at[which, side],
                device_id={"tile": near}, device_id_type=MESH,
            )
            copy.start()
            copies.append(copy)
        return copies

    def masked(brick, x):
        gate = occupancy_ref[brick][x:x + 1, :].astype(jnp.float32)
        plane = (features_ref[brick, x].astype(jnp.float32) * gate).astype(jnp.bfloat16)
        return jnp.concatenate([plane, plane], axis=1)

    for side, column, x in ((0, 1, 7), (1, 0, 0)):
        for scene in range(2):
            out1[side, scene, 0:64, :] = masked(scene * 2 + column, x)
            row = lax.rem(slots_ref[scene, column], 2).astype(jnp.float32)
            out1[side, scene, 64:80, :] = jnp.full((16, 128), row, jnp.float32).astype(jnp.bfloat16)
    pl.semaphore_wait(barrier, met)
    copies1 = exchange(0, out1, halo1)

    ones = lax.broadcasted_iota(jnp.int32, (128, 128), 0) // 64 == lax.broadcasted_iota(jnp.int32, (128, 128), 1) // 64
    ones = ones.astype(jnp.float32).astype(jnp.bfloat16)

    def blocks(twice):
        return jnp.concatenate([twice, twice], axis=0) * ones

    def keep1(moved, brick, place_x):
        moved = moved.astype(jnp.bfloat16)
        for pair in range(5):
            xs[brick, place_x, :, pair * 128:pair * 128 + 128] = moved[pair * 64:pair * 64 + 64]

    for step in range(3):
        taps = w1_ref[:, step * 576:step * 576 + 576]
        w1p[step] = jnp.concatenate([taps, jnp.zeros((64, 64), jnp.bfloat16)], axis=1)
    for tap in range(27):
        w2f[tap * 128:tap * 128 + 128, :] = w2_ref[:, (26 - tap) * 128:(26 - tap) * 128 + 128]

    def local_planes(brick, carry):
        for x in range(8):
            keep1(dot(kept1_ref[...], blocks(masked(brick, x)), 1, 1), brick, x + 1)
            gate = jnp.broadcast_to(occupancy_ref[brick][x:x + 1, :].astype(jnp.float32), (128, 64))
            mk[brick, x] = dot(order_ref[...], gate.astype(jnp.bfloat16), 1, 1)
        for x in range(4):
            largest = None
            for a in range(2):
                for quarter in range(4):
                    part = mk[brick, 2 * x + a, quarter * 16:quarter * 16 + 16, :]
                    largest = part if largest is None else jnp.maximum(largest, part)
            gate2[brick, x] = largest
        return carry

    lax.fori_loop(0, 4, local_planes, 0)

    def shares(from_row, to_row, valid):
        apart = from_row - to_row
        return [share * valid for share in (1.0 - apart * apart, 0.5 * apart * (apart + 1.0), 0.5 * apart * (apart - 1.0))]

    rows = [[jnp.full((1, 128), lax.rem(slots_ref[s, k], 2).astype(jnp.float32), jnp.float32) for k in range(2)] for s in range(2)]
    has_left = (tile > 0).astype(jnp.float32)
    has_right = (tile < tiles_in_row - 1).astype(jnp.float32)

    def border1(plane, share, brick, place_x):
        share = [part.astype(jnp.bfloat16) for part in share]
        moves = kept1_ref[...] * share[0] + after1_ref[...] * share[1] + before1_ref[...] * share[2]
        keep1(dot(moves, blocks(plane), 1, 1), brick, place_x)

    share_of = {}
    for scene in range(2):
        share_of[scene, 1] = shares(rows[scene][1], rows[scene][0], 1.0)
        share_of[scene, 2] = shares(rows[scene][0], rows[scene][1], 1.0)
        border1(masked(scene * 2 + 1, 0), share_of[scene, 1], scene * 2, 9)
        border1(masked(scene * 2, 7), share_of[scene, 2], scene * 2 + 1, 0)

    for copy in copies1:
        copy.wait_recv()
    for scene in range(2):
        from_left = halo1[0, scene, 64:80, :].astype(jnp.float32)[0:1]
        from_right = halo1[1, scene, 64:80, :].astype(jnp.float32)[0:1]
        share_of[scene, 0] = shares(from_left, rows[scene][0], has_left)
        share_of[scene, 3] = shares(from_right, rows[scene][1], has_right)
        border1(halo1[0, scene, 0:64, :], share_of[scene, 0], scene * 2, 0)
        border1(halo1[1, scene, 0:64, :], share_of[scene, 3], scene * 2 + 1, 9)

    def fine_brick(brick, carry):
        pre = None
        for step in range(3):
            window = xs[brick, step:step + 8].reshape(512, 640)
            term = dot(window, w1p[step], 1, 1)
            pre = term if pre is None else pre + term
        mask = mk[brick, :, :, 0:64].reshape(512, 64)
        act, slope = gate_slope(pre)
        slope1[brick] = (slope * mask).reshape(8, 64, 64)
        act = (act * mask).astype(jnp.bfloat16).reshape(4, 2, 4, 16, 64)
        for a in range(2):
            for half in range(2):
                pair = jnp.concatenate([act[:, a, 2 * half], act[:, a, 2 * half + 1]], axis=2)
                first = (a * 2 + half) * 128
                child[brick, :, first:first + 128] = pair.reshape(64, 128)
        return carry

    lax.fori_loop(0, 4, fine_brick, 0)

    gate = gate2[...].reshape(256, 128)
    down_pre = dot(child[...].reshape(256, 512), wd_ref[...], 1, 1)
    act, slope = gate_slope(down_pre)
    slope2[...] = slope * gate
    act2[...] = (act * gate).astype(jnp.bfloat16).reshape(4, 4, 16, 128)

    def outer2(values, outgoing):
        for scene in range(2):
            outgoing[0, scene] = values[scene * 2 + 1, 3]
            outgoing[1, scene] = values[scene * 2, 0]

    def inner2(values, into):
        for brick in range(4):
            moved = dot(kept2_ref[...], values[brick].reshape(64, 128), 1, 0).astype(jnp.bfloat16)
            base = brick * 64
            for tap in range(9):
                here = moved[tap * 64:tap * 64 + 64]
                into[base + 16:base + 64, tap * 128:tap * 128 + 128] = here[0:48]
                into[base:base + 64, (9 + tap) * 128:(10 + tap) * 128] = here
                into[base:base + 48, (18 + tap) * 128:(19 + tap) * 128] = here[16:64]

    def border2(values, halo, into):
        planes = []
        for scene in range(2):
            planes += [halo[0, scene], values[scene * 2 + 1, 0], values[scene * 2, 3], halo[1, scene]]
        moved = dot(edge2[...], jnp.concatenate(planes, axis=0), 1, 0).astype(jnp.bfloat16)
        for tap in range(9):
            for brick in range(4):
                first = tap * 128 + brick * 32
                base = brick * 64
                into[base:base + 16, tap * 128:tap * 128 + 128] = moved[first:first + 16]
                into[base + 48:base + 64, (18 + tap) * 128:(19 + tap) * 128] = moved[first + 16:first + 32]

    outer2(act2, out2)
    copies2 = exchange(1, out2, halo2)
    inner2(act2, im2)
    lane = lax.broadcasted_iota(jnp.int32, (1, 128), 1) // 16
    shared = [jnp.zeros((1, 128), jnp.float32) for _ in range(3)]
    for scene in range(2):
        for role in range(4):
            own = (lane == scene * 4 + role).astype(jnp.float32)
            shared = [so_far + own * part for so_far, part in zip(shared, share_of[scene, role])]
    shared = [part.astype(jnp.bfloat16) for part in shared]
    edge2[...] = kept8_ref[...] * shared[0] + after8_ref[...] * shared[1] + before8_ref[...] * shared[2]
    for copy in copies2:
        copy.wait_recv()
    border2(act2, halo2, im2)
    coarse_pre = dot(im2[...], w2_ref[...], 1, 1)
    act, slope = gate_slope(coarse_pre)
    section_ref[...] = (act * gate).astype(jnp.bfloat16)
    grad2[...] = (upstream_ref[...].astype(jnp.float32) * gate * slope).astype(jnp.bfloat16).reshape(4, 4, 16, 128)
    outer2(grad2, out3)
    copies3 = exchange(2, out3, halo3)

    def keep_parts(values, first, width, lane_tile):
        values = values.astype(jnp.bfloat16)
        for block in range(values.shape[0] // 16):
            for column in range(values.shape[1] // 128):
                parts[first + block * width + lane_tile + column] = values[block * 16:block * 16 + 16, column * 128:column * 128 + 128]

    inner2(grad2, img)
    grad_rows = grad2[...].reshape(256, 128)
    for step in range(3):
        keep_parts(dot(grad_rows, im2[:, step * 1152:step * 1152 + 1152], 0, 0), 0, 32, step * 9)
    for copy in copies3:
        copy.wait_recv()
    border2(grad2, halo3, img)
    down_back = dot(img[...], w2f[...], 1, 0)
    down_in = (down_back * slope2[...]).astype(jnp.bfloat16)
    keep_parts(dot(down_in, child[...].reshape(256, 512), 0, 0), 0, 32, 27)
    keep_parts(jnp.zeros((128, 128), jnp.float32), 0, 32, 31)
    for chain in chains[:3]:
        chain.start(0)

    fine_back = dot(down_in, wd_ref[...], 1, 0)
    for brick in range(4):
        for x in range(8):
            base = brick * 64 + x // 2 * 16
            first = x % 2 * 256
            back = [fine_back[base:base + 16, first + part * 64:first + part * 64 + 64] for part in range(4)]
            grad1[brick, x] = (jnp.concatenate(back, axis=0) * slope1[brick, x]).astype(jnp.bfloat16)
    for step in range(3):
        term = None
        for brick in range(4):
            window = xs[brick, step:step + 8].reshape(512, 640)
            part = dot(grad1[brick].reshape(512, 64), window, 0, 0)
            term = part if term is None else term + part
        keep_parts(term, 256, 16, step * 5)
    keep_parts(jnp.zeros((64, 128), jnp.float32), 256, 16, 15)
    chains[3].start(0)

    stages = len(STAGES["x"])
    for stage in range(1, stages):
        for chain in chains:
            chain.finish(stage - 1)
            chain.start(stage)
    for chain in chains:
        chain.finish(stages - 1)
    for copy in copies1 + copies2 + copies3:
        copy.wait_send()
    for chain in chains:
        chain.close()


def unpack_kernel(scale, section_ref, total_ref, section_out, conv1_ref, down_ref, conv2_ref):
    section_out[...] = section_ref[...]
    for block in range(8):
        rows = slice(block * 16, block * 16 + 16)
        for column in range(27):
            conv2_ref[rows, column * 128:column * 128 + 128] = total_ref[block * 32 + column].astype(jnp.float32) * scale
        for column in range(4):
            down_ref[rows, column * 128:column * 128 + 128] = total_ref[block * 32 + 27 + column].astype(jnp.float32) * scale
    for block in range(4):
        rows = slice(block * 16, block * 16 + 16)
        taps = []
        for step in range(3):
            whole = [total_ref[256 + block * 16 + step * 5 + pair].astype(jnp.float32) * scale for pair in range(5)]
            taps += whole[:4] + [whole[4][:, 0:64]]
        conv1_ref[rows, :] = jnp.concatenate(taps, axis=1)


def per_device(tiles_in_row, scale, features, occupancy, brick_slots, conv1_weight, down_weight, conv2_weight, upstream):
    tables = fine_selections() + coarse_selections(4)[:1] + coarse_selections(8)
    bf16, f32 = jnp.bfloat16, jnp.float32
    vmem, dma = pltpu.VMEM, pltpu.SemaphoreType.DMA
    scratch = [
        vmem((320, 16, 128), bf16),
        vmem((2, 2, 80, 128), bf16), vmem((2, 2, 16, 128), bf16), vmem((2, 2, 16, 128), bf16),
        vmem((2, 2, 80, 128), bf16), vmem((2, 2, 16, 128), bf16), vmem((2, 2, 16, 128), bf16),
        vmem((4, 10, 64, 640), bf16), vmem((3, 64, 640), bf16), vmem((3456, 128), bf16),
        vmem((4, 8, 64, 128), f32), vmem((4, 8, 64, 64), f32), vmem((4, 64, 512), bf16), vmem((4, 8, 64, 64), bf16),
        vmem((4, 4, 16, 128), f32), vmem((256, 128), f32), vmem((4, 4, 16, 128), bf16), vmem((1152, 128), bf16),
        vmem((256, 3456), bf16), vmem((256, 3456), bf16), vmem((4, 4, 16, 128), bf16),
        dma((3, 2)), dma((3, 2)),
    ]
    for order, first, tiles in CHAINS:
        landing, held = Chain.sizes(order, tiles)
        scratch += [vmem(size + (16, 128), bf16) for size in landing]
        scratch += [vmem((size, 16, 128), bf16) for size in held]
    scratch += [dma((len(CHAINS), 7, 7))] * 2
    whole = pl.BlockSpec(memory_space=vmem)
    section, total = pl.pallas_call(
        functools.partial(section_kernel, tiles_in_row),
        out_shape=(jax.ShapeDtypeStruct((256, 128), bf16), jax.ShapeDtypeStruct((320, 16, 128), bf16)),
        in_specs=[pl.BlockSpec(memory_space=pltpu.SMEM)] + [whole] * (6 + len(tables)),
        out_specs=(whole, whole),
        scratch_shapes=scratch,
        compiler_params=pltpu.CompilerParams(collective_id=0, has_side_effects=True, vmem_limit_bytes=48 * 2**20),
    )(
        brick_slots, features.reshape(4, 8, 64, 64), occupancy.reshape(4, 8, 64), conv1_weight, down_weight, conv2_weight,
        upstream.reshape(256, 128), *[jnp.asarray(table) for table in tables],
    )
    section, conv1, down, conv2 = pl.pallas_call(
        functools.partial(unpack_kernel, scale),
        out_shape=(
            jax.ShapeDtypeStruct((256, 128), bf16), jax.ShapeDtypeStruct((64, 1728), f32),
            jax.ShapeDtypeStruct((128, 512), f32), jax.ShapeDtypeStruct((128, 3456), f32),
        ),
        in_specs=[whole] * 2,
        out_specs=(whole,) * 4,
        compiler_params=pltpu.CompilerParams(vmem_limit_bytes=24 * 2**20),
    )(section, total)
    return section.reshape(upstream.shape), conv1, down, conv2


def solution(mesh):
    tiles_in_row, scenes = mesh.shape["tile"], mesh.shape["dp"] * 2
    scale = 1.0 / (scenes * tiles_in_row * 2)
    wide = P("dp", "tile", None, None, None)
    return jax.shard_map(
        functools.partial(per_device, tiles_in_row, scale),
        mesh=mesh,
        in_specs=(wide, P("dp", "tile", None, None), P("dp", "tile"), P(), P(), P(), wide),
        out_specs=(wide, P(), P(), P()),
        check_vma=False,
    )
```

```python
import functools

import jax
import jax.numpy as jnp
import numpy as np
from jax import lax
from jax.experimental import pallas as pl
from jax.experimental.pallas import tpu as pltpu
from jax.sharding import PartitionSpec as P

FINE = 64
COARSE = 128
MESH = pl.DeviceIdType.MESH

AXES = {"c": 2, "x": 4, "y": 8, "z": 8}
STAGES = {
    "x": (("rs", "c"), ("rs", "x"), ("rs", "y"), ("ar", "z"), ("ag", "y"), ("ag", "x"), ("ag", "c")),
    "y": (("rs", "c"), ("rs", "y"), ("rs", "x"), ("ar", "z"), ("ag", "x"), ("ag", "y"), ("ag", "c")),
    "z": (("rs", "c"), ("rs", "z"), ("rs", "x"), ("ar", "y"), ("ag", "x"), ("ag", "z"), ("ag", "c")),
}


Y_LOW = 4


def place():
    dp, tile = lax.axis_index("dp"), lax.axis_index("tile")
    c, x, z = AXES["c"], AXES["x"], AXES["z"]
    return {
        "c": lax.rem(tile, c),
        "z": lax.rem(lax.div(tile, c), z),
        "x": lax.rem(lax.div(tile, c * z), x),
        "y": lax.div(tile, c * z * x) * Y_LOW + dp,
    }


def device(at):
    c, x, z = AXES["c"], AXES["x"], AXES["z"]
    tile = ((lax.div(at["y"], Y_LOW) * x + at["x"]) * z + at["z"]) * c + at["c"]
    return {"dp": lax.rem(at["y"], Y_LOW), "tile": tile}


def peer(at, axis, step):
    moved = dict(at)
    moved[axis] = lax.rem(at[axis] + step, AXES[axis])
    return device(moved)


class Chain:
    def __init__(self, order, own, result, landing, held, send, recv, at):
        self.stages, self.at = STAGES[order], at
        self.own, self.result, self.landing, self.held = own, result, landing, held
        self.send, self.recv = send, recv
        self.copies = {}

    @staticmethod
    def sizes(order, tiles):
        landing, held = [], []
        for kind, axis in STAGES[order]:
            if kind == "rs":
                tiles //= AXES[axis]
                landing.append((AXES[axis] - 1, tiles))
                held.append(tiles)
            elif kind == "ar":
                landing.append((AXES[axis], tiles))
        return landing, held

    def source(self, stage):
        return self.own if stage == 0 else self.held[stage - 1]

    def offset(self, stages):
        first = 0
        for stage in range(stages):
            first = first + self.at[self.stages[stage][1]] * self.held[stage].shape[0]
        return first

    def start(self, stage):
        kind, axis = self.stages[stage]
        count = AXES[axis]
        for step in range(1, count):
            if kind == "rs":
                part = self.held[stage].shape[0]
                to = lax.rem(self.at[axis] + step, count)
                src = self.source(stage).at[pl.ds(to * part, part)]
                dst = self.landing[stage].at[step - 1]
            elif kind == "ar":
                src = self.source(stage)
                dst = self.landing[stage].at[self.at[axis]]
            else:
                back = len(self.stages) - 1 - stage
                part = self.held[back].shape[0]
                where = pl.ds(self.offset(back + 1), part)
                src = dst = self.result.at[where]
            copy = pltpu.make_async_remote_copy(
                src_ref=src, dst_ref=dst,
                send_sem=self.send.at[stage, step - 1], recv_sem=self.recv.at[stage, step - 1],
                device_id=peer(self.at, axis, step), device_id_type=MESH,
            )
            copy.start()
            self.copies[stage, step] = copy

    def finish(self, stage):
        kind, axis = self.stages[stage]
        count = AXES[axis]
        for step in range(1, count):
            if kind == "ag":
                back = len(self.stages) - 1 - stage
                part = self.held[back].shape[0]
                origin = dict(self.at)
                origin[axis] = lax.rem(self.at[axis] + count - step, count)
                first = 0
                for earlier in range(back + 1):
                    first = first + origin[self.stages[earlier][1]] * self.held[earlier].shape[0]
                dst = self.result.at[pl.ds(first, part)]
            elif kind == "rs":
                dst = self.landing[stage].at[step - 1]
            else:
                dst = self.landing[stage].at[lax.rem(self.at[axis] + count - step, count)]
            pltpu.make_async_remote_copy(
                src_ref=dst, dst_ref=dst,
                send_sem=self.send.at[stage, step - 1], recv_sem=self.recv.at[stage, step - 1],
                device_id=peer(self.at, axis, step), device_id_type=MESH,
            ).wait_recv()
        if kind == "rs":
            part = self.held[stage].shape[0]
            mine = self.source(stage)[pl.ds(self.at[axis] * part, part)]
            total = mine.astype(jnp.float32)
            for step in range(1, count):
                total = total + self.landing[stage][step - 1].astype(jnp.float32)
            self.held[stage][...] = total.astype(jnp.bfloat16)
        elif kind == "ar":
            self.landing[stage][self.at[axis]] = self.source(stage)[...]
            total = self.landing[stage][0].astype(jnp.float32)
            for index in range(1, count):
                total = total + self.landing[stage][index].astype(jnp.float32)
            self.result[pl.ds(self.offset(stage), total.shape[0])] = total.astype(jnp.bfloat16)

    def close(self):
        for copy in self.copies.values():
            copy.wait_send()

CHAINS = (("x", 0, 128), ("y", 128, 64), ("z", 192, 64), ("x", 256, 64))


def fine_selections():
    kept, after, before = np.zeros((3, 5, 64, 2, 64), np.float32)
    order = np.zeros((64, 64), np.float32)
    for y in range(8):
        for z in range(8):
            row = (y % 2) * 32 + (z % 2) * 16 + (y // 2) * 4 + z // 2
            order[row, y * 8 + z] = 1
            for tap in range(9):
                from_y, from_z = y + tap // 3 - 1, z + tap % 3 - 1
                if 0 <= from_z < 8:
                    into = kept if 0 <= from_y < 8 else after if from_y == 8 else before
                    into[tap // 2, row, tap % 2, (from_y % 8) * 8 + from_z] = 1
    return [table.reshape(320, 128) for table in (kept, after, before)] + [order]


def coarse_selections():
    kept, after, before = np.zeros((3, 9, 16, 16), np.float32)
    for y in range(4):
        for z in range(4):
            for tap in range(9):
                from_y, from_z = y + tap // 3 - 1, z + tap % 3 - 1
                if 0 <= from_z < 4:
                    into = kept if 0 <= from_y < 4 else after if from_y == 4 else before
                    into[tap, y * 4 + z, (from_y % 4) * 4 + from_z] = 1
    brick = np.einsum("tij,pq->tpiqj", kept, np.eye(4, dtype=np.float32)).reshape(576, 64)
    return [brick] + [np.tile(table.reshape(144, 16), (1, 8)) for table in (kept, after, before)]


def selections():
    tables = fine_selections() + coarse_selections()
    first = np.cumsum([0] + [table.shape[0] for table in tables])
    padded = [np.pad(table, ((0, 0), (0, 128 - table.shape[1]))) for table in tables]
    return np.concatenate(padded).astype(jnp.bfloat16), [int(place) for place in first]


def gate_slope(value):
    gate = jax.nn.sigmoid(value)
    return value * gate, gate * (1.0 + value * (1.0 - gate))


def dot(left, right, left_dim, right_dim):
    return lax.dot_general(left, right, (((left_dim,), (right_dim,)), ((), ())), preferred_element_type=jnp.float32)


def section_kernel(
    tiles_in_row, table_at,
    slots_ref, features_hbm, occupancy_hbm, tables_hbm, w1_hbm, wd_hbm, w2_hbm, upstream_hbm,
    section_ref, total_ref,
    features_ref, occupancy_ref, tables_ref, w1_ref, wd_ref, w2_ref, upstream_ref, load_sem,
    near_features, near_occupancy, near_upstream, near_rows, own_rows, halo_send, halo_recv,
    parts, xs, near_xs, w1p, w2f, mk, slope1, child, grad1, gate2, slope2, act2, edge2, edge3, im2, img, grad2,
    *scratch,
):
    loads = []
    operands = (
        (features_hbm, features_ref), (occupancy_hbm, occupancy_ref), (tables_hbm, tables_ref), (w1_hbm, w1_ref),
        (w2_hbm, w2_ref), (wd_hbm, wd_ref), (upstream_hbm, upstream_ref),
    )
    for index, (source, target) in enumerate(operands):
        loads.append(pltpu.make_async_copy(source, target, load_sem.at[index]))
        loads[-1].start()
    kept1_ref, after1_ref, before1_ref, order_ref, kept2_ref, kept8_ref, after8_ref, before8_ref = [
        tables_ref.at[first:last] for first, last in zip(table_at, table_at[1:])
    ]
    at = place()
    tile = lax.axis_index("tile")
    left, right = lax.rem(tile + tiles_in_row - 1, tiles_in_row), lax.rem(tile + 1, tiles_in_row)
    scratch = list(scratch)
    send, recv = scratch.pop(), scratch.pop()
    chains = []
    for index, (order, first, tiles) in enumerate(CHAINS):
        landing = [scratch.pop(0) for _ in range(4)]
        held = [scratch.pop(0) for _ in range(3)]
        where = pl.ds(first, tiles)
        chains.append(Chain(order, parts.at[where], total_ref.at[where], landing, held, send.at[index], recv.at[index], at))

    barrier = pltpu.get_barrier_semaphore()
    met = 0
    for near in (left, right):
        pl.semaphore_signal(barrier, inc=1, device_id={"tile": near}, device_id_type=MESH)
        met += 1
    for axis, count in AXES.items():
        for step in range(1, count):
            pl.semaphore_signal(barrier, inc=1, device_id=peer(at, axis, step), device_id_type=MESH)
            met += 1

    def row_of(scene, column):
        return lax.rem(slots_ref[scene, column], 2).astype(jnp.float32)

    for side in range(2):
        for scene in range(2):
            own_rows[side, scene] = jnp.full((16, 128), row_of(scene, 1 - side), jnp.float32).astype(jnp.bfloat16)
    pl.semaphore_wait(barrier, met)
    halos = []
    for side, near in enumerate((right, left)):
        column, planes, border = ((1, pl.ds(3, 5), 3), (0, pl.ds(0, 5), 0))[side]
        pieces = (
            (features_hbm.at[:, column, planes], near_features.at[side]),
            (occupancy_hbm.at[:, column], near_occupancy.at[side]),
            (own_rows.at[side], near_rows.at[side]),
            (upstream_hbm.at[:, column, border], near_upstream.at[side]),
        )
        for index, (source, target) in enumerate(pieces):
            copy = pltpu.make_async_remote_copy(
                src_ref=source, dst_ref=target, send_sem=halo_send.at[side, index], recv_sem=halo_recv.at[side, index],
                device_id={"tile": near}, device_id_type=MESH,
            )
            copy.start()
            halos.append(copy)

    same_half = lax.broadcasted_iota(jnp.int32, (128, 128), 0) // 64 == lax.broadcasted_iota(jnp.int32, (128, 128), 1) // 64
    same_half = same_half.astype(jnp.float32).astype(jnp.bfloat16)

    def blocks(plane, gate):
        plane = (plane.astype(jnp.float32) * gate).astype(jnp.bfloat16)
        twice = jnp.concatenate([plane, plane], axis=1)
        return jnp.concatenate([twice, twice], axis=0) * same_half

    def own_plane(brick, x):
        return blocks(features_ref[brick // 2, brick % 2, x], gate_row(occupancy_ref[brick // 2, brick % 2], x))

    def gate_row(occupied, x):
        return occupied[x:x + 1, :].astype(jnp.float32)

    def keep1(moved, into):
        moved = moved.astype(jnp.bfloat16)
        for pair in range(5):
            into[:, pair * 128:pair * 128 + 128] = moved[pair * 64:pair * 64 + 64]

    def voxel_gate(row):
        return dot(order_ref[:, 0:64], jnp.broadcast_to(row, (128, 64)).astype(jnp.bfloat16), 1, 1)

    def coarse_gate(first):
        largest = None
        for a in range(2):
            for quarter in range(4):
                part = mk[first + a, quarter * 16:quarter * 16 + 16, :]
                largest = part if largest is None else jnp.maximum(largest, part)
        return largest

    for load in loads:
        load.wait()
    for step in range(3):
        taps = w1_ref[:, step * 576:step * 576 + 576]
        w1p[step] = jnp.concatenate([taps, jnp.zeros((64, 64), jnp.bfloat16)], axis=1)

    def local_planes(brick, carry):
        scene, column = lax.div(brick, 2), lax.rem(brick, 2)
        occupied = occupancy_ref[scene, column]
        for x in range(8):
            row = gate_row(occupied, x)
            keep1(dot(kept1_ref[...], blocks(features_ref[scene, column, x], row), 1, 1), xs.at[brick, x + 1])
            mk[brick * 8 + x] = voxel_gate(row)
        for x in range(4):
            gate2[brick * 4 + x] = coarse_gate(brick * 8 + 2 * x)
        return carry

    lax.fori_loop(0, 4, local_planes, 0)
    for tap in range(27):
        w2f[tap * 128:tap * 128 + 128, :] = w2_ref[:, (26 - tap) * 128:(26 - tap) * 128 + 128]

    def shares(from_row, to_row, valid):
        apart = from_row - to_row
        return [share * valid for share in (1.0 - apart * apart, 0.5 * apart * (apart + 1.0), 0.5 * apart * (apart - 1.0))]

    rows = [[jnp.full((1, 128), row_of(scene, column), jnp.float32) for column in range(2)] for scene in range(2)]
    has_left = (tile > 0).astype(jnp.float32)
    has_right = (tile < tiles_in_row - 1).astype(jnp.float32)

    def border1(plane, share, into):
        share = [part.astype(jnp.bfloat16) for part in share]
        moves = kept1_ref[...] * share[0] + after1_ref[...] * share[1] + before1_ref[...] * share[2]
        keep1(dot(moves, plane, 1, 1), into)

    share_of = {}
    for scene in range(2):
        share_of[scene, 1] = shares(rows[scene][1], rows[scene][0], 1.0)
        share_of[scene, 2] = shares(rows[scene][0], rows[scene][1], 1.0)
        border1(own_plane(scene * 2 + 1, 0), share_of[scene, 1], xs.at[scene * 2, 9])
        border1(own_plane(scene * 2, 7), share_of[scene, 2], xs.at[scene * 2 + 1, 0])

    def fine(source, first, count, gates, children, child_row, first_x, slopes):
        pre = None
        for step in range(3):
            window = source[first + step:first + step + count].reshape(count * 64, 640)
            term = dot(window, w1p[step], 1, 1)
            pre = term if pre is None else pre + term
        mask = gates[:, :, 0:64].reshape(count * 64, 64)
        act, slope = gate_slope(pre)
        if slopes is not None:
            slopes[...] = (slope * mask).reshape(count, 64, 64)
        act = (act * mask).astype(jnp.bfloat16).reshape(count, 4, 16, 64)
        for index in range(count):
            x = first_x + index
            for half in range(2):
                pair = jnp.concatenate([act[index, 2 * half], act[index, 2 * half + 1]], axis=1)
                lanes = (x % 2 * 2 + half) * 128
                children[pl.ds(child_row + x // 2 * 16, 16), lanes:lanes + 128] = pair

    def inner_planes(scene, carry):
        for column in range(2):
            brick = scene * 2 + column
            first = 1 - column
            fine(
                xs.at[brick], first, 7, mk[pl.ds(brick * 8 + first, 7)], child, brick * 64, first,
                slope1.at[brick, pl.ds(first, 7)],
            )
        return carry

    lax.fori_loop(0, 2, inner_planes, 0)

    for copy in halos:
        copy.wait_recv()

    def near_planes(unit, carry):
        side, scene = lax.div(unit, 2), lax.rem(unit, 2)
        occupied = near_occupancy[side, scene].astype(jnp.float32)
        after = (side == 0).astype(jnp.float32)
        for x in range(5):
            row = occupied[x + 3:x + 4] * after + occupied[x:x + 1] * (1.0 - after)
            moved = dot(kept1_ref[...], blocks(near_features[side, scene, x], row), 1, 1)
            keep1(moved, near_xs.at[unit, x + side])
            near_gate = voxel_gate(row)
            mk[32 + unit * 5 + x] = near_gate
        for x in range(2):
            gate2[16 + unit * 2 + x] = coarse_gate(32 + unit * 5 + 1 - side + 2 * x)
        return carry

    lax.fori_loop(0, 4, near_planes, 0)
    for scene in range(2):
        from_left = near_rows[0, scene].astype(jnp.float32)[0:1]
        from_right = near_rows[1, scene].astype(jnp.float32)[0:1]
        to_left = shares(from_left, rows[scene][0], has_left)
        to_right = shares(from_right, rows[scene][1], has_right)
        share_of[scene, 0], share_of[scene, 3] = to_left, to_right
        share_of[scene, 4] = [to_left[0], to_left[2], to_left[1]]
        share_of[scene, 5] = [to_right[0], to_right[2], to_right[1]]
        last = blocks(near_features[0, scene, 4], gate_row(near_occupancy[0, scene], 7))
        border1(last, share_of[scene, 0], xs.at[scene * 2, 0])
        first = blocks(near_features[1, scene, 0], gate_row(near_occupancy[1, scene], 0))
        border1(first, share_of[scene, 3], xs.at[scene * 2 + 1, 9])
        border1(own_plane(scene * 2, 0), share_of[scene, 4], near_xs.at[scene, 5])
        border1(own_plane(scene * 2 + 1, 7), share_of[scene, 5], near_xs.at[2 + scene, 0])

    for scene in range(2):
        brick = scene * 2
        fine(xs.at[brick], 0, 1, mk[brick * 8:brick * 8 + 1], child, brick * 64, 0, slope1.at[brick, 0:1])
        brick = scene * 2 + 1
        fine(xs.at[brick], 7, 1, mk[brick * 8 + 7:brick * 8 + 8], child, brick * 64, 7, slope1.at[brick, 7:8])

    for unit in range(4):
        first = 32 + unit * 5 + (1 if unit < 2 else 0)
        fine(near_xs.at[unit], 0, 4, mk[first:first + 4], child, 256 + unit * 32, 0, None)

    gate = gate2[...].reshape(384, 128)
    down_pre = dot(child[...], wd_ref[...], 1, 1)
    act, slope = gate_slope(down_pre)
    slope2[...] = slope[0:256] * gate[0:256]
    act2[...] = (act * gate).astype(jnp.bfloat16).reshape(24, 16, 128)

    def lanes_of(tap, step):
        first = (step * 9 + tap) * 128
        return slice(first, first + 128)

    def inner2(values, into):
        for brick in range(4):
            moved = dot(kept2_ref[:, 0:64], values[brick * 4:brick * 4 + 4].reshape(64, 128), 1, 0).astype(jnp.bfloat16)
            base = brick * 64
            for tap in range(9):
                here = moved[tap * 64:tap * 64 + 64]
                into[base + 16:base + 64, lanes_of(tap, 0)] = here[0:48]
                into[base:base + 64, lanes_of(tap, 1)] = here
                into[base:base + 48, lanes_of(tap, 2)] = here[16:64]

    def border2(values, near, into):
        planes = []
        for scene in range(2):
            planes += [near[0][scene], values[scene * 8 + 4], values[scene * 8 + 3], near[1][scene]]
        moved = dot(edge2[...], jnp.concatenate(planes, axis=0), 1, 0).astype(jnp.bfloat16)
        for tap in range(9):
            for brick in range(4):
                first = tap * 128 + brick * 32
                base = brick * 64
                into[base:base + 16, lanes_of(tap, 0)] = moved[first:first + 16]
                into[base + 48:base + 64, lanes_of(tap, 2)] = moved[first + 16:first + 32]

    def near2():
        outer = [act2[16 + 4 * side:20 + 4 * side].reshape(64, 128) for side in range(2)]
        moved = [dot(kept2_ref[:, 0:64], part, 1, 0).astype(jnp.bfloat16) for part in outer]
        planes = [act2[scene * 8 + plane] for scene in range(2) for plane in (0, 7)]
        edges = dot(edge3[:, 0:64], jnp.concatenate(planes, axis=0), 1, 0).astype(jnp.bfloat16)
        for tap in range(9):
            for scene in range(2):
                first = tap * 64 + scene * 32
                base = 256 + scene * 16
                im2[base:base + 16, lanes_of(tap, 0)] = moved[0][first:first + 16]
                im2[base:base + 16, lanes_of(tap, 1)] = moved[0][first + 16:first + 32]
                im2[base:base + 16, lanes_of(tap, 2)] = edges[first:first + 16]
                im2[base + 32:base + 48, lanes_of(tap, 0)] = edges[first + 16:first + 32]
                im2[base + 32:base + 48, lanes_of(tap, 1)] = moved[1][first:first + 16]
                im2[base + 32:base + 48, lanes_of(tap, 2)] = moved[1][first + 16:first + 32]

    def edges_of(roles, count):
        lane = lax.broadcasted_iota(jnp.int32, (1, 128), 1) // 16
        shared = [jnp.zeros((1, 128), jnp.float32) for _ in range(3)]
        for index, role in enumerate(roles):
            own = (lane == index).astype(jnp.float32)
            shared = [so_far + own * part for so_far, part in zip(shared, share_of[role])]
        shared = [part.astype(jnp.bfloat16) for part in shared]
        same = lax.broadcasted_iota(jnp.int32, (count, 16, 128), 0) == lax.broadcasted_iota(jnp.int32, (count, 16, 128), 2) // 16
        same = same.astype(jnp.float32).astype(jnp.bfloat16).reshape(1, count, 16, 128)
        moves = kept8_ref[...] * shared[0] + after8_ref[...] * shared[1] + before8_ref[...] * shared[2]
        return (moves.reshape(9, 1, 16, 128) * same).reshape(9 * count * 16, 128)

    edge2[...] = edges_of([(scene, role) for scene in range(2) for role in range(4)], 8)
    edge3[...] = edges_of([(scene, role) for scene in range(2) for role in (4, 5)], 4)
    inner2(act2, im2)
    border2(act2, ([act2[17], act2[19]], [act2[20], act2[22]]), im2)
    near2()
    coarse_pre = dot(im2[...], w2_ref[...], 1, 1)
    act, slope = gate_slope(coarse_pre)
    section_ref[...] = (act[0:256] * gate[0:256]).astype(jnp.bfloat16)
    upstream = [upstream_ref[...].reshape(256, 128), near_upstream[...].reshape(64, 128)]
    gates = [gate[0:256], gate[272:288], gate[304:320], gate[320:336], gate[352:368]]
    upstream = jnp.concatenate(upstream, axis=0).astype(jnp.float32) * jnp.concatenate(gates, axis=0)
    grad2[...] = (upstream * slope).astype(jnp.bfloat16).reshape(20, 16, 128)

    def keep_parts(values, first, width, lane_tile):
        values = values.astype(jnp.bfloat16)
        for block in range(values.shape[0] // 16):
            for column in range(values.shape[1] // 128):
                parts[first + block * width + lane_tile + column] = values[block * 16:block * 16 + 16, column * 128:column * 128 + 128]

    grad_rows = grad2[0:16].reshape(256, 128)
    for step in range(3):
        keep_parts(dot(grad_rows, im2[0:256, step * 1152:step * 1152 + 1152], 0, 0), 0, 32, step * 9)
    inner2(grad2, img)
    border2(grad2, ([grad2[16], grad2[17]], [grad2[18], grad2[19]]), img)
    down_back = dot(img[...], w2f[...], 1, 0)
    down_in = (down_back * slope2[...]).astype(jnp.bfloat16)
    keep_parts(dot(down_in, child[0:256], 0, 0), 0, 32, 27)
    keep_parts(jnp.zeros((128, 128), jnp.float32), 0, 32, 31)
    for chain in chains[:3]:
        chain.start(0)

    fine_back = dot(down_in, wd_ref[...], 1, 0)
    for brick in range(4):
        for x in range(8):
            base = brick * 64 + x // 2 * 16
            first = x % 2 * 256
            back = [fine_back[base:base + 16, first + part * 64:first + part * 64 + 64] for part in range(4)]
            grad1[brick, x] = (jnp.concatenate(back, axis=0) * slope1[brick, x]).astype(jnp.bfloat16)
    for step in range(3):
        term = None
        for brick in range(4):
            window = xs[brick, step:step + 8].reshape(512, 640)
            part = dot(grad1[brick].reshape(512, 64), window, 0, 0)
            term = part if term is None else term + part
        keep_parts(term, 256, 16, step * 5)
    keep_parts(jnp.zeros((64, 128), jnp.float32), 256, 16, 15)
    chains[3].start(0)

    stages = len(STAGES["x"])
    for stage in range(1, stages):
        for chain in chains:
            chain.finish(stage - 1)
            chain.start(stage)
    for chain in chains:
        chain.finish(stages - 1)
    for copy in halos:
        copy.wait_send()
    for chain in chains:
        chain.close()


def unpack_kernel(scale, section_ref, total_ref, section_out, conv1_ref, down_ref, conv2_ref):
    section_out[...] = section_ref[...]
    for block in range(8):
        rows = slice(block * 16, block * 16 + 16)
        for column in range(27):
            conv2_ref[rows, column * 128:column * 128 + 128] = total_ref[block * 32 + column].astype(jnp.float32) * scale
        for column in range(4):
            down_ref[rows, column * 128:column * 128 + 128] = total_ref[block * 32 + 27 + column].astype(jnp.float32) * scale
    for block in range(4):
        rows = slice(block * 16, block * 16 + 16)
        taps = []
        for step in range(3):
            whole = [total_ref[256 + block * 16 + step * 5 + pair].astype(jnp.float32) * scale for pair in range(5)]
            taps += whole[:4] + [whole[4][:, 0:64]]
        conv1_ref[rows, :] = jnp.concatenate(taps, axis=1)


def per_device(tiles_in_row, scale, features, occupancy, brick_slots, conv1_weight, down_weight, conv2_weight, upstream):
    tables, table_at = selections()
    bf16, f32 = jnp.bfloat16, jnp.float32
    vmem, dma = pltpu.VMEM, pltpu.SemaphoreType.DMA
    scratch = [
        vmem((2, 2, 8, 64, 64), bf16), vmem((2, 2, 8, 64), jnp.int32), vmem(tables.shape, bf16), vmem((64, 1728), bf16),
        vmem((128, 512), bf16), vmem((128, 3456), bf16), vmem((2, 2, 4, 16, 128), bf16), dma((7,)),
        vmem((2, 2, 5, 64, 64), bf16), vmem((2, 2, 8, 64), jnp.int32), vmem((2, 2, 16, 128), bf16),
        vmem((2, 2, 16, 128), bf16), vmem((2, 2, 16, 128), bf16), dma((2, 4)), dma((2, 4)),
        vmem((320, 16, 128), bf16), vmem((4, 10, 64, 640), bf16), vmem((4, 6, 64, 640), bf16), vmem((3, 64, 640), bf16),
        vmem((3456, 128), bf16), vmem((52, 64, 128), f32), vmem((4, 8, 64, 64), f32), vmem((384, 512), bf16),
        vmem((4, 8, 64, 64), bf16), vmem((24, 16, 128), f32), vmem((256, 128), f32), vmem((24, 16, 128), bf16),
        vmem((1152, 128), bf16), vmem((576, 128), bf16), vmem((320, 3456), bf16), vmem((256, 3456), bf16),
        vmem((20, 16, 128), bf16),
    ]
    for order, first, tiles in CHAINS:
        landing, held = Chain.sizes(order, tiles)
        scratch += [vmem(size + (16, 128), bf16) for size in landing]
        scratch += [vmem((size, 16, 128), bf16) for size in held]
    scratch += [dma((len(CHAINS), 7, 7))] * 2
    whole = pl.BlockSpec(memory_space=vmem)
    section, total = pl.pallas_call(
        functools.partial(section_kernel, tiles_in_row, table_at),
        out_shape=(jax.ShapeDtypeStruct((256, 128), bf16), jax.ShapeDtypeStruct((320, 16, 128), bf16)),
        in_specs=[pl.BlockSpec(memory_space=pltpu.SMEM)] + [pl.BlockSpec(memory_space=pltpu.HBM)] * 7,
        out_specs=(whole, whole),
        scratch_shapes=scratch,
        compiler_params=pltpu.CompilerParams(collective_id=0, has_side_effects=True, vmem_limit_bytes=63 * 2**20),
    )(
        brick_slots, features, occupancy, jnp.asarray(tables), conv1_weight, down_weight, conv2_weight, upstream,
    )
    section, conv1, down, conv2 = pl.pallas_call(
        functools.partial(unpack_kernel, scale),
        out_shape=(
            jax.ShapeDtypeStruct((256, 128), bf16), jax.ShapeDtypeStruct((64, 1728), f32),
            jax.ShapeDtypeStruct((128, 512), f32), jax.ShapeDtypeStruct((128, 3456), f32),
        ),
        in_specs=[whole] * 2,
        out_specs=(whole,) * 4,
        compiler_params=pltpu.CompilerParams(vmem_limit_bytes=63 * 2**20),
    )(section, total)
    return section.reshape(upstream.shape), conv1, down, conv2


def solution(mesh):
    tiles_in_row, scenes = mesh.shape["tile"], mesh.shape["dp"] * 2
    scale = 1.0 / (scenes * tiles_in_row * 2)
    wide = P("dp", "tile", None, None, None)
    return jax.shard_map(
        functools.partial(per_device, tiles_in_row, scale),
        mesh=mesh,
        in_specs=(wide, P("dp", "tile", None, None), P("dp", "tile"), P(), P(), P(), wide),
        out_specs=(wide, P(), P(), P()),
        check_vma=False,
    )
```

```python
import functools

import jax
import jax.numpy as jnp
import numpy as np
from jax import lax
from jax.experimental import pallas as pl
from jax.experimental.pallas import tpu as pltpu
from jax.sharding import PartitionSpec as P

FINE = 64
COARSE = 128
MESH = pl.DeviceIdType.MESH

AXES = {"c": 2, "x": 4, "y": 8, "z": 8}
STAGES = {
    "x": (("rs", "c"), ("rs", "x"), ("rs", "y"), ("ar", "z"), ("ag", "y"), ("ag", "x"), ("ag", "c")),
    "y": (("rs", "c"), ("rs", "y"), ("rs", "x"), ("ar", "z"), ("ag", "x"), ("ag", "y"), ("ag", "c")),
    "z": (("rs", "c"), ("rs", "z"), ("rs", "x"), ("ar", "y"), ("ag", "x"), ("ag", "z"), ("ag", "c")),
}


Y_LOW = 4


def place():
    dp, tile = lax.axis_index("dp"), lax.axis_index("tile")
    c, x, z = AXES["c"], AXES["x"], AXES["z"]
    return {
        "c": lax.rem(tile, c),
        "z": lax.rem(lax.div(tile, c), z),
        "x": lax.rem(lax.div(tile, c * z), x),
        "y": lax.div(tile, c * z * x) * Y_LOW + dp,
    }


def device(at):
    c, x, z = AXES["c"], AXES["x"], AXES["z"]
    tile = ((lax.div(at["y"], Y_LOW) * x + at["x"]) * z + at["z"]) * c + at["c"]
    return {"dp": lax.rem(at["y"], Y_LOW), "tile": tile}


def peer(at, axis, step):
    moved = dict(at)
    moved[axis] = lax.rem(at[axis] + step, AXES[axis])
    return device(moved)


class Chain:
    def __init__(self, order, own, result, landing, held, send, recv, at, peers):
        self.stages, self.at, self.peers = STAGES[order], at, peers
        self.own, self.result, self.landing, self.held = own, result, landing, held
        self.send, self.recv = send, recv
        self.copies = {}

    @staticmethod
    def sizes(order, tiles):
        landing, held = [], []
        for kind, axis in STAGES[order]:
            if kind == "rs":
                tiles //= AXES[axis]
                landing.append((AXES[axis] - 1, tiles))
                held.append(tiles)
            elif kind == "ar":
                landing.append((AXES[axis], tiles))
        return landing, held

    def source(self, stage):
        return self.own if stage == 0 else self.held[stage - 1]

    def offset(self, stages):
        first = 0
        for stage in range(stages):
            first = first + self.at[self.stages[stage][1]] * self.held[stage].shape[0]
        return first

    def start(self, stage):
        kind, axis = self.stages[stage]
        count = AXES[axis]
        for step in range(1, count):
            if kind == "rs":
                part = self.held[stage].shape[0]
                to = lax.rem(self.at[axis] + step, count)
                src = self.source(stage).at[pl.ds(to * part, part)]
                dst = self.landing[stage].at[step - 1]
            elif kind == "ar":
                src = self.source(stage)
                dst = self.landing[stage].at[self.at[axis]]
            else:
                back = len(self.stages) - 1 - stage
                part = self.held[back].shape[0]
                where = pl.ds(self.offset(back + 1), part)
                src = dst = self.result.at[where]
            copy = pltpu.make_async_remote_copy(
                src_ref=src, dst_ref=dst,
                send_sem=self.send.at[stage, step - 1], recv_sem=self.recv.at[stage, step - 1],
                device_id=self.peers[axis, step], device_id_type=MESH,
            )
            copy.start()
            self.copies[stage, step] = copy

    def finish(self, stage):
        kind, axis = self.stages[stage]
        count = AXES[axis]
        for step in range(1, count):
            if kind == "ag":
                back = len(self.stages) - 1 - stage
                part = self.held[back].shape[0]
                origin = dict(self.at)
                origin[axis] = lax.rem(self.at[axis] + count - step, count)
                first = 0
                for earlier in range(back + 1):
                    first = first + origin[self.stages[earlier][1]] * self.held[earlier].shape[0]
                dst = self.result.at[pl.ds(first, part)]
            elif kind == "rs":
                dst = self.landing[stage].at[step - 1]
            else:
                dst = self.landing[stage].at[lax.rem(self.at[axis] + count - step, count)]
            pltpu.make_async_remote_copy(
                src_ref=dst, dst_ref=dst,
                send_sem=self.send.at[stage, step - 1], recv_sem=self.recv.at[stage, step - 1],
                device_id=self.peers[axis, step], device_id_type=MESH,
            ).wait_recv()
        if kind == "rs":
            part = self.held[stage].shape[0]
            mine = self.source(stage)[pl.ds(self.at[axis] * part, part)]
            total = mine.astype(jnp.float32)
            for step in range(1, count):
                total = total + self.landing[stage][step - 1].astype(jnp.float32)
            self.held[stage][...] = total.astype(jnp.bfloat16)
        elif kind == "ar":
            self.landing[stage][self.at[axis]] = self.source(stage)[...]
            total = self.landing[stage][0].astype(jnp.float32)
            for index in range(1, count):
                total = total + self.landing[stage][index].astype(jnp.float32)
            self.result[pl.ds(self.offset(stage), total.shape[0])] = total.astype(jnp.bfloat16)

    def close(self):
        for copy in self.copies.values():
            copy.wait_send()

DOWN_AT, CONV1_AT, TILES = 216, 248, 320
CHAINS = (("x", 0, 128), ("z", 128, 64), ("x", 192, 128))


def fine_selections():
    kept, after, before = np.zeros((3, 5, 64, 2, 64), np.float32)
    order = np.zeros((64, 64), np.float32)
    for y in range(8):
        for z in range(8):
            row = (y % 2) * 32 + (z % 2) * 16 + (y // 2) * 4 + z // 2
            order[row, y * 8 + z] = 1
            for tap in range(9):
                from_y, from_z = y + tap // 3 - 1, z + tap % 3 - 1
                if 0 <= from_z < 8:
                    into = kept if 0 <= from_y < 8 else after if from_y == 8 else before
                    into[tap // 2, row, tap % 2, (from_y % 8) * 8 + from_z] = 1
    return [table.reshape(320, 128) for table in (kept, after, before)] + [order]


def coarse_selections():
    kept, after, before = np.zeros((3, 9, 16, 16), np.float32)
    for y in range(4):
        for z in range(4):
            for tap in range(9):
                from_y, from_z = y + tap // 3 - 1, z + tap % 3 - 1
                if 0 <= from_z < 4:
                    into = kept if 0 <= from_y < 4 else after if from_y == 4 else before
                    into[tap, y * 4 + z, (from_y % 4) * 4 + from_z] = 1
    brick = np.einsum("tij,pq->tpiqj", kept, np.eye(4, dtype=np.float32)).reshape(576, 64)
    return [brick] + [np.tile(table.reshape(144, 16), (1, 8)) for table in (kept, after, before)]


def selections():
    tables = fine_selections() + coarse_selections()
    first = np.cumsum([0] + [table.shape[0] for table in tables])
    padded = [np.pad(table, ((0, 0), (0, 128 - table.shape[1]))) for table in tables]
    return np.concatenate(padded).astype(jnp.bfloat16), [int(place) for place in first]


def gate_slope(value):
    gate = jax.nn.sigmoid(value)
    return value * gate, gate * (1.0 + value * (1.0 - gate))


def dot(left, right, left_dim, right_dim):
    return lax.dot_general(left, right, (((left_dim,), (right_dim,)), ((), ())), preferred_element_type=jnp.float32)


def section_kernel(
    tiles_in_row, table_at,
    slots_ref, features_hbm, occupancy_hbm, tables_hbm, w1_hbm, wd_hbm, w2_hbm, upstream_hbm,
    section_ref, total_ref,
    features_ref, occupancy_ref, tables_ref, w1_ref, wd_ref, w2_ref, upstream_ref, load_sem,
    near_features, near_occupancy, near_upstream, near_rows, own_rows, halo_send, halo_recv,
    parts, xs, near_xs, w1p, w2f, mk, slope1, child, grad1, gate2, slope2, act2, edge2, edge3, im2, img, grad2,
    *scratch,
):
    loads = []
    operands = (
        (features_hbm, features_ref), (occupancy_hbm, occupancy_ref), (tables_hbm, tables_ref), (w1_hbm, w1_ref),
        (w2_hbm, w2_ref), (wd_hbm, wd_ref), (upstream_hbm, upstream_ref),
    )
    for index, (source, target) in enumerate(operands):
        loads.append(pltpu.make_async_copy(source, target, load_sem.at[index]))
        loads[-1].start()
    kept1_ref, after1_ref, before1_ref, order_ref, kept2_ref, kept8_ref, after8_ref, before8_ref = [
        tables_ref.at[first:last] for first, last in zip(table_at, table_at[1:])
    ]
    at = place()
    tile = lax.axis_index("tile")
    left, right = lax.rem(tile + tiles_in_row - 1, tiles_in_row), lax.rem(tile + 1, tiles_in_row)
    peers = {(axis, step): peer(at, axis, step) for axis, count in AXES.items() for step in range(1, count)}
    scratch = list(scratch)
    send, recv = scratch.pop(), scratch.pop()
    chains = []
    for index, (order, first, tiles) in enumerate(CHAINS):
        landing = [scratch.pop(0) for _ in range(4)]
        held = [scratch.pop(0) for _ in range(3)]
        where = pl.ds(first, tiles)
        chains.append(Chain(order, parts.at[where], total_ref.at[where], landing, held, send.at[index], recv.at[index], at, peers))

    barrier = pltpu.get_barrier_semaphore()
    met = 0
    for near in (left, right):
        pl.semaphore_signal(barrier, inc=1, device_id={"tile": near}, device_id_type=MESH)
        met += 1
    for other in peers.values():
        pl.semaphore_signal(barrier, inc=1, device_id=other, device_id_type=MESH)
        met += 1

    def row_of(scene, column):
        return lax.rem(slots_ref[scene, column], 2).astype(jnp.float32)

    for side in range(2):
        for scene in range(2):
            own_rows[side, scene] = jnp.full((16, 128), row_of(scene, 1 - side), jnp.float32).astype(jnp.bfloat16)
    pl.semaphore_wait(barrier, met)
    halos = []
    for side, near in enumerate((right, left)):
        column, planes, border = ((1, pl.ds(3, 5), 3), (0, pl.ds(0, 5), 0))[side]
        pieces = (
            (features_hbm.at[:, column, planes], near_features.at[side]),
            (occupancy_hbm.at[:, column], near_occupancy.at[side]),
            (own_rows.at[side], near_rows.at[side]),
            (upstream_hbm.at[:, column, border], near_upstream.at[side]),
        )
        for index, (source, target) in enumerate(pieces):
            copy = pltpu.make_async_remote_copy(
                src_ref=source, dst_ref=target, send_sem=halo_send.at[side, index], recv_sem=halo_recv.at[side, index],
                device_id={"tile": near}, device_id_type=MESH,
            )
            copy.start()
            halos.append(copy)

    same_half = lax.broadcasted_iota(jnp.int32, (128, 128), 0) // 64 == lax.broadcasted_iota(jnp.int32, (128, 128), 1) // 64
    same_half = same_half.astype(jnp.float32).astype(jnp.bfloat16)

    def blocks(plane, gate):
        plane = (plane.astype(jnp.float32) * gate).astype(jnp.bfloat16)
        twice = jnp.concatenate([plane, plane], axis=1)
        return jnp.concatenate([twice, twice], axis=0) * same_half

    def own_plane(brick, x):
        return blocks(features_ref[brick // 2, brick % 2, x], gate_row(occupancy_ref[brick // 2, brick % 2], x))

    def gate_row(occupied, x):
        return occupied[x:x + 1, :].astype(jnp.float32)

    def keep1(moved, into):
        moved = moved.astype(jnp.bfloat16)
        for pair in range(5):
            into[:, pair * 128:pair * 128 + 128] = moved[pair * 64:pair * 64 + 64]

    def voxel_gate(row):
        return dot(order_ref[:, 0:64], jnp.broadcast_to(row, (128, 64)).astype(jnp.bfloat16), 1, 1)

    def coarse_gate(first):
        largest = None
        for a in range(2):
            for quarter in range(4):
                part = mk[first + a, quarter * 16:quarter * 16 + 16, :]
                largest = part if largest is None else jnp.maximum(largest, part)
        return largest

    for load in loads:
        load.wait()
    for step in range(3):
        taps = w1_ref[:, step * 576:step * 576 + 576]
        w1p[step] = jnp.concatenate([taps, jnp.zeros((64, 64), jnp.bfloat16)], axis=1)

    def local_planes(brick, carry):
        scene, column = lax.div(brick, 2), lax.rem(brick, 2)
        occupied = occupancy_ref[scene, column]
        for x in range(8):
            row = gate_row(occupied, x)
            keep1(dot(kept1_ref[...], blocks(features_ref[scene, column, x], row), 1, 1), xs.at[brick, x + 1])
            mk[brick * 8 + x] = voxel_gate(row)
        for x in range(4):
            gate2[brick * 4 + x] = coarse_gate(brick * 8 + 2 * x)
        return carry

    lax.fori_loop(0, 4, local_planes, 0)
    for tap in range(27):
        w2f[tap * 128:tap * 128 + 128, :] = w2_ref[:, (26 - tap) * 128:(26 - tap) * 128 + 128]

    def shares(from_row, to_row, valid):
        apart = from_row - to_row
        return [share * valid for share in (1.0 - apart * apart, 0.5 * apart * (apart + 1.0), 0.5 * apart * (apart - 1.0))]

    rows = [[jnp.full((1, 128), row_of(scene, column), jnp.float32) for column in range(2)] for scene in range(2)]
    has_left = (tile > 0).astype(jnp.float32)
    has_right = (tile < tiles_in_row - 1).astype(jnp.float32)

    def border1(plane, share, into):
        share = [part.astype(jnp.bfloat16) for part in share]
        moves = kept1_ref[...] * share[0] + after1_ref[...] * share[1] + before1_ref[...] * share[2]
        keep1(dot(moves, plane, 1, 1), into)

    share_of = {}
    for scene in range(2):
        share_of[scene, 1] = shares(rows[scene][1], rows[scene][0], 1.0)
        share_of[scene, 2] = shares(rows[scene][0], rows[scene][1], 1.0)
        border1(own_plane(scene * 2 + 1, 0), share_of[scene, 1], xs.at[scene * 2, 9])
        border1(own_plane(scene * 2, 7), share_of[scene, 2], xs.at[scene * 2 + 1, 0])

    def fine(source, first, count, gates, children, child_row, first_x, slopes):
        pre = None
        for step in range(3):
            window = source[first + step:first + step + count].reshape(count * 64, 640)
            term = dot(window, w1p[step], 1, 1)
            pre = term if pre is None else pre + term
        mask = gates[:, :, 0:64].reshape(count * 64, 64)
        act, slope = gate_slope(pre)
        if slopes is not None:
            slopes[...] = (slope * mask).reshape(count, 64, 64)
        act = (act * mask).astype(jnp.bfloat16).reshape(count, 4, 16, 64)
        for index in range(count):
            x = first_x + index
            for half in range(2):
                pair = jnp.concatenate([act[index, 2 * half], act[index, 2 * half + 1]], axis=1)
                lanes = (x % 2 * 2 + half) * 128
                children[pl.ds(child_row + x // 2 * 16, 16), lanes:lanes + 128] = pair

    def inner_planes(scene, carry):
        for column in range(2):
            brick = scene * 2 + column
            first = 1 - column
            fine(
                xs.at[brick], first, 7, mk[pl.ds(brick * 8 + first, 7)], child, brick * 64, first,
                slope1.at[brick, pl.ds(first, 7)],
            )
        return carry

    lax.fori_loop(0, 2, inner_planes, 0)

    for copy in halos:
        copy.wait_recv()

    def near_planes(unit, carry):
        side, scene = lax.div(unit, 2), lax.rem(unit, 2)
        occupied = near_occupancy[side, scene].astype(jnp.float32)
        after = (side == 0).astype(jnp.float32)
        for x in range(5):
            row = occupied[x + 3:x + 4] * after + occupied[x:x + 1] * (1.0 - after)
            moved = dot(kept1_ref[...], blocks(near_features[side, scene, x], row), 1, 1)
            keep1(moved, near_xs.at[unit, x + side])
            near_gate = voxel_gate(row)
            mk[32 + unit * 5 + x] = near_gate
        for x in range(2):
            gate2[16 + unit * 2 + x] = coarse_gate(32 + unit * 5 + 1 - side + 2 * x)
        return carry

    lax.fori_loop(0, 4, near_planes, 0)
    for scene in range(2):
        from_left = near_rows[0, scene].astype(jnp.float32)[0:1]
        from_right = near_rows[1, scene].astype(jnp.float32)[0:1]
        to_left = shares(from_left, rows[scene][0], has_left)
        to_right = shares(from_right, rows[scene][1], has_right)
        share_of[scene, 0], share_of[scene, 3] = to_left, to_right
        share_of[scene, 4] = [to_left[0], to_left[2], to_left[1]]
        share_of[scene, 5] = [to_right[0], to_right[2], to_right[1]]
        last = blocks(near_features[0, scene, 4], gate_row(near_occupancy[0, scene], 7))
        border1(last, share_of[scene, 0], xs.at[scene * 2, 0])
        first = blocks(near_features[1, scene, 0], gate_row(near_occupancy[1, scene], 0))
        border1(first, share_of[scene, 3], xs.at[scene * 2 + 1, 9])
        border1(own_plane(scene * 2, 0), share_of[scene, 4], near_xs.at[scene, 5])
        border1(own_plane(scene * 2 + 1, 7), share_of[scene, 5], near_xs.at[2 + scene, 0])

    for scene in range(2):
        brick = scene * 2
        fine(xs.at[brick], 0, 1, mk[brick * 8:brick * 8 + 1], child, brick * 64, 0, slope1.at[brick, 0:1])
        brick = scene * 2 + 1
        fine(xs.at[brick], 7, 1, mk[brick * 8 + 7:brick * 8 + 8], child, brick * 64, 7, slope1.at[brick, 7:8])

    for unit in range(4):
        first = 32 + unit * 5 + (1 if unit < 2 else 0)
        fine(near_xs.at[unit], 0, 4, mk[first:first + 4], child, 256 + unit * 32, 0, None)

    gate = gate2[...].reshape(384, 128)
    down_pre = dot(child[...], wd_ref[...], 1, 1)
    act, slope = gate_slope(down_pre)
    slope2[...] = slope[0:256] * gate[0:256]
    act2[...] = (act * gate).astype(jnp.bfloat16).reshape(24, 16, 128)

    def lanes_of(tap, step):
        first = (step * 9 + tap) * 128
        return slice(first, first + 128)

    def inner2(values, into):
        for brick in range(4):
            moved = dot(kept2_ref[:, 0:64], values[brick * 4:brick * 4 + 4].reshape(64, 128), 1, 0).astype(jnp.bfloat16)
            base = brick * 64
            for tap in range(9):
                here = moved[tap * 64:tap * 64 + 64]
                into[base + 16:base + 64, lanes_of(tap, 0)] = here[0:48]
                into[base:base + 64, lanes_of(tap, 1)] = here
                into[base:base + 48, lanes_of(tap, 2)] = here[16:64]

    def border2(values, near, into):
        planes = []
        for scene in range(2):
            planes += [near[0][scene], values[scene * 8 + 4], values[scene * 8 + 3], near[1][scene]]
        moved = dot(edge2[...], jnp.concatenate(planes, axis=0), 1, 0).astype(jnp.bfloat16)
        for tap in range(9):
            for brick in range(4):
                first = tap * 128 + brick * 32
                base = brick * 64
                into[base:base + 16, lanes_of(tap, 0)] = moved[first:first + 16]
                into[base + 48:base + 64, lanes_of(tap, 2)] = moved[first + 16:first + 32]

    def near2():
        outer = [act2[16 + 4 * side:20 + 4 * side].reshape(64, 128) for side in range(2)]
        moved = [dot(kept2_ref[:, 0:64], part, 1, 0).astype(jnp.bfloat16) for part in outer]
        planes = [act2[scene * 8 + plane] for scene in range(2) for plane in (0, 7)]
        edges = dot(edge3[:, 0:64], jnp.concatenate(planes, axis=0), 1, 0).astype(jnp.bfloat16)
        for tap in range(9):
            for scene in range(2):
                first = tap * 64 + scene * 32
                base = 256 + scene * 16
                im2[base:base + 16, lanes_of(tap, 0)] = moved[0][first:first + 16]
                im2[base:base + 16, lanes_of(tap, 1)] = moved[0][first + 16:first + 32]
                im2[base:base + 16, lanes_of(tap, 2)] = edges[first:first + 16]
                im2[base + 32:base + 48, lanes_of(tap, 0)] = edges[first + 16:first + 32]
                im2[base + 32:base + 48, lanes_of(tap, 1)] = moved[1][first:first + 16]
                im2[base + 32:base + 48, lanes_of(tap, 2)] = moved[1][first + 16:first + 32]

    def edges_of(roles, count):
        lane = lax.broadcasted_iota(jnp.int32, (1, 128), 1) // 16
        shared = [jnp.zeros((1, 128), jnp.float32) for _ in range(3)]
        for index, role in enumerate(roles):
            own = (lane == index).astype(jnp.float32)
            shared = [so_far + own * part for so_far, part in zip(shared, share_of[role])]
        shared = [part.astype(jnp.bfloat16) for part in shared]
        same = lax.broadcasted_iota(jnp.int32, (count, 16, 128), 0) == lax.broadcasted_iota(jnp.int32, (count, 16, 128), 2) // 16
        same = same.astype(jnp.float32).astype(jnp.bfloat16).reshape(1, count, 16, 128)
        moves = kept8_ref[...] * shared[0] + after8_ref[...] * shared[1] + before8_ref[...] * shared[2]
        return (moves.reshape(9, 1, 16, 128) * same).reshape(9 * count * 16, 128)

    edge2[...] = edges_of([(scene, role) for scene in range(2) for role in range(4)], 8)
    edge3[...] = edges_of([(scene, role) for scene in range(2) for role in (4, 5)], 4)
    inner2(act2, im2)
    border2(act2, ([act2[17], act2[19]], [act2[20], act2[22]]), im2)
    near2()
    coarse_pre = dot(im2[...], w2_ref[...], 1, 1)
    act, slope = gate_slope(coarse_pre)
    section_ref[...] = (act[0:256] * gate[0:256]).astype(jnp.bfloat16)
    upstream = [upstream_ref[...].reshape(256, 128), near_upstream[...].reshape(64, 128)]
    gates = [gate[0:256], gate[272:288], gate[304:320], gate[320:336], gate[352:368]]
    upstream = jnp.concatenate(upstream, axis=0).astype(jnp.float32) * jnp.concatenate(gates, axis=0)
    grad2[...] = (upstream * slope).astype(jnp.bfloat16).reshape(20, 16, 128)

    def keep_parts(values, first, width, lane_tile):
        values = values.astype(jnp.bfloat16)
        for block in range(values.shape[0] // 16):
            for column in range(values.shape[1] // 128):
                parts[first + block * width + lane_tile + column] = values[block * 16:block * 16 + 16, column * 128:column * 128 + 128]

    grad_rows = grad2[0:16].reshape(256, 128)
    for step in range(3):
        keep_parts(dot(grad_rows, im2[0:256, step * 1152:step * 1152 + 1152], 0, 0), 0, 27, step * 9)
    for chain in chains[:-1]:
        chain.start(0)
    inner2(grad2, img)
    border2(grad2, ([grad2[16], grad2[17]], [grad2[18], grad2[19]]), img)
    down_back = dot(img[...], w2f[...], 1, 0)
    down_in = (down_back * slope2[...]).astype(jnp.bfloat16)
    keep_parts(dot(down_in, child[0:256], 0, 0), DOWN_AT, 4, 0)

    def advance(some, stage):
        for chain in some:
            chain.finish(stage - 1)
            if stage < len(STAGES["x"]):
                chain.start(stage)

    advance(chains[:-1], 1)

    fine_back = dot(down_in, wd_ref[...], 1, 0)
    for brick in range(4):
        for x in range(8):
            base = brick * 64 + x // 2 * 16
            first = x % 2 * 256
            back = [fine_back[base:base + 16, first + part * 64:first + part * 64 + 64] for part in range(4)]
            grad1[brick, x] = (jnp.concatenate(back, axis=0) * slope1[brick, x]).astype(jnp.bfloat16)
    for step in range(3):
        term = None
        for brick in range(4):
            window = xs[brick, step:step + 8].reshape(512, 640)
            part = dot(grad1[brick].reshape(512, 64), window, 0, 0)
            term = part if term is None else term + part
        keep_parts(term, CONV1_AT, 15, step * 5)
    parts[CONV1_AT + 60:TILES] = jnp.zeros((TILES - CONV1_AT - 60, 16, 128), jnp.bfloat16)
    chains[-1].start(0)

    for stage in range(1, len(STAGES["x"]) + 1):
        if stage < len(STAGES["x"]):
            advance(chains[:-1], stage + 1)
        advance(chains[-1:], stage)
    for copy in halos:
        copy.wait_send()
    for chain in chains:
        chain.close()


def unpack_kernel(scale, section_ref, total_ref, section_out, conv1_ref, down_ref, conv2_ref):
    section_out[...] = section_ref[...]
    for block in range(8):
        rows = slice(block * 16, block * 16 + 16)
        for column in range(27):
            conv2_ref[rows, column * 128:column * 128 + 128] = total_ref[block * 27 + column].astype(jnp.float32) * scale
        for column in range(4):
            down_ref[rows, column * 128:column * 128 + 128] = total_ref[DOWN_AT + block * 4 + column].astype(jnp.float32) * scale
    for block in range(4):
        rows = slice(block * 16, block * 16 + 16)
        taps = []
        for step in range(3):
            whole = [total_ref[CONV1_AT + block * 15 + step * 5 + pair].astype(jnp.float32) * scale for pair in range(5)]
            taps += whole[:4] + [whole[4][:, 0:64]]
        conv1_ref[rows, :] = jnp.concatenate(taps, axis=1)


def per_device(tiles_in_row, scale, features, occupancy, brick_slots, conv1_weight, down_weight, conv2_weight, upstream):
    tables, table_at = selections()
    bf16, f32 = jnp.bfloat16, jnp.float32
    vmem, dma = pltpu.VMEM, pltpu.SemaphoreType.DMA
    scratch = [
        vmem((2, 2, 8, 64, 64), bf16), vmem((2, 2, 8, 64), jnp.int32), vmem(tables.shape, bf16), vmem((64, 1728), bf16),
        vmem((128, 512), bf16), vmem((128, 3456), bf16), vmem((2, 2, 4, 16, 128), bf16), dma((7,)),
        vmem((2, 2, 5, 64, 64), bf16), vmem((2, 2, 8, 64), jnp.int32), vmem((2, 2, 16, 128), bf16),
        vmem((2, 2, 16, 128), bf16), vmem((2, 2, 16, 128), bf16), dma((2, 4)), dma((2, 4)),
        vmem((TILES, 16, 128), bf16), vmem((4, 10, 64, 640), bf16), vmem((4, 6, 64, 640), bf16), vmem((3, 64, 640), bf16),
        vmem((3456, 128), bf16), vmem((52, 64, 128), f32), vmem((4, 8, 64, 64), f32), vmem((384, 512), bf16),
        vmem((4, 8, 64, 64), bf16), vmem((24, 16, 128), f32), vmem((256, 128), f32), vmem((24, 16, 128), bf16),
        vmem((1152, 128), bf16), vmem((576, 128), bf16), vmem((320, 3456), bf16), vmem((256, 3456), bf16),
        vmem((20, 16, 128), bf16),
    ]
    for order, first, tiles in CHAINS:
        landing, held = Chain.sizes(order, tiles)
        scratch += [vmem(size + (16, 128), bf16) for size in landing]
        scratch += [vmem((size, 16, 128), bf16) for size in held]
    scratch += [dma((len(CHAINS), 7, 7))] * 2
    whole = pl.BlockSpec(memory_space=vmem)
    section, total = pl.pallas_call(
        functools.partial(section_kernel, tiles_in_row, table_at),
        out_shape=(jax.ShapeDtypeStruct((256, 128), bf16), jax.ShapeDtypeStruct((TILES, 16, 128), bf16)),
        in_specs=[pl.BlockSpec(memory_space=pltpu.SMEM)] + [pl.BlockSpec(memory_space=pltpu.HBM)] * 7,
        out_specs=(whole, whole),
        scratch_shapes=scratch,
        compiler_params=pltpu.CompilerParams(collective_id=0, has_side_effects=True, vmem_limit_bytes=63 * 2**20),
    )(
        brick_slots, features, occupancy, jnp.asarray(tables), conv1_weight, down_weight, conv2_weight, upstream,
    )
    section, conv1, down, conv2 = pl.pallas_call(
        functools.partial(unpack_kernel, scale),
        out_shape=(
            jax.ShapeDtypeStruct((256, 128), bf16), jax.ShapeDtypeStruct((64, 1728), f32),
            jax.ShapeDtypeStruct((128, 512), f32), jax.ShapeDtypeStruct((128, 3456), f32),
        ),
        in_specs=[whole] * 2,
        out_specs=(whole,) * 4,
        compiler_params=pltpu.CompilerParams(vmem_limit_bytes=63 * 2**20),
    )(section, total)
    return section.reshape(upstream.shape), conv1, down, conv2


def solution(mesh):
    tiles_in_row, scenes = mesh.shape["tile"], mesh.shape["dp"] * 2
    scale = 1.0 / (scenes * tiles_in_row * 2)
    wide = P("dp", "tile", None, None, None)
    return jax.shard_map(
        functools.partial(per_device, tiles_in_row, scale),
        mesh=mesh,
        in_specs=(wide, P("dp", "tile", None, None), P("dp", "tile"), P(), P(), P(), wide),
        out_specs=(wide, P(), P(), P()),
        check_vma=False,
    )
```

```python
import functools

import jax
import jax.numpy as jnp
import numpy as np
from jax import lax
from jax.experimental import pallas as pl
from jax.experimental.pallas import tpu as pltpu
from jax.sharding import PartitionSpec as P

FINE = 64
COARSE = 128
MESH = pl.DeviceIdType.MESH

AXES = {"c": 2, "x": 4, "y": 8, "z": 8}
STAGES = {
    "x": (("rs", "c"), ("rs", "x"), ("rs", "y"), ("ar", "z"), ("ag", "y"), ("ag", "x"), ("ag", "c")),
    "y": (("rs", "c"), ("rs", "y"), ("rs", "x"), ("ar", "z"), ("ag", "x"), ("ag", "y"), ("ag", "c")),
    "z": (("rs", "c"), ("rs", "z"), ("rs", "x"), ("ar", "y"), ("ag", "x"), ("ag", "z"), ("ag", "c")),
}


Y_LOW = 4


def place():
    dp, tile = lax.axis_index("dp"), lax.axis_index("tile")
    c, x, z = AXES["c"], AXES["x"], AXES["z"]
    return {
        "c": lax.rem(tile, c),
        "z": lax.rem(lax.div(tile, c), z),
        "x": lax.rem(lax.div(tile, c * z), x),
        "y": lax.div(tile, c * z * x) * Y_LOW + dp,
    }


def device(at):
    c, x, z = AXES["c"], AXES["x"], AXES["z"]
    tile = ((lax.div(at["y"], Y_LOW) * x + at["x"]) * z + at["z"]) * c + at["c"]
    return {"dp": lax.rem(at["y"], Y_LOW), "tile": tile}


def peer(at, axis, step):
    moved = dict(at)
    moved[axis] = lax.rem(at[axis] + step, AXES[axis])
    return device(moved)


def far_first(count):
    return sorted(range(1, count), key=lambda step: -min(step, count - step))


class Chain:
    def __init__(self, order, own, result, landing, held, send, recv, at, peers):
        self.stages, self.at, self.peers = STAGES[order], at, peers
        self.own, self.result, self.landing, self.held = own, result, landing, held
        self.send, self.recv = send, recv
        self.copies = {}

    @staticmethod
    def sizes(order, tiles):
        landing, held = [], []
        for kind, axis in STAGES[order]:
            if kind == "rs":
                tiles //= AXES[axis]
                landing.append((AXES[axis] - 1, tiles))
                held.append(tiles)
            elif kind == "ar":
                landing.append((AXES[axis], tiles))
        return landing, held

    def source(self, stage):
        return self.own if stage == 0 else self.held[stage - 1]

    def offset(self, stages):
        first = 0
        for stage in range(stages):
            first = first + self.at[self.stages[stage][1]] * self.held[stage].shape[0]
        return first

    def start(self, stage):
        kind, axis = self.stages[stage]
        count = AXES[axis]
        for step in far_first(count):
            if kind == "rs":
                part = self.held[stage].shape[0]
                to = lax.rem(self.at[axis] + step, count)
                src = self.source(stage).at[pl.ds(to * part, part)]
                dst = self.landing[stage].at[step - 1]
            elif kind == "ar":
                src = self.source(stage)
                dst = self.landing[stage].at[self.at[axis]]
            else:
                back = len(self.stages) - 1 - stage
                part = self.held[back].shape[0]
                where = pl.ds(self.offset(back + 1), part)
                src = dst = self.result.at[where]
            copy = pltpu.make_async_remote_copy(
                src_ref=src, dst_ref=dst,
                send_sem=self.send.at[stage, step - 1], recv_sem=self.recv.at[stage, step - 1],
                device_id=self.peers[axis, step], device_id_type=MESH,
            )
            copy.start()
            self.copies[stage, step] = copy

    def finish(self, stage):
        kind, axis = self.stages[stage]
        count = AXES[axis]
        for step in range(1, count):
            if kind == "ag":
                back = len(self.stages) - 1 - stage
                part = self.held[back].shape[0]
                origin = dict(self.at)
                origin[axis] = lax.rem(self.at[axis] + count - step, count)
                first = 0
                for earlier in range(back + 1):
                    first = first + origin[self.stages[earlier][1]] * self.held[earlier].shape[0]
                dst = self.result.at[pl.ds(first, part)]
            elif kind == "rs":
                dst = self.landing[stage].at[step - 1]
            else:
                dst = self.landing[stage].at[lax.rem(self.at[axis] + count - step, count)]
            pltpu.make_async_remote_copy(
                src_ref=dst, dst_ref=dst,
                send_sem=self.send.at[stage, step - 1], recv_sem=self.recv.at[stage, step - 1],
                device_id=self.peers[axis, step], device_id_type=MESH,
            ).wait_recv()
        if kind == "rs":
            part = self.held[stage].shape[0]
            mine = self.source(stage)[pl.ds(self.at[axis] * part, part)]
            total = mine.astype(jnp.float32)
            for step in range(1, count):
                total = total + self.landing[stage][step - 1].astype(jnp.float32)
            self.held[stage][...] = total.astype(jnp.bfloat16)
        elif kind == "ar":
            self.landing[stage][self.at[axis]] = self.source(stage)[...]
            total = self.landing[stage][0].astype(jnp.float32)
            for index in range(1, count):
                total = total + self.landing[stage][index].astype(jnp.float32)
            self.result[pl.ds(self.offset(stage), total.shape[0])] = total.astype(jnp.bfloat16)

    def close(self):
        for copy in self.copies.values():
            copy.wait_send()

DOWN_AT, CONV1_AT, TILES = 216, 256, 320
CHAINS = (("x", 0, 128), ("y", 128, 64), ("z", 192, 64), ("x", 256, 64))


def fine_selections():
    kept, after, before = np.zeros((3, 5, 64, 2, 64), np.float32)
    order = np.zeros((64, 64), np.float32)
    for y in range(8):
        for z in range(8):
            row = (y % 2) * 32 + (z % 2) * 16 + (y // 2) * 4 + z // 2
            order[row, y * 8 + z] = 1
            for tap in range(9):
                from_y, from_z = y + tap // 3 - 1, z + tap % 3 - 1
                if 0 <= from_z < 8:
                    into = kept if 0 <= from_y < 8 else after if from_y == 8 else before
                    into[tap // 2, row, tap % 2, (from_y % 8) * 8 + from_z] = 1
    return [table.reshape(320, 128) for table in (kept, after, before)] + [order]


def coarse_selections():
    kept, after, before = np.zeros((3, 9, 16, 16), np.float32)
    for y in range(4):
        for z in range(4):
            for tap in range(9):
                from_y, from_z = y + tap // 3 - 1, z + tap % 3 - 1
                if 0 <= from_z < 4:
                    into = kept if 0 <= from_y < 4 else after if from_y == 4 else before
                    into[tap, y * 4 + z, (from_y % 4) * 4 + from_z] = 1
    brick = np.einsum("tij,pq->tpiqj", kept, np.eye(4, dtype=np.float32)).reshape(576, 64)
    return [brick] + [np.tile(table.reshape(144, 16), (1, 8)) for table in (kept, after, before)]


def selections():
    tables = fine_selections() + coarse_selections()
    first = np.cumsum([0] + [table.shape[0] for table in tables])
    padded = [np.pad(table, ((0, 0), (0, 128 - table.shape[1]))) for table in tables]
    return np.concatenate(padded).astype(jnp.bfloat16), [int(place) for place in first]


def gate_slope(value):
    gate = jax.nn.sigmoid(value)
    return value * gate, gate * (1.0 + value * (1.0 - gate))


def dot(left, right, left_dim, right_dim):
    return lax.dot_general(left, right, (((left_dim,), (right_dim,)), ((), ())), preferred_element_type=jnp.float32)


def section_kernel(
    tiles_in_row, table_at,
    slots_ref, features_hbm, occupancy_hbm, tables_hbm, w1_hbm, wd_hbm, w2_hbm, upstream_hbm,
    section_ref, total_ref,
    features_ref, occupancy_ref, tables_ref, w1_ref, wd_ref, w2_ref, upstream_ref, load_sem,
    outgoing, near, halo_send, halo_recv,
    parts, xs, near_xs, w1p, w2f, mk, slope1, child, grad1, gate2, slope2, act2, edge2, edge3, im2, img, grad2,
    *scratch,
):
    loads = []
    operands = (
        (features_hbm, features_ref), (occupancy_hbm, occupancy_ref), (upstream_hbm, upstream_ref), (tables_hbm, tables_ref),
        (w1_hbm, w1_ref), (w2_hbm, w2_ref), (wd_hbm, wd_ref),
    )
    for index, (source, target) in enumerate(operands):
        loads.append(pltpu.make_async_copy(source, target, load_sem.at[index]))
        loads[-1].start()
    kept1_ref, after1_ref, before1_ref, order_ref, kept2_ref, kept8_ref, after8_ref, before8_ref = [
        tables_ref.at[first:last] for first, last in zip(table_at, table_at[1:])
    ]
    at = place()
    tile = lax.axis_index("tile")
    left, right = lax.rem(tile + tiles_in_row - 1, tiles_in_row), lax.rem(tile + 1, tiles_in_row)
    peers = {(axis, step): peer(at, axis, step) for axis, count in reversed(AXES.items()) for step in far_first(count)}
    scratch = list(scratch)
    send, recv = scratch.pop(), scratch.pop()
    chains = []
    for index, (order, first, tiles) in enumerate(CHAINS):
        landing = [scratch.pop(0) for _ in range(4)]
        held = [scratch.pop(0) for _ in range(3)]
        where = pl.ds(first, tiles)
        chains.append(Chain(order, parts.at[where], total_ref.at[where], landing, held, send.at[index], recv.at[index], at, peers))

    barrier = pltpu.get_barrier_semaphore()
    met = 0
    for other in (left, right):
        pl.semaphore_signal(barrier, inc=1, device_id={"tile": other}, device_id_type=MESH)
        met += 1
    for other in peers.values():
        pl.semaphore_signal(barrier, inc=1, device_id=other, device_id_type=MESH)
        met += 1

    def row_of(scene, column):
        return lax.rem(slots_ref[scene, column], 2).astype(jnp.float32)

    same_half = lax.broadcasted_iota(jnp.int32, (128, 128), 0) // 64 == lax.broadcasted_iota(jnp.int32, (128, 128), 1) // 64
    same_half = same_half.astype(jnp.float32).astype(jnp.bfloat16)

    def twice(plane, gate):
        plane = (plane.astype(jnp.float32) * gate).astype(jnp.bfloat16)
        return jnp.concatenate([plane, plane], axis=1)

    def diagonal(both):
        return jnp.concatenate([both, both], axis=0) * same_half

    def blocks(plane, gate):
        return diagonal(twice(plane, gate))

    def own_plane(brick, x):
        return blocks(features_ref[brick // 2, brick % 2, x], gate_row(occupancy_ref[brick // 2, brick % 2], x))

    def gate_row(occupied, x):
        return occupied[x:x + 1, :].astype(jnp.float32)

    loads[0].wait()
    loads[1].wait()
    loads[2].wait()
    for side in range(2):
        column, first_x, border = ((1, 3, 3), (0, 0, 0))[side]
        for scene in range(2):
            occupied = occupancy_ref[scene, column].astype(jnp.float32)
            for index in range(5):
                x = first_x + index
                both = twice(features_ref[scene, column, x], occupied[x:x + 1])
                outgoing[side, scene, index * 64:index * 64 + 64, :] = both
            row = jnp.full((8, 128), row_of(scene, column), jnp.float32)
            gates = jnp.concatenate([jnp.concatenate([occupied, occupied], axis=1), row], axis=0)
            outgoing[side, scene, 320:336, :] = gates.astype(jnp.bfloat16)
            outgoing[side, scene, 336:352, :] = upstream_ref[scene, column, border]
    pl.semaphore_wait(barrier, met)
    halos = []
    for side, other in enumerate((right, left)):
        copy = pltpu.make_async_remote_copy(
            src_ref=outgoing.at[side], dst_ref=near.at[side], send_sem=halo_send.at[side], recv_sem=halo_recv.at[side],
            device_id={"tile": other}, device_id_type=MESH,
        )
        copy.start()
        halos.append(copy)

    def keep1(moved, into):
        moved = moved.astype(jnp.bfloat16)
        for pair in range(5):
            into[:, pair * 128:pair * 128 + 128] = moved[pair * 64:pair * 64 + 64]

    def voxel_gate(row):
        return dot(order_ref[:, 0:64], jnp.broadcast_to(row, (128, 64)).astype(jnp.bfloat16), 1, 1)

    def coarse_gate(first):
        largest = None
        for a in range(2):
            for quarter in range(4):
                part = mk[first + a, quarter * 16:quarter * 16 + 16, :]
                largest = part if largest is None else jnp.maximum(largest, part)
        return largest

    for load in loads[3:]:
        load.wait()
    for step in range(3):
        taps = w1_ref[:, step * 576:step * 576 + 576]
        w1p[step] = jnp.concatenate([taps, jnp.zeros((64, 64), jnp.bfloat16)], axis=1)

    def local_planes(brick, carry):
        scene, column = lax.div(brick, 2), lax.rem(brick, 2)
        occupied = occupancy_ref[scene, column]
        for x in range(8):
            row = gate_row(occupied, x)
            keep1(dot(kept1_ref[...], blocks(features_ref[scene, column, x], row), 1, 1), xs.at[brick, x + 1])
            mk[brick * 8 + x] = voxel_gate(row)
        for x in range(4):
            gate2[brick * 4 + x] = coarse_gate(brick * 8 + 2 * x)
        return carry

    lax.fori_loop(0, 4, local_planes, 0)
    for tap in range(27):
        w2f[tap * 128:tap * 128 + 128, :] = w2_ref[:, (26 - tap) * 128:(26 - tap) * 128 + 128]

    def shares(from_row, to_row, valid):
        apart = from_row - to_row
        return [share * valid for share in (1.0 - apart * apart, 0.5 * apart * (apart + 1.0), 0.5 * apart * (apart - 1.0))]

    rows = [[jnp.full((1, 128), row_of(scene, column), jnp.float32) for column in range(2)] for scene in range(2)]
    has_left = (tile > 0).astype(jnp.float32)
    has_right = (tile < tiles_in_row - 1).astype(jnp.float32)

    def border1(plane, share, into):
        share = [part.astype(jnp.bfloat16) for part in share]
        moves = kept1_ref[...] * share[0] + after1_ref[...] * share[1] + before1_ref[...] * share[2]
        keep1(dot(moves, plane, 1, 1), into)

    share_of = {}
    for scene in range(2):
        share_of[scene, 1] = shares(rows[scene][1], rows[scene][0], 1.0)
        share_of[scene, 2] = shares(rows[scene][0], rows[scene][1], 1.0)
        border1(own_plane(scene * 2 + 1, 0), share_of[scene, 1], xs.at[scene * 2, 9])
        border1(own_plane(scene * 2, 7), share_of[scene, 2], xs.at[scene * 2 + 1, 0])

    def fine(source, first, count, gates, children, child_row, first_x, slopes):
        pre = None
        for step in range(3):
            window = source[first + step:first + step + count].reshape(count * 64, 640)
            term = dot(window, w1p[step], 1, 1)
            pre = term if pre is None else pre + term
        mask = gates[:, :, 0:64].reshape(count * 64, 64)
        act, slope = gate_slope(pre)
        if slopes is not None:
            slopes[...] = (slope * mask).reshape(count, 64, 64)
        act = (act * mask).astype(jnp.bfloat16).reshape(count, 4, 16, 64)
        for index in range(count):
            x = first_x + index
            for half in range(2):
                pair = jnp.concatenate([act[index, 2 * half], act[index, 2 * half + 1]], axis=1)
                lanes = (x % 2 * 2 + half) * 128
                children[pl.ds(child_row + x // 2 * 16, 16), lanes:lanes + 128] = pair

    def inner_planes(scene, carry):
        for column in range(2):
            brick = scene * 2 + column
            first = 1 - column
            fine(
                xs.at[brick], first, 7, mk[pl.ds(brick * 8 + first, 7)], child, brick * 64, first,
                slope1.at[brick, pl.ds(first, 7)],
            )
        return carry

    lax.fori_loop(0, 2, inner_planes, 0)

    for copy in halos:
        copy.wait_recv()

    def near_planes(unit, carry):
        side, scene = lax.div(unit, 2), lax.rem(unit, 2)
        occupied = near[side, scene, 320:336, 0:64].astype(jnp.float32)
        after = (side == 0).astype(jnp.float32)
        for x in range(5):
            row = occupied[x + 3:x + 4] * after + occupied[x:x + 1] * (1.0 - after)
            moved = dot(kept1_ref[...], diagonal(near[side, scene, x * 64:x * 64 + 64, :]), 1, 1)
            keep1(moved, near_xs.at[unit, x + side])
            near_gate = voxel_gate(row)
            mk[32 + unit * 5 + x] = near_gate
        for x in range(2):
            gate2[16 + unit * 2 + x] = coarse_gate(32 + unit * 5 + 1 - side + 2 * x)
        return carry

    lax.fori_loop(0, 4, near_planes, 0)
    for scene in range(2):
        from_left = near[0, scene, 320:336, :].astype(jnp.float32)[8:9]
        from_right = near[1, scene, 320:336, :].astype(jnp.float32)[8:9]
        to_left = shares(from_left, rows[scene][0], has_left)
        to_right = shares(from_right, rows[scene][1], has_right)
        share_of[scene, 0], share_of[scene, 3] = to_left, to_right
        share_of[scene, 4] = [to_left[0], to_left[2], to_left[1]]
        share_of[scene, 5] = [to_right[0], to_right[2], to_right[1]]
        last = diagonal(near[0, scene, 256:320, :])
        border1(last, share_of[scene, 0], xs.at[scene * 2, 0])
        first = diagonal(near[1, scene, 0:64, :])
        border1(first, share_of[scene, 3], xs.at[scene * 2 + 1, 9])
        border1(own_plane(scene * 2, 0), share_of[scene, 4], near_xs.at[scene, 5])
        border1(own_plane(scene * 2 + 1, 7), share_of[scene, 5], near_xs.at[2 + scene, 0])

    for scene in range(2):
        brick = scene * 2
        fine(xs.at[brick], 0, 1, mk[brick * 8:brick * 8 + 1], child, brick * 64, 0, slope1.at[brick, 0:1])
        brick = scene * 2 + 1
        fine(xs.at[brick], 7, 1, mk[brick * 8 + 7:brick * 8 + 8], child, brick * 64, 7, slope1.at[brick, 7:8])

    for unit in range(4):
        first = 32 + unit * 5 + (1 if unit < 2 else 0)
        fine(near_xs.at[unit], 0, 4, mk[first:first + 4], child, 256 + unit * 32, 0, None)

    gate = gate2[...].reshape(384, 128)
    down_pre = dot(child[...], wd_ref[...], 1, 1)
    act, slope = gate_slope(down_pre)
    slope2[...] = slope[0:256] * gate[0:256]
    act2[...] = (act * gate).astype(jnp.bfloat16).reshape(24, 16, 128)

    def lanes_of(tap, step):
        first = (step * 9 + tap) * 128
        return slice(first, first + 128)

    def inner2(values, into):
        for brick in range(4):
            moved = dot(kept2_ref[:, 0:64], values[brick * 4:brick * 4 + 4].reshape(64, 128), 1, 0).astype(jnp.bfloat16)
            base = brick * 64
            for tap in range(9):
                here = moved[tap * 64:tap * 64 + 64]
                into[base + 16:base + 64, lanes_of(tap, 0)] = here[0:48]
                into[base:base + 64, lanes_of(tap, 1)] = here
                into[base:base + 48, lanes_of(tap, 2)] = here[16:64]

    def border2(values, beside, into):
        planes = []
        for scene in range(2):
            planes += [beside[0][scene], values[scene * 8 + 4], values[scene * 8 + 3], beside[1][scene]]
        moved = dot(edge2[...], jnp.concatenate(planes, axis=0), 1, 0).astype(jnp.bfloat16)
        for tap in range(9):
            for brick in range(4):
                first = tap * 128 + brick * 32
                base = brick * 64
                into[base:base + 16, lanes_of(tap, 0)] = moved[first:first + 16]
                into[base + 48:base + 64, lanes_of(tap, 2)] = moved[first + 16:first + 32]

    def near2():
        outer = [act2[16 + 4 * side:20 + 4 * side].reshape(64, 128) for side in range(2)]
        moved = [dot(kept2_ref[:, 0:64], part, 1, 0).astype(jnp.bfloat16) for part in outer]
        planes = [act2[scene * 8 + plane] for scene in range(2) for plane in (0, 7)]
        edges = dot(edge3[:, 0:64], jnp.concatenate(planes, axis=0), 1, 0).astype(jnp.bfloat16)
        for tap in range(9):
            for scene in range(2):
                first = tap * 64 + scene * 32
                base = 256 + scene * 16
                im2[base:base + 16, lanes_of(tap, 0)] = moved[0][first:first + 16]
                im2[base:base + 16, lanes_of(tap, 1)] = moved[0][first + 16:first + 32]
                im2[base:base + 16, lanes_of(tap, 2)] = edges[first:first + 16]
                im2[base + 32:base + 48, lanes_of(tap, 0)] = edges[first + 16:first + 32]
                im2[base + 32:base + 48, lanes_of(tap, 1)] = moved[1][first:first + 16]
                im2[base + 32:base + 48, lanes_of(tap, 2)] = moved[1][first + 16:first + 32]

    def edges_of(roles, count):
        lane = lax.broadcasted_iota(jnp.int32, (1, 128), 1) // 16
        shared = [jnp.zeros((1, 128), jnp.float32) for _ in range(3)]
        for index, role in enumerate(roles):
            own = (lane == index).astype(jnp.float32)
            shared = [so_far + own * part for so_far, part in zip(shared, share_of[role])]
        shared = [part.astype(jnp.bfloat16) for part in shared]
        same = lax.broadcasted_iota(jnp.int32, (count, 16, 128), 0) == lax.broadcasted_iota(jnp.int32, (count, 16, 128), 2) // 16
        same = same.astype(jnp.float32).astype(jnp.bfloat16).reshape(1, count, 16, 128)
        moves = kept8_ref[...] * shared[0] + after8_ref[...] * shared[1] + before8_ref[...] * shared[2]
        return (moves.reshape(9, 1, 16, 128) * same).reshape(9 * count * 16, 128)

    edge2[...] = edges_of([(scene, role) for scene in range(2) for role in range(4)], 8)
    edge3[...] = edges_of([(scene, role) for scene in range(2) for role in (4, 5)], 4)
    inner2(act2, im2)
    border2(act2, ([act2[17], act2[19]], [act2[20], act2[22]]), im2)
    near2()
    coarse_pre = dot(im2[...], w2_ref[...], 1, 1)
    act, slope = gate_slope(coarse_pre)
    section_ref[...] = (act[0:256] * gate[0:256]).astype(jnp.bfloat16)
    upstream = [upstream_ref[...].reshape(256, 128), near[:, :, 336:352, :].reshape(64, 128)]
    gates = [gate[0:256], gate[272:288], gate[304:320], gate[320:336], gate[352:368]]
    upstream = jnp.concatenate(upstream, axis=0).astype(jnp.float32) * jnp.concatenate(gates, axis=0)
    grad2[...] = (upstream * slope).astype(jnp.bfloat16).reshape(20, 16, 128)

    def keep_parts(values, first, width, lane_tile):
        values = values.astype(jnp.bfloat16)
        for block in range(values.shape[0] // 16):
            for column in range(values.shape[1] // 128):
                parts[first + block * width + lane_tile + column] = values[block * 16:block * 16 + 16, column * 128:column * 128 + 128]

    grad_rows = grad2[0:16].reshape(256, 128)
    for step in range(3):
        keep_parts(dot(grad_rows, im2[0:256, step * 1152:step * 1152 + 1152], 0, 0), 0, 27, step * 9)
    for chain in chains[:2]:
        chain.start(0)
    inner2(grad2, img)
    border2(grad2, ([grad2[16], grad2[17]], [grad2[18], grad2[19]]), img)
    down_back = dot(img[...], w2f[...], 1, 0)
    down_in = (down_back * slope2[...]).astype(jnp.bfloat16)
    keep_parts(dot(down_in, child[0:256], 0, 0), DOWN_AT, 4, 0)
    parts[DOWN_AT + 32:CONV1_AT] = jnp.zeros((CONV1_AT - DOWN_AT - 32, 16, 128), jnp.bfloat16)
    chains[2].start(0)

    def advance(some, stage):
        for chain in some:
            chain.finish(stage - 1)
            if stage < len(STAGES["x"]):
                chain.start(stage)

    advance(chains[:2], 1)

    fine_back = dot(down_in, wd_ref[...], 1, 0)
    for brick in range(4):
        for x in range(8):
            base = brick * 64 + x // 2 * 16
            first = x % 2 * 256
            back = [fine_back[base:base + 16, first + part * 64:first + part * 64 + 64] for part in range(4)]
            grad1[brick, x] = (jnp.concatenate(back, axis=0) * slope1[brick, x]).astype(jnp.bfloat16)
    for step in range(3):
        term = None
        for brick in range(4):
            window = xs[brick, step:step + 8].reshape(512, 640)
            part = dot(grad1[brick].reshape(512, 64), window, 0, 0)
            term = part if term is None else term + part
        keep_parts(term, CONV1_AT, 15, step * 5)
    parts[CONV1_AT + 60:TILES] = jnp.zeros((TILES - CONV1_AT - 60, 16, 128), jnp.bfloat16)
    chains[-1].start(0)

    for stage in range(1, len(STAGES["x"]) + 1):
        if stage < len(STAGES["x"]):
            advance(chains[:2], stage + 1)
        advance(chains[2:], stage)
    for copy in halos:
        copy.wait_send()
    for chain in chains:
        chain.close()


def unpack_kernel(scale, section_ref, total_ref, section_out, conv1_ref, down_ref, conv2_ref):
    section_out[...] = section_ref[...]
    for block in range(8):
        rows = slice(block * 16, block * 16 + 16)
        for column in range(27):
            conv2_ref[rows, column * 128:column * 128 + 128] = total_ref[block * 27 + column].astype(jnp.float32) * scale
        for column in range(4):
            down_ref[rows, column * 128:column * 128 + 128] = total_ref[DOWN_AT + block * 4 + column].astype(jnp.float32) * scale
    for block in range(4):
        rows = slice(block * 16, block * 16 + 16)
        taps = []
        for step in range(3):
            whole = [total_ref[CONV1_AT + block * 15 + step * 5 + pair].astype(jnp.float32) * scale for pair in range(5)]
            taps += whole[:4] + [whole[4][:, 0:64]]
        conv1_ref[rows, :] = jnp.concatenate(taps, axis=1)


def per_device(tiles_in_row, scale, features, occupancy, brick_slots, conv1_weight, down_weight, conv2_weight, upstream):
    tables, table_at = selections()
    bf16, f32 = jnp.bfloat16, jnp.float32
    vmem, dma = pltpu.VMEM, pltpu.SemaphoreType.DMA
    scratch = [
        vmem((2, 2, 8, 64, 64), bf16), vmem((2, 2, 8, 64), jnp.int32), vmem(tables.shape, bf16), vmem((64, 1728), bf16),
        vmem((128, 512), bf16), vmem((128, 3456), bf16), vmem((2, 2, 4, 16, 128), bf16), dma((7,)),
        vmem((2, 2, 352, 128), bf16), vmem((2, 2, 352, 128), bf16), dma((2,)), dma((2,)),
        vmem((TILES, 16, 128), bf16), vmem((4, 10, 64, 640), bf16), vmem((4, 6, 64, 640), bf16), vmem((3, 64, 640), bf16),
        vmem((3456, 128), bf16), vmem((52, 64, 128), f32), vmem((4, 8, 64, 64), f32), vmem((384, 512), bf16),
        vmem((4, 8, 64, 64), bf16), vmem((24, 16, 128), f32), vmem((256, 128), f32), vmem((24, 16, 128), bf16),
        vmem((1152, 128), bf16), vmem((576, 128), bf16), vmem((320, 3456), bf16), vmem((256, 3456), bf16),
        vmem((20, 16, 128), bf16),
    ]
    for order, first, tiles in CHAINS:
        landing, held = Chain.sizes(order, tiles)
        scratch += [vmem(size + (16, 128), bf16) for size in landing]
        scratch += [vmem((size, 16, 128), bf16) for size in held]
    scratch += [dma((len(CHAINS), 7, 7))] * 2
    whole = pl.BlockSpec(memory_space=vmem)
    section, total = pl.pallas_call(
        functools.partial(section_kernel, tiles_in_row, table_at),
        out_shape=(jax.ShapeDtypeStruct((256, 128), bf16), jax.ShapeDtypeStruct((TILES, 16, 128), bf16)),
        in_specs=[pl.BlockSpec(memory_space=pltpu.SMEM)] + [pl.BlockSpec(memory_space=pltpu.HBM)] * 7,
        out_specs=(whole, whole),
        scratch_shapes=scratch,
        compiler_params=pltpu.CompilerParams(collective_id=0, has_side_effects=True, vmem_limit_bytes=63 * 2**20),
    )(
        brick_slots, features, occupancy, jnp.asarray(tables), conv1_weight, down_weight, conv2_weight, upstream,
    )
    section, conv1, down, conv2 = pl.pallas_call(
        functools.partial(unpack_kernel, scale),
        out_shape=(
            jax.ShapeDtypeStruct((256, 128), bf16), jax.ShapeDtypeStruct((64, 1728), f32),
            jax.ShapeDtypeStruct((128, 512), f32), jax.ShapeDtypeStruct((128, 3456), f32),
        ),
        in_specs=[whole] * 2,
        out_specs=(whole,) * 4,
        compiler_params=pltpu.CompilerParams(vmem_limit_bytes=63 * 2**20),
    )(section, total)
    return section.reshape(upstream.shape), conv1, down, conv2


def solution(mesh):
    tiles_in_row, scenes = mesh.shape["tile"], mesh.shape["dp"] * 2
    scale = 1.0 / (scenes * tiles_in_row * 2)
    wide = P("dp", "tile", None, None, None)
    return jax.shard_map(
        functools.partial(per_device, tiles_in_row, scale),
        mesh=mesh,
        in_specs=(wide, P("dp", "tile", None, None), P("dp", "tile"), P(), P(), P(), wide),
        out_specs=(wide, P(), P(), P()),
        check_vma=False,
    )
```

```python
import functools

import jax
import jax.numpy as jnp
import numpy as np
from jax import lax
from jax.experimental import pallas as pl
from jax.experimental.pallas import tpu as pltpu
from jax.sharding import PartitionSpec as P

FINE = 64
COARSE = 128
MESH = pl.DeviceIdType.MESH

AXES = {"c": 2, "x": 4, "y": 8, "z": 8}
STAGES = {
    "x": (("rs", "c"), ("rs", "x"), ("rs", "y"), ("ar", "z"), ("ag", "y"), ("ag", "x"), ("ag", "c")),
    "y": (("rs", "c"), ("rs", "y"), ("rs", "x"), ("ar", "z"), ("ag", "x"), ("ag", "y"), ("ag", "c")),
    "z": (("rs", "c"), ("rs", "z"), ("rs", "x"), ("ar", "y"), ("ag", "x"), ("ag", "z"), ("ag", "c")),
}


Y_LOW = 4


def place():
    dp, tile = lax.axis_index("dp"), lax.axis_index("tile")
    c, x, z = AXES["c"], AXES["x"], AXES["z"]
    return {
        "c": lax.rem(tile, c),
        "z": lax.rem(lax.div(tile, c), z),
        "x": lax.rem(lax.div(tile, c * z), x),
        "y": lax.div(tile, c * z * x) * Y_LOW + dp,
    }


def device(at):
    c, x, z = AXES["c"], AXES["x"], AXES["z"]
    tile = ((lax.div(at["y"], Y_LOW) * x + at["x"]) * z + at["z"]) * c + at["c"]
    return {"dp": lax.rem(at["y"], Y_LOW), "tile": tile}


def peer(at, axis, step):
    moved = dict(at)
    moved[axis] = lax.rem(at[axis] + step, AXES[axis])
    return device(moved)


def far_first(count):
    return sorted(range(1, count), key=lambda step: -min(step, count - step))


class Chain:
    def __init__(self, order, own, result, landing, held, send, recv, at, peers):
        self.stages, self.at, self.peers = STAGES[order], at, peers
        self.own, self.result, self.landing, self.held = own, result, landing, held
        self.send, self.recv = send, recv
        self.copies = {}

    @staticmethod
    def sizes(order, tiles):
        landing, held = [], []
        for kind, axis in STAGES[order]:
            if kind == "rs":
                tiles //= AXES[axis]
                landing.append((AXES[axis] - 1, tiles))
                held.append(tiles)
            elif kind == "ar":
                landing.append((AXES[axis], tiles))
        return landing, held

    def source(self, stage):
        return self.own if stage == 0 else self.held[stage - 1]

    def offset(self, stages):
        first = 0
        for stage in range(stages):
            first = first + self.at[self.stages[stage][1]] * self.held[stage].shape[0]
        return first

    def start(self, stage):
        kind, axis = self.stages[stage]
        count = AXES[axis]
        for step in far_first(count):
            if kind == "rs":
                part = self.held[stage].shape[0]
                to = lax.rem(self.at[axis] + step, count)
                src = self.source(stage).at[pl.ds(to * part, part)]
                dst = self.landing[stage].at[step - 1]
            elif kind == "ar":
                src = self.source(stage)
                dst = self.landing[stage].at[self.at[axis]]
            else:
                back = len(self.stages) - 1 - stage
                part = self.held[back].shape[0]
                where = pl.ds(self.offset(back + 1), part)
                src = dst = self.result.at[where]
            copy = pltpu.make_async_remote_copy(
                src_ref=src, dst_ref=dst,
                send_sem=self.send.at[stage, step - 1], recv_sem=self.recv.at[stage, step - 1],
                device_id=self.peers[axis, step], device_id_type=MESH,
            )
            copy.start()
            self.copies[stage, step] = copy

    def finish(self, stage):
        kind, axis = self.stages[stage]
        count = AXES[axis]
        for step in range(1, count):
            if kind == "ag":
                back = len(self.stages) - 1 - stage
                part = self.held[back].shape[0]
                origin = dict(self.at)
                origin[axis] = lax.rem(self.at[axis] + count - step, count)
                first = 0
                for earlier in range(back + 1):
                    first = first + origin[self.stages[earlier][1]] * self.held[earlier].shape[0]
                dst = self.result.at[pl.ds(first, part)]
            elif kind == "rs":
                dst = self.landing[stage].at[step - 1]
            else:
                dst = self.landing[stage].at[lax.rem(self.at[axis] + count - step, count)]
            pltpu.make_async_remote_copy(
                src_ref=dst, dst_ref=dst,
                send_sem=self.send.at[stage, step - 1], recv_sem=self.recv.at[stage, step - 1],
                device_id=self.peers[axis, step], device_id_type=MESH,
            ).wait_recv()
        if kind == "rs":
            part = self.held[stage].shape[0]
            mine = self.source(stage)[pl.ds(self.at[axis] * part, part)]
            if count == 2:
                self.held[stage][...] = mine + self.landing[stage][0]
                return
            total = mine.astype(jnp.float32)
            for step in range(1, count):
                total = total + self.landing[stage][step - 1].astype(jnp.float32)
            self.held[stage][...] = total.astype(jnp.bfloat16)
        elif kind == "ar":
            self.landing[stage][self.at[axis]] = self.source(stage)[...]
            total = self.landing[stage][0].astype(jnp.float32)
            for index in range(1, count):
                total = total + self.landing[stage][index].astype(jnp.float32)
            self.result[pl.ds(self.offset(stage), total.shape[0])] = total.astype(jnp.bfloat16)

    def close(self):
        for copy in self.copies.values():
            copy.wait_send()

DOWN_AT, CONV1_AT, TILES = 216, 256, 320
CHAINS = (("x", 0, 128), ("y", 128, 64), ("z", 192, 64), ("x", 256, 64))


def fine_selections():
    kept, after, before = np.zeros((3, 5, 64, 2, 64), np.float32)
    order = np.zeros((64, 64), np.float32)
    for y in range(8):
        for z in range(8):
            row = (y % 2) * 32 + (z % 2) * 16 + (y // 2) * 4 + z // 2
            order[row, y * 8 + z] = 1
            for tap in range(9):
                from_y, from_z = y + tap // 3 - 1, z + tap % 3 - 1
                if 0 <= from_z < 8:
                    into = kept if 0 <= from_y < 8 else after if from_y == 8 else before
                    into[tap // 2, row, tap % 2, (from_y % 8) * 8 + from_z] = 1
    return [table.reshape(320, 128) for table in (kept, after, before)] + [order]


def coarse_selections():
    kept, after, before = np.zeros((3, 9, 16, 16), np.float32)
    for y in range(4):
        for z in range(4):
            for tap in range(9):
                from_y, from_z = y + tap // 3 - 1, z + tap % 3 - 1
                if 0 <= from_z < 4:
                    into = kept if 0 <= from_y < 4 else after if from_y == 4 else before
                    into[tap, y * 4 + z, (from_y % 4) * 4 + from_z] = 1
    brick = np.einsum("tij,pq->tpiqj", kept, np.eye(4, dtype=np.float32)).reshape(576, 64)
    return [brick] + [np.tile(table.reshape(144, 16), (1, 8)) for table in (kept, after, before)]


def selections():
    tables = fine_selections() + coarse_selections()
    first = np.cumsum([0] + [table.shape[0] for table in tables])
    padded = [np.pad(table, ((0, 0), (0, 128 - table.shape[1]))) for table in tables]
    return np.concatenate(padded).astype(jnp.bfloat16), [int(place) for place in first]


def gate_slope(value):
    gate = jax.nn.sigmoid(value)
    return value * gate, gate * (1.0 + value * (1.0 - gate))


def dot(left, right, left_dim, right_dim):
    return lax.dot_general(left, right, (((left_dim,), (right_dim,)), ((), ())), preferred_element_type=jnp.float32)


def section_kernel(
    tiles_in_row, table_at,
    slots_ref, features_hbm, occupancy_hbm, tables_hbm, w1_hbm, wd_hbm, w2_hbm, upstream_hbm,
    section_ref, total_ref,
    features_ref, occupancy_ref, tables_ref, w1_ref, wd_ref, w2_ref, upstream_ref, load_sem,
    outgoing, near, halo_send, halo_recv,
    parts, xs, near_xs, w1p, w2f, mk, slope1, child, grad1, gate2, slope2, act2, edge2, edge3, im2, img, grad2,
    *scratch,
):
    loads = []
    operands = (
        (features_hbm, features_ref), (occupancy_hbm, occupancy_ref), (upstream_hbm, upstream_ref), (tables_hbm, tables_ref),
        (w1_hbm, w1_ref), (w2_hbm, w2_ref), (wd_hbm, wd_ref),
    )
    for index, (source, target) in enumerate(operands):
        loads.append(pltpu.make_async_copy(source, target, load_sem.at[index]))
        loads[-1].start()
    kept1_ref, after1_ref, before1_ref, order_ref, kept2_ref, kept8_ref, after8_ref, before8_ref = [
        tables_ref.at[first:last] for first, last in zip(table_at, table_at[1:])
    ]
    at = place()
    tile = lax.axis_index("tile")
    left, right = lax.rem(tile + tiles_in_row - 1, tiles_in_row), lax.rem(tile + 1, tiles_in_row)
    peers = {(axis, step): peer(at, axis, step) for axis, count in reversed(AXES.items()) for step in far_first(count)}
    scratch = list(scratch)
    send, recv = scratch.pop(), scratch.pop()
    chains = []
    for index, (order, first, tiles) in enumerate(CHAINS):
        landing = [scratch.pop(0) for _ in range(4)]
        held = [scratch.pop(0) for _ in range(3)]
        where = pl.ds(first, tiles)
        chains.append(Chain(order, parts.at[where], total_ref.at[where], landing, held, send.at[index], recv.at[index], at, peers))

    barrier = pltpu.get_barrier_semaphore()
    met = 0
    for other in (left, right):
        pl.semaphore_signal(barrier, inc=1, device_id={"tile": other}, device_id_type=MESH)
        met += 1
    for other in peers.values():
        pl.semaphore_signal(barrier, inc=1, device_id=other, device_id_type=MESH)
        met += 1

    def row_of(scene, column):
        return lax.rem(slots_ref[scene, column], 2).astype(jnp.float32)

    same_half = lax.broadcasted_iota(jnp.int32, (128, 128), 0) // 64 == lax.broadcasted_iota(jnp.int32, (128, 128), 1) // 64
    same_half = same_half.astype(jnp.float32).astype(jnp.bfloat16)

    def twice(plane, gate):
        plane = (plane.astype(jnp.float32) * gate).astype(jnp.bfloat16)
        return jnp.concatenate([plane, plane], axis=1)

    def diagonal(both):
        return jnp.concatenate([both, both], axis=0) * same_half

    def blocks(plane, gate):
        return diagonal(twice(plane, gate))

    def own_plane(brick, x):
        return blocks(features_ref[brick // 2, brick % 2, x], gate_row(occupancy_ref[brick // 2, brick % 2], x))

    def gate_row(occupied, x):
        return occupied[x:x + 1, :].astype(jnp.float32)

    loads[0].wait()
    loads[1].wait()
    loads[2].wait()
    for side in range(2):
        column, first_x, border = ((1, 3, 3), (0, 0, 0))[side]
        for scene in range(2):
            occupied = occupancy_ref[scene, column].astype(jnp.float32)
            for index in range(5):
                x = first_x + index
                both = twice(features_ref[scene, column, x], occupied[x:x + 1])
                outgoing[side, scene, index * 64:index * 64 + 64, :] = both
            row = jnp.full((8, 128), row_of(scene, column), jnp.float32)
            gates = jnp.concatenate([jnp.concatenate([occupied, occupied], axis=1), row], axis=0)
            outgoing[side, scene, 320:336, :] = gates.astype(jnp.bfloat16)
            outgoing[side, scene, 336:352, :] = upstream_ref[scene, column, border]
    pl.semaphore_wait(barrier, met)
    halos = []
    for side, other in enumerate((right, left)):
        copy = pltpu.make_async_remote_copy(
            src_ref=outgoing.at[side], dst_ref=near.at[side], send_sem=halo_send.at[side], recv_sem=halo_recv.at[side],
            device_id={"tile": other}, device_id_type=MESH,
        )
        copy.start()
        halos.append(copy)

    def keep1(moved, into):
        moved = moved.astype(jnp.bfloat16)
        for pair in range(5):
            into[:, pair * 128:pair * 128 + 128] = moved[pair * 64:pair * 64 + 64]

    def voxel_gate(row):
        return dot(order_ref[:, 0:64], jnp.broadcast_to(row, (128, 64)).astype(jnp.bfloat16), 1, 1)

    def coarse_gate(first):
        largest = None
        for a in range(2):
            for quarter in range(4):
                part = mk[first + a, quarter * 16:quarter * 16 + 16, :]
                largest = part if largest is None else jnp.maximum(largest, part)
        return largest

    for load in loads[3:]:
        load.wait()
    for step in range(3):
        taps = w1_ref[:, step * 576:step * 576 + 576]
        w1p[step] = jnp.concatenate([taps, jnp.zeros((64, 64), jnp.bfloat16)], axis=1)

    def local_planes(brick, carry):
        scene, column = lax.div(brick, 2), lax.rem(brick, 2)
        occupied = occupancy_ref[scene, column]
        for x in range(8):
            row = gate_row(occupied, x)
            keep1(dot(kept1_ref[...], blocks(features_ref[scene, column, x], row), 1, 1), xs.at[brick, x + 1])
            mk[brick * 8 + x] = voxel_gate(row)
        for x in range(4):
            gate2[brick * 4 + x] = coarse_gate(brick * 8 + 2 * x)
        return carry

    lax.fori_loop(0, 4, local_planes, 0)
    for tap in range(27):
        w2f[tap * 128:tap * 128 + 128, :] = w2_ref[:, (26 - tap) * 128:(26 - tap) * 128 + 128]

    def shares(from_row, to_row, valid):
        apart = from_row - to_row
        return [share * valid for share in (1.0 - apart * apart, 0.5 * apart * (apart + 1.0), 0.5 * apart * (apart - 1.0))]

    rows = [[jnp.full((1, 128), row_of(scene, column), jnp.float32) for column in range(2)] for scene in range(2)]
    has_left = (tile > 0).astype(jnp.float32)
    has_right = (tile < tiles_in_row - 1).astype(jnp.float32)

    def border1(plane, share, into):
        share = [part.astype(jnp.bfloat16) for part in share]
        moves = kept1_ref[...] * share[0] + after1_ref[...] * share[1] + before1_ref[...] * share[2]
        keep1(dot(moves, plane, 1, 1), into)

    share_of = {}
    for scene in range(2):
        share_of[scene, 1] = shares(rows[scene][1], rows[scene][0], 1.0)
        share_of[scene, 2] = shares(rows[scene][0], rows[scene][1], 1.0)
        border1(own_plane(scene * 2 + 1, 0), share_of[scene, 1], xs.at[scene * 2, 9])
        border1(own_plane(scene * 2, 7), share_of[scene, 2], xs.at[scene * 2 + 1, 0])

    def fine(source, first, count, gates, children, child_row, first_x, slopes):
        size = count * 64
        wide = dot(source[first:first + count + 2].reshape(size + 128, 640), w1p[...].reshape(192, 640), 1, 1)
        pre = wide[0:size, 0:64] + wide[64:size + 64, 64:128] + wide[128:size + 128, 128:192]
        mask = gates[:, :, 0:64].reshape(count * 64, 64)
        act, slope = gate_slope(pre)
        if slopes is not None:
            slopes[...] = (slope * mask).reshape(count, 64, 64)
        act = (act * mask).astype(jnp.bfloat16).reshape(count, 4, 16, 64)
        for index in range(count):
            x = first_x + index
            for half in range(2):
                pair = jnp.concatenate([act[index, 2 * half], act[index, 2 * half + 1]], axis=1)
                lanes = (x % 2 * 2 + half) * 128
                children[pl.ds(child_row + x // 2 * 16, 16), lanes:lanes + 128] = pair

    def inner_planes(scene, carry):
        for column in range(2):
            brick = scene * 2 + column
            first = 1 - column
            fine(
                xs.at[brick], first, 7, mk[pl.ds(brick * 8 + first, 7)], child, brick * 64, first,
                slope1.at[brick, pl.ds(first, 7)],
            )
        return carry

    lax.fori_loop(0, 2, inner_planes, 0)

    for copy in halos:
        copy.wait_recv()

    def near_planes(unit, carry):
        side, scene = lax.div(unit, 2), lax.rem(unit, 2)
        occupied = near[side, scene, 320:336, 0:64].astype(jnp.float32)
        after = (side == 0).astype(jnp.float32)
        for x in range(5):
            row = occupied[x + 3:x + 4] * after + occupied[x:x + 1] * (1.0 - after)
            moved = dot(kept1_ref[...], diagonal(near[side, scene, x * 64:x * 64 + 64, :]), 1, 1)
            keep1(moved, near_xs.at[unit, x + side])
            near_gate = voxel_gate(row)
            mk[32 + unit * 5 + x] = near_gate
        for x in range(2):
            gate2[16 + unit * 2 + x] = coarse_gate(32 + unit * 5 + 1 - side + 2 * x)
        return carry

    lax.fori_loop(0, 4, near_planes, 0)
    for scene in range(2):
        from_left = near[0, scene, 320:336, :].astype(jnp.float32)[8:9]
        from_right = near[1, scene, 320:336, :].astype(jnp.float32)[8:9]
        to_left = shares(from_left, rows[scene][0], has_left)
        to_right = shares(from_right, rows[scene][1], has_right)
        share_of[scene, 0], share_of[scene, 3] = to_left, to_right
        share_of[scene, 4] = [to_left[0], to_left[2], to_left[1]]
        share_of[scene, 5] = [to_right[0], to_right[2], to_right[1]]
        last = diagonal(near[0, scene, 256:320, :])
        border1(last, share_of[scene, 0], xs.at[scene * 2, 0])
        first = diagonal(near[1, scene, 0:64, :])
        border1(first, share_of[scene, 3], xs.at[scene * 2 + 1, 9])
        border1(own_plane(scene * 2, 0), share_of[scene, 4], near_xs.at[scene, 5])
        border1(own_plane(scene * 2 + 1, 7), share_of[scene, 5], near_xs.at[2 + scene, 0])

    for scene in range(2):
        brick = scene * 2
        fine(xs.at[brick], 0, 1, mk[brick * 8:brick * 8 + 1], child, brick * 64, 0, slope1.at[brick, 0:1])
        brick = scene * 2 + 1
        fine(xs.at[brick], 7, 1, mk[brick * 8 + 7:brick * 8 + 8], child, brick * 64, 7, slope1.at[brick, 7:8])

    for unit in range(4):
        first = 32 + unit * 5 + (1 if unit < 2 else 0)
        fine(near_xs.at[unit], 0, 4, mk[first:first + 4], child, 256 + unit * 32, 0, None)

    gate = gate2[...].reshape(384, 128)
    down_pre = dot(child[...], wd_ref[...], 1, 1)
    act, slope = gate_slope(down_pre)
    slope2[...] = slope[0:256] * gate[0:256]
    act2[...] = (act * gate).astype(jnp.bfloat16).reshape(24, 16, 128)

    def lanes_of(tap, step):
        first = (step * 9 + tap) * 128
        return slice(first, first + 128)

    def inner2(values, into):
        for brick in range(4):
            moved = dot(kept2_ref[:, 0:64], values[brick * 4:brick * 4 + 4].reshape(64, 128), 1, 0).astype(jnp.bfloat16)
            base = brick * 64
            for tap in range(9):
                here = moved[tap * 64:tap * 64 + 64]
                into[base + 16:base + 64, lanes_of(tap, 0)] = here[0:48]
                into[base:base + 64, lanes_of(tap, 1)] = here
                into[base:base + 48, lanes_of(tap, 2)] = here[16:64]

    def border2(values, beside, into):
        planes = []
        for scene in range(2):
            planes += [beside[0][scene], values[scene * 8 + 4], values[scene * 8 + 3], beside[1][scene]]
        moved = dot(edge2[...], jnp.concatenate(planes, axis=0), 1, 0).astype(jnp.bfloat16)
        for tap in range(9):
            for brick in range(4):
                first = tap * 128 + brick * 32
                base = brick * 64
                into[base:base + 16, lanes_of(tap, 0)] = moved[first:first + 16]
                into[base + 48:base + 64, lanes_of(tap, 2)] = moved[first + 16:first + 32]

    def near2():
        outer = [act2[16 + 4 * side:20 + 4 * side].reshape(64, 128) for side in range(2)]
        moved = [dot(kept2_ref[:, 0:64], part, 1, 0).astype(jnp.bfloat16) for part in outer]
        planes = [act2[scene * 8 + plane] for scene in range(2) for plane in (0, 7)]
        edges = dot(edge3[:, 0:64], jnp.concatenate(planes, axis=0), 1, 0).astype(jnp.bfloat16)
        for tap in range(9):
            for scene in range(2):
                first = tap * 64 + scene * 32
                base = 256 + scene * 16
                im2[base:base + 16, lanes_of(tap, 0)] = moved[0][first:first + 16]
                im2[base:base + 16, lanes_of(tap, 1)] = moved[0][first + 16:first + 32]
                im2[base:base + 16, lanes_of(tap, 2)] = edges[first:first + 16]
                im2[base + 32:base + 48, lanes_of(tap, 0)] = edges[first + 16:first + 32]
                im2[base + 32:base + 48, lanes_of(tap, 1)] = moved[1][first:first + 16]
                im2[base + 32:base + 48, lanes_of(tap, 2)] = moved[1][first + 16:first + 32]

    def edges_of(roles, count):
        lane = lax.broadcasted_iota(jnp.int32, (1, 128), 1) // 16
        shared = [jnp.zeros((1, 128), jnp.float32) for _ in range(3)]
        for index, role in enumerate(roles):
            own = (lane == index).astype(jnp.float32)
            shared = [so_far + own * part for so_far, part in zip(shared, share_of[role])]
        shared = [part.astype(jnp.bfloat16) for part in shared]
        same = lax.broadcasted_iota(jnp.int32, (count, 16, 128), 0) == lax.broadcasted_iota(jnp.int32, (count, 16, 128), 2) // 16
        same = same.astype(jnp.float32).astype(jnp.bfloat16).reshape(1, count, 16, 128)
        moves = kept8_ref[...] * shared[0] + after8_ref[...] * shared[1] + before8_ref[...] * shared[2]
        return (moves.reshape(9, 1, 16, 128) * same).reshape(9 * count * 16, 128)

    edge2[...] = edges_of([(scene, role) for scene in range(2) for role in range(4)], 8)
    edge3[...] = edges_of([(scene, role) for scene in range(2) for role in (4, 5)], 4)
    inner2(act2, im2)
    border2(act2, ([act2[17], act2[19]], [act2[20], act2[22]]), im2)
    near2()
    coarse_pre = dot(im2[...], w2_ref[...], 1, 1)
    act, slope = gate_slope(coarse_pre)
    section_ref[...] = (act[0:256] * gate[0:256]).astype(jnp.bfloat16)
    upstream = [upstream_ref[...].reshape(256, 128), near[:, :, 336:352, :].reshape(64, 128)]
    gates = [gate[0:256], gate[272:288], gate[304:320], gate[320:336], gate[352:368]]
    upstream = jnp.concatenate(upstream, axis=0).astype(jnp.float32) * jnp.concatenate(gates, axis=0)
    grad2[...] = (upstream * slope).astype(jnp.bfloat16).reshape(20, 16, 128)

    def keep_parts(values, first, width, lane_tile):
        values = values.astype(jnp.bfloat16)
        for block in range(values.shape[0] // 16):
            for column in range(values.shape[1] // 128):
                parts[first + block * width + lane_tile + column] = values[block * 16:block * 16 + 16, column * 128:column * 128 + 128]

    grad_rows = grad2[0:16].reshape(256, 128)
    for step in range(3):
        keep_parts(dot(grad_rows, im2[0:256, step * 1152:step * 1152 + 1152], 0, 0), 0, 27, step * 9)
    for chain in chains[:2]:
        chain.start(0)
    inner2(grad2, img)
    border2(grad2, ([grad2[16], grad2[17]], [grad2[18], grad2[19]]), img)
    down_back = dot(img[...], w2f[...], 1, 0)
    down_in = (down_back * slope2[...]).astype(jnp.bfloat16)
    keep_parts(dot(down_in, child[0:256], 0, 0), DOWN_AT, 4, 0)
    parts[DOWN_AT + 32:CONV1_AT] = jnp.zeros((CONV1_AT - DOWN_AT - 32, 16, 128), jnp.bfloat16)
    chains[2].start(0)

    def advance(some, stage):
        for chain in some:
            chain.finish(stage - 1)
            if stage < len(STAGES["x"]):
                chain.start(stage)

    advance(chains[:2], 1)

    fine_back = dot(down_in, wd_ref[...], 1, 0)
    for brick in range(4):
        for x in range(8):
            base = brick * 64 + x // 2 * 16
            first = x % 2 * 256
            back = [fine_back[base:base + 16, first + part * 64:first + part * 64 + 64] for part in range(4)]
            grad1[brick, x] = (jnp.concatenate(back, axis=0) * slope1[brick, x]).astype(jnp.bfloat16)
    for step in range(3):
        term = None
        for brick in range(4):
            window = xs[brick, step:step + 8].reshape(512, 640)
            part = dot(grad1[brick].reshape(512, 64), window, 0, 0)
            term = part if term is None else term + part
        keep_parts(term, CONV1_AT, 15, step * 5)
    parts[CONV1_AT + 60:TILES] = jnp.zeros((TILES - CONV1_AT - 60, 16, 128), jnp.bfloat16)
    chains[-1].start(0)

    for stage in range(1, len(STAGES["x"]) + 1):
        if stage < len(STAGES["x"]):
            advance(chains[:2], stage + 1)
        advance(chains[2:], stage)
    for copy in halos:
        copy.wait_send()
    for chain in chains:
        chain.close()


def unpack_kernel(scale, section_ref, total_ref, section_out, conv1_ref, down_ref, conv2_ref):
    section_out[...] = section_ref[...]
    for block in range(8):
        rows = slice(block * 16, block * 16 + 16)
        for column in range(27):
            conv2_ref[rows, column * 128:column * 128 + 128] = total_ref[block * 27 + column].astype(jnp.float32) * scale
        for column in range(4):
            down_ref[rows, column * 128:column * 128 + 128] = total_ref[DOWN_AT + block * 4 + column].astype(jnp.float32) * scale
    for block in range(4):
        rows = slice(block * 16, block * 16 + 16)
        taps = []
        for step in range(3):
            whole = [total_ref[CONV1_AT + block * 15 + step * 5 + pair].astype(jnp.float32) * scale for pair in range(5)]
            taps += whole[:4] + [whole[4][:, 0:64]]
        conv1_ref[rows, :] = jnp.concatenate(taps, axis=1)


def per_device(tiles_in_row, scale, features, occupancy, brick_slots, conv1_weight, down_weight, conv2_weight, upstream):
    tables, table_at = selections()
    bf16, f32 = jnp.bfloat16, jnp.float32
    vmem, dma = pltpu.VMEM, pltpu.SemaphoreType.DMA
    scratch = [
        vmem((2, 2, 8, 64, 64), bf16), vmem((2, 2, 8, 64), jnp.int32), vmem(tables.shape, bf16), vmem((64, 1728), bf16),
        vmem((128, 512), bf16), vmem((128, 3456), bf16), vmem((2, 2, 4, 16, 128), bf16), dma((7,)),
        vmem((2, 2, 352, 128), bf16), vmem((2, 2, 352, 128), bf16), dma((2,)), dma((2,)),
        vmem((TILES, 16, 128), bf16), vmem((4, 10, 64, 640), bf16), vmem((4, 6, 64, 640), bf16), vmem((3, 64, 640), bf16),
        vmem((3456, 128), bf16), vmem((52, 64, 128), f32), vmem((4, 8, 64, 64), f32), vmem((384, 512), bf16),
        vmem((4, 8, 64, 64), bf16), vmem((24, 16, 128), f32), vmem((256, 128), f32), vmem((24, 16, 128), bf16),
        vmem((1152, 128), bf16), vmem((576, 128), bf16), vmem((320, 3456), bf16), vmem((256, 3456), bf16),
        vmem((20, 16, 128), bf16),
    ]
    for order, first, tiles in CHAINS:
        landing, held = Chain.sizes(order, tiles)
        scratch += [vmem(size + (16, 128), bf16) for size in landing]
        scratch += [vmem((size, 16, 128), bf16) for size in held]
    scratch += [dma((len(CHAINS), 7, 7))] * 2
    whole = pl.BlockSpec(memory_space=vmem)
    section, total = pl.pallas_call(
        functools.partial(section_kernel, tiles_in_row, table_at),
        out_shape=(jax.ShapeDtypeStruct((256, 128), bf16), jax.ShapeDtypeStruct((TILES, 16, 128), bf16)),
        in_specs=[pl.BlockSpec(memory_space=pltpu.SMEM)] + [pl.BlockSpec(memory_space=pltpu.HBM)] * 7,
        out_specs=(whole, whole),
        scratch_shapes=scratch,
        compiler_params=pltpu.CompilerParams(collective_id=0, has_side_effects=True, vmem_limit_bytes=63 * 2**20),
    )(
        brick_slots, features, occupancy, jnp.asarray(tables), conv1_weight, down_weight, conv2_weight, upstream,
    )
    section, conv1, down, conv2 = pl.pallas_call(
        functools.partial(unpack_kernel, scale),
        out_shape=(
            jax.ShapeDtypeStruct((256, 128), bf16), jax.ShapeDtypeStruct((64, 1728), f32),
            jax.ShapeDtypeStruct((128, 512), f32), jax.ShapeDtypeStruct((128, 3456), f32),
        ),
        in_specs=[whole] * 2,
        out_specs=(whole,) * 4,
        compiler_params=pltpu.CompilerParams(vmem_limit_bytes=63 * 2**20),
    )(section, total)
    return section.reshape(upstream.shape), conv1, down, conv2


def solution(mesh):
    tiles_in_row, scenes = mesh.shape["tile"], mesh.shape["dp"] * 2
    scale = 1.0 / (scenes * tiles_in_row * 2)
    wide = P("dp", "tile", None, None, None)
    return jax.shard_map(
        functools.partial(per_device, tiles_in_row, scale),
        mesh=mesh,
        in_specs=(wide, P("dp", "tile", None, None), P("dp", "tile"), P(), P(), P(), wide),
        out_specs=(wide, P(), P(), P()),
        check_vma=False,
    )
```

```python
import functools

import jax
import jax.numpy as jnp
import numpy as np
from jax import lax
from jax.experimental import pallas as pl
from jax.experimental.pallas import tpu as pltpu
from jax.sharding import PartitionSpec as P

FINE = 64
COARSE = 128
MESH = pl.DeviceIdType.MESH

AXES = {"c": 2, "x": 4, "y": 8, "z": 8}
STAGES = {
    "x": (("rs", "c"), ("rs", "x"), ("rs", "y"), ("ar", "z"), ("ag", "y"), ("ag", "x"), ("ag", "c")),
    "y": (("rs", "c"), ("rs", "y"), ("rs", "x"), ("ar", "z"), ("ag", "x"), ("ag", "y"), ("ag", "c")),
    "z": (("rs", "c"), ("rs", "z"), ("rs", "x"), ("ar", "y"), ("ag", "x"), ("ag", "z"), ("ag", "c")),
}


Y_LOW = 4


def place():
    dp, tile = lax.axis_index("dp"), lax.axis_index("tile")
    c, x, z = AXES["c"], AXES["x"], AXES["z"]
    return {
        "c": lax.rem(tile, c),
        "z": lax.rem(lax.div(tile, c), z),
        "x": lax.rem(lax.div(tile, c * z), x),
        "y": lax.div(tile, c * z * x) * Y_LOW + dp,
    }


def device(at):
    c, x, z = AXES["c"], AXES["x"], AXES["z"]
    tile = ((lax.div(at["y"], Y_LOW) * x + at["x"]) * z + at["z"]) * c + at["c"]
    return {"dp": lax.rem(at["y"], Y_LOW), "tile": tile}


def peer(at, axis, step):
    moved = dict(at)
    moved[axis] = lax.rem(at[axis] + step, AXES[axis])
    return device(moved)


def far_first(count):
    return sorted(range(1, count), key=lambda step: -min(step, count - step))


class Chain:
    def __init__(self, order, own, result, landing, held, send, recv, at, peers):
        self.stages, self.at, self.peers = STAGES[order], at, peers
        self.own, self.result, self.landing, self.held = own, result, landing, held
        self.send, self.recv = send, recv
        self.copies = {}

    @staticmethod
    def sizes(order, tiles):
        landing, held = [], []
        for kind, axis in STAGES[order]:
            if kind == "rs":
                tiles //= AXES[axis]
                landing.append((AXES[axis] - 1, tiles))
                held.append(tiles)
            elif kind == "ar":
                landing.append((AXES[axis], tiles))
        return landing, held

    def source(self, stage):
        return self.own if stage == 0 else self.held[stage - 1]

    def offset(self, stages):
        first = 0
        for stage in range(stages):
            first = first + self.at[self.stages[stage][1]] * self.held[stage].shape[0]
        return first

    def start(self, stage):
        kind, axis = self.stages[stage]
        count = AXES[axis]
        for step in far_first(count):
            if kind == "rs":
                part = self.held[stage].shape[0]
                to = lax.rem(self.at[axis] + step, count)
                src = self.source(stage).at[pl.ds(to * part, part)]
                dst = self.landing[stage].at[step - 1]
            elif kind == "ar":
                src = self.source(stage)
                dst = self.landing[stage].at[self.at[axis]]
            else:
                back = len(self.stages) - 1 - stage
                part = self.held[back].shape[0]
                where = pl.ds(self.offset(back + 1), part)
                src = dst = self.result.at[where]
            copy = pltpu.make_async_remote_copy(
                src_ref=src, dst_ref=dst,
                send_sem=self.send.at[stage, step - 1], recv_sem=self.recv.at[stage, step - 1],
                device_id=self.peers[axis, step], device_id_type=MESH,
            )
            copy.start()
            self.copies[stage, step] = copy

    def finish(self, stage):
        kind, axis = self.stages[stage]
        count = AXES[axis]
        for step in range(1, count):
            if kind == "ag":
                back = len(self.stages) - 1 - stage
                part = self.held[back].shape[0]
                origin = dict(self.at)
                origin[axis] = lax.rem(self.at[axis] + count - step, count)
                first = 0
                for earlier in range(back + 1):
                    first = first + origin[self.stages[earlier][1]] * self.held[earlier].shape[0]
                dst = self.result.at[pl.ds(first, part)]
            elif kind == "rs":
                dst = self.landing[stage].at[step - 1]
            else:
                dst = self.landing[stage].at[lax.rem(self.at[axis] + count - step, count)]
            pltpu.make_async_remote_copy(
                src_ref=dst, dst_ref=dst,
                send_sem=self.send.at[stage, step - 1], recv_sem=self.recv.at[stage, step - 1],
                device_id=self.peers[axis, step], device_id_type=MESH,
            ).wait_recv()
        if kind == "rs":
            part = self.held[stage].shape[0]
            mine = self.source(stage)[pl.ds(self.at[axis] * part, part)]
            if count == 2:
                self.held[stage][...] = mine + self.landing[stage][0]
                return
            total = mine.astype(jnp.float32)
            for step in range(1, count):
                total = total + self.landing[stage][step - 1].astype(jnp.float32)
            self.held[stage][...] = total.astype(jnp.bfloat16)
        elif kind == "ar":
            self.landing[stage][self.at[axis]] = self.source(stage)[...]
            total = self.landing[stage][0].astype(jnp.float32)
            for index in range(1, count):
                total = total + self.landing[stage][index].astype(jnp.float32)
            self.result[pl.ds(self.offset(stage), total.shape[0])] = total.astype(jnp.bfloat16)

    def close(self):
        for copy in self.copies.values():
            copy.wait_send()

DOWN_AT, CONV1_AT, TILES = 216, 256, 320
CHAINS = (("x", 0, 128), ("y", 128, 64), ("z", 192, 64), ("x", 256, 64))
ARRIVALS = (2, 3, 0, 1, 3, 2, 1, 0, 2, 3, 1, 0, 2, 3, 1, 2, 0, 3, 1, 0, 1, 2, 3, 0, 2, 3)


def fine_selections():
    kept, after, before = np.zeros((3, 5, 64, 2, 64), np.float32)
    order = np.zeros((64, 64), np.float32)
    for y in range(8):
        for z in range(8):
            row = (y % 2) * 32 + (z % 2) * 16 + (y // 2) * 4 + z // 2
            order[row, y * 8 + z] = 1
            for tap in range(9):
                from_y, from_z = y + tap // 3 - 1, z + tap % 3 - 1
                if 0 <= from_z < 8:
                    into = kept if 0 <= from_y < 8 else after if from_y == 8 else before
                    into[tap // 2, row, tap % 2, (from_y % 8) * 8 + from_z] = 1
    return [table.reshape(320, 128) for table in (kept, after, before)] + [order]


def coarse_selections():
    kept, after, before = np.zeros((3, 9, 16, 16), np.float32)
    for y in range(4):
        for z in range(4):
            for tap in range(9):
                from_y, from_z = y + tap // 3 - 1, z + tap % 3 - 1
                if 0 <= from_z < 4:
                    into = kept if 0 <= from_y < 4 else after if from_y == 4 else before
                    into[tap, y * 4 + z, (from_y % 4) * 4 + from_z] = 1
    brick = np.einsum("tij,pq->tpiqj", kept, np.eye(4, dtype=np.float32)).reshape(576, 64)
    return [brick] + [np.tile(table.reshape(144, 16), (1, 8)) for table in (kept, after, before)]


def selections():
    tables = fine_selections() + coarse_selections()
    first = np.cumsum([0] + [table.shape[0] for table in tables])
    padded = [np.pad(table, ((0, 0), (0, 128 - table.shape[1]))) for table in tables]
    return np.concatenate(padded).astype(jnp.bfloat16), [int(place) for place in first]


def gate_slope(value):
    gate = jax.nn.sigmoid(value)
    return value * gate, gate * (1.0 + value * (1.0 - gate))


def dot(left, right, left_dim, right_dim):
    return lax.dot_general(left, right, (((left_dim,), (right_dim,)), ((), ())), preferred_element_type=jnp.float32)


def section_kernel(
    tiles_in_row, table_at,
    slots_ref, features_hbm, occupancy_hbm, tables_hbm, w1_hbm, wd_hbm, w2_hbm, upstream_hbm,
    section_ref, total_ref,
    features_ref, occupancy_ref, tables_ref, w1_ref, wd_ref, w2_ref, upstream_ref, load_sem,
    outgoing, near, halo_send, halo_recv,
    parts, xs, near_xs, w1p, w2f, mk, slope1, child, grad1, gate2, slope2, act2, edge2, edge3, im2, img, grad2,
    *scratch,
):
    loads = []
    operands = (
        (features_hbm, features_ref), (occupancy_hbm, occupancy_ref), (upstream_hbm, upstream_ref), (tables_hbm, tables_ref),
        (w1_hbm, w1_ref), (w2_hbm, w2_ref), (wd_hbm, wd_ref),
    )
    for index, (source, target) in enumerate(operands):
        loads.append(pltpu.make_async_copy(source, target, load_sem.at[index]))
        loads[-1].start()
    kept1_ref, after1_ref, before1_ref, order_ref, kept2_ref, kept8_ref, after8_ref, before8_ref = [
        tables_ref.at[first:last] for first, last in zip(table_at, table_at[1:])
    ]
    at = place()
    tile = lax.axis_index("tile")
    left, right = lax.rem(tile + tiles_in_row - 1, tiles_in_row), lax.rem(tile + 1, tiles_in_row)
    peers = {(axis, step): peer(at, axis, step) for axis, count in reversed(AXES.items()) for step in far_first(count)}
    scratch = list(scratch)
    send, recv = scratch.pop(), scratch.pop()
    chains = []
    for index, (order, first, tiles) in enumerate(CHAINS):
        landing = [scratch.pop(0) for _ in range(4)]
        held = [scratch.pop(0) for _ in range(3)]
        where = pl.ds(first, tiles)
        chains.append(Chain(order, parts.at[where], total_ref.at[where], landing, held, send.at[index], recv.at[index], at, peers))

    barrier = pltpu.get_barrier_semaphore()
    met = 0
    for other in (left, right):
        pl.semaphore_signal(barrier, inc=1, device_id={"tile": other}, device_id_type=MESH)
        met += 1
    for other in peers.values():
        pl.semaphore_signal(barrier, inc=1, device_id=other, device_id_type=MESH)
        met += 1

    def row_of(scene, column):
        return lax.rem(slots_ref[scene, column], 2).astype(jnp.float32)

    same_half = lax.broadcasted_iota(jnp.int32, (128, 128), 0) // 64 == lax.broadcasted_iota(jnp.int32, (128, 128), 1) // 64
    same_half = same_half.astype(jnp.float32).astype(jnp.bfloat16)

    def twice(plane, gate):
        plane = (plane.astype(jnp.float32) * gate).astype(jnp.bfloat16)
        return jnp.concatenate([plane, plane], axis=1)

    def diagonal(both):
        return jnp.concatenate([both, both], axis=0) * same_half

    def blocks(plane, gate):
        return diagonal(twice(plane, gate))

    def own_plane(brick, x):
        return blocks(features_ref[brick // 2, brick % 2, x], gate_row(occupancy_ref[brick // 2, brick % 2], x))

    def gate_row(occupied, x):
        return occupied[x:x + 1, :].astype(jnp.float32)

    loads[0].wait()
    loads[1].wait()
    loads[2].wait()
    for side in range(2):
        column, first_x, border = ((1, 3, 3), (0, 0, 0))[side]
        for scene in range(2):
            occupied = occupancy_ref[scene, column].astype(jnp.float32)
            for index in range(5):
                x = first_x + index
                both = twice(features_ref[scene, column, x], occupied[x:x + 1])
                outgoing[side, scene, index * 64:index * 64 + 64, :] = both
            row = jnp.full((8, 128), row_of(scene, column), jnp.float32)
            gates = jnp.concatenate([jnp.concatenate([occupied, occupied], axis=1), row], axis=0)
            outgoing[side, scene, 320:336, :] = gates.astype(jnp.bfloat16)
            outgoing[side, scene, 336:352, :] = upstream_ref[scene, column, border]
    pl.semaphore_wait(barrier, met)
    halos = []
    for side, other in enumerate((right, left)):
        copy = pltpu.make_async_remote_copy(
            src_ref=outgoing.at[side], dst_ref=near.at[side], send_sem=halo_send.at[side], recv_sem=halo_recv.at[side],
            device_id={"tile": other}, device_id_type=MESH,
        )
        copy.start()
        halos.append(copy)

    def keep1(moved, into):
        moved = moved.astype(jnp.bfloat16)
        for pair in range(5):
            into[:, pair * 128:pair * 128 + 128] = moved[pair * 64:pair * 64 + 64]

    def voxel_gate(row):
        return dot(order_ref[:, 0:64], jnp.broadcast_to(row, (128, 64)).astype(jnp.bfloat16), 1, 1)

    def coarse_gate(first):
        largest = None
        for a in range(2):
            for quarter in range(4):
                part = mk[first + a, quarter * 16:quarter * 16 + 16, :]
                largest = part if largest is None else jnp.maximum(largest, part)
        return largest

    for load in loads[3:]:
        load.wait()
    for step in range(3):
        taps = w1_ref[:, step * 576:step * 576 + 576]
        w1p[step] = jnp.concatenate([taps, jnp.zeros((64, 64), jnp.bfloat16)], axis=1)

    def local_planes(brick, carry):
        scene, column = lax.div(brick, 2), lax.rem(brick, 2)
        occupied = occupancy_ref[scene, column]
        for x in range(8):
            row = gate_row(occupied, x)
            keep1(dot(kept1_ref[...], blocks(features_ref[scene, column, x], row), 1, 1), xs.at[brick, x + 1])
            mk[brick * 8 + x] = voxel_gate(row)
        for x in range(4):
            gate2[brick * 4 + x] = coarse_gate(brick * 8 + 2 * x)
        return carry

    lax.fori_loop(0, 4, local_planes, 0)
    for tap in range(27):
        w2f[tap * 128:tap * 128 + 128, :] = w2_ref[:, (26 - tap) * 128:(26 - tap) * 128 + 128]

    def shares(from_row, to_row, valid):
        apart = from_row - to_row
        return [share * valid for share in (1.0 - apart * apart, 0.5 * apart * (apart + 1.0), 0.5 * apart * (apart - 1.0))]

    rows = [[jnp.full((1, 128), row_of(scene, column), jnp.float32) for column in range(2)] for scene in range(2)]
    has_left = (tile > 0).astype(jnp.float32)
    has_right = (tile < tiles_in_row - 1).astype(jnp.float32)

    def border1(plane, share, into):
        share = [part.astype(jnp.bfloat16) for part in share]
        moves = kept1_ref[...] * share[0] + after1_ref[...] * share[1] + before1_ref[...] * share[2]
        keep1(dot(moves, plane, 1, 1), into)

    share_of = {}
    for scene in range(2):
        share_of[scene, 1] = shares(rows[scene][1], rows[scene][0], 1.0)
        share_of[scene, 2] = shares(rows[scene][0], rows[scene][1], 1.0)
        border1(own_plane(scene * 2 + 1, 0), share_of[scene, 1], xs.at[scene * 2, 9])
        border1(own_plane(scene * 2, 7), share_of[scene, 2], xs.at[scene * 2 + 1, 0])

    def fine(source, first, count, gates, children, child_row, first_x, slopes):
        size = count * 64
        wide = dot(source[first:first + count + 2].reshape(size + 128, 640), w1p[...].reshape(192, 640), 1, 1)
        pre = wide[0:size, 0:64] + wide[64:size + 64, 64:128] + wide[128:size + 128, 128:192]
        mask = gates[:, :, 0:64].reshape(count * 64, 64)
        act, slope = gate_slope(pre)
        if slopes is not None:
            slopes[...] = (slope * mask).reshape(count, 64, 64)
        act = (act * mask).astype(jnp.bfloat16).reshape(count, 4, 16, 64)
        for index in range(count):
            x = first_x + index
            for half in range(2):
                pair = jnp.concatenate([act[index, 2 * half], act[index, 2 * half + 1]], axis=1)
                lanes = (x % 2 * 2 + half) * 128
                children[pl.ds(child_row + x // 2 * 16, 16), lanes:lanes + 128] = pair

    def inner_planes(scene, carry):
        for column in range(2):
            brick = scene * 2 + column
            first = 1 - column
            fine(
                xs.at[brick], first, 7, mk[pl.ds(brick * 8 + first, 7)], child, brick * 64, first,
                slope1.at[brick, pl.ds(first, 7)],
            )
        return carry

    lax.fori_loop(0, 2, inner_planes, 0)

    for copy in halos:
        copy.wait_recv()

    def near_planes(unit, carry):
        side, scene = lax.div(unit, 2), lax.rem(unit, 2)
        occupied = near[side, scene, 320:336, 0:64].astype(jnp.float32)
        after = (side == 0).astype(jnp.float32)
        for x in range(5):
            row = occupied[x + 3:x + 4] * after + occupied[x:x + 1] * (1.0 - after)
            moved = dot(kept1_ref[...], diagonal(near[side, scene, x * 64:x * 64 + 64, :]), 1, 1)
            keep1(moved, near_xs.at[unit, x + side])
            near_gate = voxel_gate(row)
            mk[32 + unit * 5 + x] = near_gate
        for x in range(2):
            gate2[16 + unit * 2 + x] = coarse_gate(32 + unit * 5 + 1 - side + 2 * x)
        return carry

    lax.fori_loop(0, 4, near_planes, 0)
    for scene in range(2):
        from_left = near[0, scene, 320:336, :].astype(jnp.float32)[8:9]
        from_right = near[1, scene, 320:336, :].astype(jnp.float32)[8:9]
        to_left = shares(from_left, rows[scene][0], has_left)
        to_right = shares(from_right, rows[scene][1], has_right)
        share_of[scene, 0], share_of[scene, 3] = to_left, to_right
        share_of[scene, 4] = [to_left[0], to_left[2], to_left[1]]
        share_of[scene, 5] = [to_right[0], to_right[2], to_right[1]]
        last = diagonal(near[0, scene, 256:320, :])
        border1(last, share_of[scene, 0], xs.at[scene * 2, 0])
        first = diagonal(near[1, scene, 0:64, :])
        border1(first, share_of[scene, 3], xs.at[scene * 2 + 1, 9])
        border1(own_plane(scene * 2, 0), share_of[scene, 4], near_xs.at[scene, 5])
        border1(own_plane(scene * 2 + 1, 7), share_of[scene, 5], near_xs.at[2 + scene, 0])

    for scene in range(2):
        brick = scene * 2
        fine(xs.at[brick], 0, 1, mk[brick * 8:brick * 8 + 1], child, brick * 64, 0, slope1.at[brick, 0:1])
        brick = scene * 2 + 1
        fine(xs.at[brick], 7, 1, mk[brick * 8 + 7:brick * 8 + 8], child, brick * 64, 7, slope1.at[brick, 7:8])

    for unit in range(4):
        first = 32 + unit * 5 + (1 if unit < 2 else 0)
        fine(near_xs.at[unit], 0, 4, mk[first:first + 4], child, 256 + unit * 32, 0, None)

    gate = gate2[...].reshape(384, 128)
    down_pre = dot(child[...], wd_ref[...], 1, 1)
    act, slope = gate_slope(down_pre)
    slope2[...] = slope[0:256] * gate[0:256]
    act2[...] = (act * gate).astype(jnp.bfloat16).reshape(24, 16, 128)

    def lanes_of(tap, step):
        first = (step * 9 + tap) * 128
        return slice(first, first + 128)

    def inner2(values, into):
        for brick in range(4):
            moved = dot(kept2_ref[:, 0:64], values[brick * 4:brick * 4 + 4].reshape(64, 128), 1, 0).astype(jnp.bfloat16)
            base = brick * 64
            for tap in range(9):
                here = moved[tap * 64:tap * 64 + 64]
                into[base + 16:base + 64, lanes_of(tap, 0)] = here[0:48]
                into[base:base + 64, lanes_of(tap, 1)] = here
                into[base:base + 48, lanes_of(tap, 2)] = here[16:64]

    def border2(values, beside, into):
        planes = []
        for scene in range(2):
            planes += [beside[0][scene], values[scene * 8 + 4], values[scene * 8 + 3], beside[1][scene]]
        moved = dot(edge2[...], jnp.concatenate(planes, axis=0), 1, 0).astype(jnp.bfloat16)
        for tap in range(9):
            for brick in range(4):
                first = tap * 128 + brick * 32
                base = brick * 64
                into[base:base + 16, lanes_of(tap, 0)] = moved[first:first + 16]
                into[base + 48:base + 64, lanes_of(tap, 2)] = moved[first + 16:first + 32]

    def near2():
        outer = [act2[16 + 4 * side:20 + 4 * side].reshape(64, 128) for side in range(2)]
        moved = [dot(kept2_ref[:, 0:64], part, 1, 0).astype(jnp.bfloat16) for part in outer]
        planes = [act2[scene * 8 + plane] for scene in range(2) for plane in (0, 7)]
        edges = dot(edge3[:, 0:64], jnp.concatenate(planes, axis=0), 1, 0).astype(jnp.bfloat16)
        for tap in range(9):
            for scene in range(2):
                first = tap * 64 + scene * 32
                base = 256 + scene * 16
                im2[base:base + 16, lanes_of(tap, 0)] = moved[0][first:first + 16]
                im2[base:base + 16, lanes_of(tap, 1)] = moved[0][first + 16:first + 32]
                im2[base:base + 16, lanes_of(tap, 2)] = edges[first:first + 16]
                im2[base + 32:base + 48, lanes_of(tap, 0)] = edges[first + 16:first + 32]
                im2[base + 32:base + 48, lanes_of(tap, 1)] = moved[1][first:first + 16]
                im2[base + 32:base + 48, lanes_of(tap, 2)] = moved[1][first + 16:first + 32]

    def edges_of(roles, count):
        lane = lax.broadcasted_iota(jnp.int32, (1, 128), 1) // 16
        shared = [jnp.zeros((1, 128), jnp.float32) for _ in range(3)]
        for index, role in enumerate(roles):
            own = (lane == index).astype(jnp.float32)
            shared = [so_far + own * part for so_far, part in zip(shared, share_of[role])]
        shared = [part.astype(jnp.bfloat16) for part in shared]
        same = lax.broadcasted_iota(jnp.int32, (count, 16, 128), 0) == lax.broadcasted_iota(jnp.int32, (count, 16, 128), 2) // 16
        same = same.astype(jnp.float32).astype(jnp.bfloat16).reshape(1, count, 16, 128)
        moves = kept8_ref[...] * shared[0] + after8_ref[...] * shared[1] + before8_ref[...] * shared[2]
        return (moves.reshape(9, 1, 16, 128) * same).reshape(9 * count * 16, 128)

    edge2[...] = edges_of([(scene, role) for scene in range(2) for role in range(4)], 8)
    edge3[...] = edges_of([(scene, role) for scene in range(2) for role in (4, 5)], 4)
    inner2(act2, im2)
    border2(act2, ([act2[17], act2[19]], [act2[20], act2[22]]), im2)
    near2()
    coarse_pre = dot(im2[...], w2_ref[...], 1, 1)
    act, slope = gate_slope(coarse_pre)
    section_ref[...] = (act[0:256] * gate[0:256]).astype(jnp.bfloat16)
    upstream = [upstream_ref[...].reshape(256, 128), near[:, :, 336:352, :].reshape(64, 128)]
    gates = [gate[0:256], gate[272:288], gate[304:320], gate[320:336], gate[352:368]]
    upstream = jnp.concatenate(upstream, axis=0).astype(jnp.float32) * jnp.concatenate(gates, axis=0)
    grad2[...] = (upstream * slope).astype(jnp.bfloat16).reshape(20, 16, 128)

    def keep_parts(values, first, width, lane_tile):
        values = values.astype(jnp.bfloat16)
        for block in range(values.shape[0] // 16):
            for column in range(values.shape[1] // 128):
                parts[first + block * width + lane_tile + column] = values[block * 16:block * 16 + 16, column * 128:column * 128 + 128]

    grad_rows = grad2[0:16].reshape(256, 128)
    for step in range(3):
        keep_parts(dot(grad_rows, im2[0:256, step * 1152:step * 1152 + 1152], 0, 0), 0, 27, step * 9)
    for chain in chains[:2]:
        chain.start(0)
    inner2(grad2, img)
    border2(grad2, ([grad2[16], grad2[17]], [grad2[18], grad2[19]]), img)
    down_back = dot(img[...], w2f[...], 1, 0)
    down_in = (down_back * slope2[...]).astype(jnp.bfloat16)
    keep_parts(dot(down_in, child[0:256], 0, 0), DOWN_AT, 4, 0)
    parts[DOWN_AT + 32:CONV1_AT] = jnp.zeros((CONV1_AT - DOWN_AT - 32, 16, 128), jnp.bfloat16)
    chains[2].start(0)

    def advance(some, stage):
        for chain in some:
            chain.finish(stage - 1)
            if stage < len(STAGES["x"]):
                chain.start(stage)

    advance(chains[:2], 1)

    fine_back = dot(down_in, wd_ref[...], 1, 0)
    for brick in range(4):
        for x in range(8):
            base = brick * 64 + x // 2 * 16
            first = x % 2 * 256
            back = [fine_back[base:base + 16, first + part * 64:first + part * 64 + 64] for part in range(4)]
            grad1[brick, x] = (jnp.concatenate(back, axis=0) * slope1[brick, x]).astype(jnp.bfloat16)
    for step in range(3):
        term = None
        for brick in range(4):
            window = xs[brick, step:step + 8].reshape(512, 640)
            part = dot(grad1[brick].reshape(512, 64), window, 0, 0)
            term = part if term is None else term + part
        keep_parts(term, CONV1_AT, 15, step * 5)
    parts[CONV1_AT + 60:TILES] = jnp.zeros((TILES - CONV1_AT - 60, 16, 128), jnp.bfloat16)
    chains[-1].start(0)

    stages = [2, 2, 1, 1]
    for index in ARRIVALS:
        advance([chains[index]], stages[index])
        stages[index] += 1
    for copy in halos:
        copy.wait_send()
    for chain in chains:
        chain.close()


def unpack_kernel(scale, section_ref, total_ref, section_out, conv1_ref, down_ref, conv2_ref):
    section_out[...] = section_ref[...]
    for block in range(8):
        rows = slice(block * 16, block * 16 + 16)
        for column in range(27):
            conv2_ref[rows, column * 128:column * 128 + 128] = total_ref[block * 27 + column].astype(jnp.float32) * scale
        for column in range(4):
            down_ref[rows, column * 128:column * 128 + 128] = total_ref[DOWN_AT + block * 4 + column].astype(jnp.float32) * scale
    for block in range(4):
        rows = slice(block * 16, block * 16 + 16)
        taps = []
        for step in range(3):
            whole = [total_ref[CONV1_AT + block * 15 + step * 5 + pair].astype(jnp.float32) * scale for pair in range(5)]
            taps += whole[:4] + [whole[4][:, 0:64]]
        conv1_ref[rows, :] = jnp.concatenate(taps, axis=1)


def per_device(tiles_in_row, scale, features, occupancy, brick_slots, conv1_weight, down_weight, conv2_weight, upstream):
    tables, table_at = selections()
    bf16, f32 = jnp.bfloat16, jnp.float32
    vmem, dma = pltpu.VMEM, pltpu.SemaphoreType.DMA
    scratch = [
        vmem((2, 2, 8, 64, 64), bf16), vmem((2, 2, 8, 64), jnp.int32), vmem(tables.shape, bf16), vmem((64, 1728), bf16),
        vmem((128, 512), bf16), vmem((128, 3456), bf16), vmem((2, 2, 4, 16, 128), bf16), dma((7,)),
        vmem((2, 2, 352, 128), bf16), vmem((2, 2, 352, 128), bf16), dma((2,)), dma((2,)),
        vmem((TILES, 16, 128), bf16), vmem((4, 10, 64, 640), bf16), vmem((4, 6, 64, 640), bf16), vmem((3, 64, 640), bf16),
        vmem((3456, 128), bf16), vmem((52, 64, 128), f32), vmem((4, 8, 64, 64), f32), vmem((384, 512), bf16),
        vmem((4, 8, 64, 64), bf16), vmem((24, 16, 128), f32), vmem((256, 128), f32), vmem((24, 16, 128), bf16),
        vmem((1152, 128), bf16), vmem((576, 128), bf16), vmem((320, 3456), bf16), vmem((256, 3456), bf16),
        vmem((20, 16, 128), bf16),
    ]
    for order, first, tiles in CHAINS:
        landing, held = Chain.sizes(order, tiles)
        scratch += [vmem(size + (16, 128), bf16) for size in landing]
        scratch += [vmem((size, 16, 128), bf16) for size in held]
    scratch += [dma((len(CHAINS), 7, 7))] * 2
    whole = pl.BlockSpec(memory_space=vmem)
    section, total = pl.pallas_call(
        functools.partial(section_kernel, tiles_in_row, table_at),
        out_shape=(jax.ShapeDtypeStruct((256, 128), bf16), jax.ShapeDtypeStruct((TILES, 16, 128), bf16)),
        in_specs=[pl.BlockSpec(memory_space=pltpu.SMEM)] + [pl.BlockSpec(memory_space=pltpu.HBM)] * 7,
        out_specs=(whole, whole),
        scratch_shapes=scratch,
        compiler_params=pltpu.CompilerParams(collective_id=0, has_side_effects=True, vmem_limit_bytes=63 * 2**20),
    )(
        brick_slots, features, occupancy, jnp.asarray(tables), conv1_weight, down_weight, conv2_weight, upstream,
    )
    section, conv1, down, conv2 = pl.pallas_call(
        functools.partial(unpack_kernel, scale),
        out_shape=(
            jax.ShapeDtypeStruct((256, 128), bf16), jax.ShapeDtypeStruct((64, 1728), f32),
            jax.ShapeDtypeStruct((128, 512), f32), jax.ShapeDtypeStruct((128, 3456), f32),
        ),
        in_specs=[whole] * 2,
        out_specs=(whole,) * 4,
        compiler_params=pltpu.CompilerParams(vmem_limit_bytes=63 * 2**20),
    )(section, total)
    return section.reshape(upstream.shape), conv1, down, conv2


def solution(mesh):
    tiles_in_row, scenes = mesh.shape["tile"], mesh.shape["dp"] * 2
    scale = 1.0 / (scenes * tiles_in_row * 2)
    wide = P("dp", "tile", None, None, None)
    return jax.shard_map(
        functools.partial(per_device, tiles_in_row, scale),
        mesh=mesh,
        in_specs=(wide, P("dp", "tile", None, None), P("dp", "tile"), P(), P(), P(), wide),
        out_specs=(wide, P(), P(), P()),
        check_vma=False,
    )
```

```python
import functools

import jax
import jax.numpy as jnp
import numpy as np
from jax import lax
from jax.experimental import pallas as pl
from jax.experimental.pallas import tpu as pltpu
from jax.sharding import PartitionSpec as P

FINE = 64
COARSE = 128
MESH = pl.DeviceIdType.MESH

AXES = {"c": 2, "x": 4, "y": 8, "z": 8}
STAGES = {
    "x": (("rs", "c"), ("rs", "x"), ("rs", "y"), ("ar", "z"), ("ag", "y"), ("ag", "x"), ("ag", "c")),
    "y": (("rs", "c"), ("rs", "y"), ("rs", "x"), ("ar", "z"), ("ag", "x"), ("ag", "y"), ("ag", "c")),
    "z": (("rs", "c"), ("rs", "z"), ("rs", "x"), ("ar", "y"), ("ag", "x"), ("ag", "z"), ("ag", "c")),
}


Y_LOW = 4


def place():
    dp, tile = lax.axis_index("dp"), lax.axis_index("tile")
    c, x, z = AXES["c"], AXES["x"], AXES["z"]
    return {
        "c": lax.rem(tile, c),
        "z": lax.rem(lax.div(tile, c), z),
        "x": lax.rem(lax.div(tile, c * z), x),
        "y": lax.div(tile, c * z * x) * Y_LOW + dp,
    }


def device(at):
    c, x, z = AXES["c"], AXES["x"], AXES["z"]
    tile = ((lax.div(at["y"], Y_LOW) * x + at["x"]) * z + at["z"]) * c + at["c"]
    return {"dp": lax.rem(at["y"], Y_LOW), "tile": tile}


def peer(at, axis, step):
    moved = dict(at)
    moved[axis] = lax.rem(at[axis] + step, AXES[axis])
    return device(moved)


def far_first(count):
    return sorted(range(1, count), key=lambda step: -min(step, count - step))


class Chain:
    def __init__(self, order, own, result, landing, held, send, recv, at, peers):
        self.stages, self.at, self.peers = STAGES[order], at, peers
        self.own, self.result, self.landing, self.held = own, result, landing, held
        self.send, self.recv = send, recv
        self.copies = {}

    @staticmethod
    def sizes(order, tiles):
        landing, held = [], []
        for kind, axis in STAGES[order]:
            if kind == "rs":
                tiles //= AXES[axis]
                landing.append((AXES[axis] - 1, tiles))
                held.append(tiles)
            elif kind == "ar":
                landing.append((AXES[axis], tiles))
        return landing, held

    def source(self, stage):
        return self.own if stage == 0 else self.held[stage - 1]

    def offset(self, stages):
        first = 0
        for stage in range(stages):
            first = first + self.at[self.stages[stage][1]] * self.held[stage].shape[0]
        return first

    def start(self, stage):
        kind, axis = self.stages[stage]
        count = AXES[axis]
        for step in far_first(count):
            if kind == "rs":
                part = self.held[stage].shape[0]
                to = lax.rem(self.at[axis] + step, count)
                src = self.source(stage).at[pl.ds(to * part, part)]
                dst = self.landing[stage].at[step - 1]
            elif kind == "ar":
                src = self.source(stage)
                dst = self.landing[stage].at[self.at[axis]]
            else:
                back = len(self.stages) - 1 - stage
                part = self.held[back].shape[0]
                where = pl.ds(self.offset(back + 1), part)
                src = dst = self.result.at[where]
            copy = pltpu.make_async_remote_copy(
                src_ref=src, dst_ref=dst,
                send_sem=self.send.at[stage, step - 1], recv_sem=self.recv.at[stage, step - 1],
                device_id=self.peers[axis, step], device_id_type=MESH,
            )
            copy.start()
            self.copies[stage, step] = copy

    def finish(self, stage):
        kind, axis = self.stages[stage]
        count = AXES[axis]
        for step in range(1, count):
            if kind == "ag":
                back = len(self.stages) - 1 - stage
                part = self.held[back].shape[0]
                origin = dict(self.at)
                origin[axis] = lax.rem(self.at[axis] + count - step, count)
                first = 0
                for earlier in range(back + 1):
                    first = first + origin[self.stages[earlier][1]] * self.held[earlier].shape[0]
                dst = self.result.at[pl.ds(first, part)]
            elif kind == "rs":
                dst = self.landing[stage].at[step - 1]
            else:
                dst = self.landing[stage].at[lax.rem(self.at[axis] + count - step, count)]
            pltpu.make_async_remote_copy(
                src_ref=dst, dst_ref=dst,
                send_sem=self.send.at[stage, step - 1], recv_sem=self.recv.at[stage, step - 1],
                device_id=self.peers[axis, step], device_id_type=MESH,
            ).wait_recv()
        if kind == "rs":
            part = self.held[stage].shape[0]
            mine = self.source(stage)[pl.ds(self.at[axis] * part, part)]
            if count == 2:
                self.held[stage][...] = mine + self.landing[stage][0]
                return
            total = mine.astype(jnp.float32)
            for step in range(1, count):
                total = total + self.landing[stage][step - 1].astype(jnp.float32)
            self.held[stage][...] = total.astype(jnp.bfloat16)
        elif kind == "ar":
            self.landing[stage][self.at[axis]] = self.source(stage)[...]
            total = self.landing[stage][0].astype(jnp.float32)
            for index in range(1, count):
                total = total + self.landing[stage][index].astype(jnp.float32)
            self.result[pl.ds(self.offset(stage), total.shape[0])] = total.astype(jnp.bfloat16)

    def close(self):
        for copy in self.copies.values():
            copy.wait_send()

DOWN_AT, CONV1_AT, TILES = 216, 256, 320
CHAINS = (("x", 0, 128), ("y", 128, 64), ("z", 192, 64), ("x", 256, 64))
ARRIVALS = (3, 0, 1, 2, 3, 1, 0, 2, 3, 1, 0, 2, 3, 1, 2, 0, 3, 1, 2, 0, 1, 3, 0, 2, 3)


def fine_selections():
    kept, after, before = np.zeros((3, 5, 64, 2, 64), np.float32)
    order = np.zeros((64, 64), np.float32)
    for y in range(8):
        for z in range(8):
            row = (y % 2) * 32 + (z % 2) * 16 + (y // 2) * 4 + z // 2
            order[row, y * 8 + z] = 1
            for tap in range(9):
                from_y, from_z = y + tap // 3 - 1, z + tap % 3 - 1
                if 0 <= from_z < 8:
                    into = kept if 0 <= from_y < 8 else after if from_y == 8 else before
                    into[tap // 2, row, tap % 2, (from_y % 8) * 8 + from_z] = 1
    return [table.reshape(320, 128) for table in (kept, after, before)] + [order]


def coarse_selections():
    kept, after, before = np.zeros((3, 9, 16, 16), np.float32)
    for y in range(4):
        for z in range(4):
            for tap in range(9):
                from_y, from_z = y + tap // 3 - 1, z + tap % 3 - 1
                if 0 <= from_z < 4:
                    into = kept if 0 <= from_y < 4 else after if from_y == 4 else before
                    into[tap, y * 4 + z, (from_y % 4) * 4 + from_z] = 1
    brick = np.einsum("tij,pq->tpiqj", kept, np.eye(4, dtype=np.float32)).reshape(576, 64)
    return [brick] + [np.tile(table.reshape(144, 16), (1, 8)) for table in (kept, after, before)]


def selections():
    tables = fine_selections() + coarse_selections()
    first = np.cumsum([0] + [table.shape[0] for table in tables])
    padded = [np.pad(table, ((0, 0), (0, 128 - table.shape[1]))) for table in tables]
    return np.concatenate(padded).astype(jnp.bfloat16), [int(place) for place in first]


def gate_slope(value):
    gate = jax.nn.sigmoid(value)
    return value * gate, gate * (1.0 + value * (1.0 - gate))


def dot(left, right, left_dim, right_dim):
    return lax.dot_general(left, right, (((left_dim,), (right_dim,)), ((), ())), preferred_element_type=jnp.float32)


def section_kernel(
    tiles_in_row, table_at,
    slots_ref, features_hbm, occupancy_hbm, tables_hbm, w1_hbm, wd_hbm, w2_hbm, upstream_hbm,
    section_ref, total_ref,
    features_ref, occupancy_ref, tables_ref, w1_ref, wd_ref, w2_ref, upstream_ref, load_sem,
    outgoing, near, halo_send, halo_recv,
    parts, xs, near_xs, w1p, w2f, mk, slope1, child, grad1, gate2, slope2, act2, edge2, edge3, im2, img, grad2,
    *scratch,
):
    loads = []
    operands = (
        (features_hbm, features_ref), (occupancy_hbm, occupancy_ref), (upstream_hbm, upstream_ref), (tables_hbm, tables_ref),
        (w1_hbm, w1_ref), (w2_hbm, w2_ref), (wd_hbm, wd_ref),
    )
    for index, (source, target) in enumerate(operands):
        loads.append(pltpu.make_async_copy(source, target, load_sem.at[index]))
        loads[-1].start()
    kept1_ref, after1_ref, before1_ref, order_ref, kept2_ref, kept8_ref, after8_ref, before8_ref = [
        tables_ref.at[first:last] for first, last in zip(table_at, table_at[1:])
    ]
    at = place()
    tile = lax.axis_index("tile")
    left, right = lax.rem(tile + tiles_in_row - 1, tiles_in_row), lax.rem(tile + 1, tiles_in_row)
    peers = {(axis, step): peer(at, axis, step) for axis, count in reversed(AXES.items()) for step in far_first(count)}
    scratch = list(scratch)
    send, recv = scratch.pop(), scratch.pop()
    chains = []
    for index, (order, first, tiles) in enumerate(CHAINS):
        landing = [scratch.pop(0) for _ in range(4)]
        held = [scratch.pop(0) for _ in range(3)]
        where = pl.ds(first, tiles)
        chains.append(Chain(order, parts.at[where], total_ref.at[where], landing, held, send.at[index], recv.at[index], at, peers))

    barrier = pltpu.get_barrier_semaphore()
    met = 0
    for other in (left, right):
        pl.semaphore_signal(barrier, inc=1, device_id={"tile": other}, device_id_type=MESH)
        met += 1
    for other in peers.values():
        pl.semaphore_signal(barrier, inc=1, device_id=other, device_id_type=MESH)
        met += 1

    def row_of(scene, column):
        return lax.rem(slots_ref[scene, column], 2).astype(jnp.float32)

    same_half = lax.broadcasted_iota(jnp.int32, (128, 128), 0) // 64 == lax.broadcasted_iota(jnp.int32, (128, 128), 1) // 64
    same_half = same_half.astype(jnp.float32).astype(jnp.bfloat16)

    def twice(plane, gate):
        plane = (plane.astype(jnp.float32) * gate).astype(jnp.bfloat16)
        return jnp.concatenate([plane, plane], axis=1)

    def diagonal(both):
        return jnp.concatenate([both, both], axis=0) * same_half

    def blocks(plane, gate):
        return diagonal(twice(plane, gate))

    def own_plane(brick, x):
        return blocks(features_ref[brick // 2, brick % 2, x], gate_row(occupancy_ref[brick // 2, brick % 2], x))

    def gate_row(occupied, x):
        return occupied[x:x + 1, :].astype(jnp.float32)

    loads[0].wait()
    loads[1].wait()
    loads[2].wait()
    for side in range(2):
        column, first_x, border = ((1, 3, 3), (0, 0, 0))[side]
        for scene in range(2):
            occupied = occupancy_ref[scene, column].astype(jnp.float32)
            for index in range(5):
                x = first_x + index
                both = twice(features_ref[scene, column, x], occupied[x:x + 1])
                outgoing[side, scene, index * 64:index * 64 + 64, :] = both
            row = jnp.full((8, 128), row_of(scene, column), jnp.float32)
            gates = jnp.concatenate([jnp.concatenate([occupied, occupied], axis=1), row], axis=0)
            outgoing[side, scene, 320:336, :] = gates.astype(jnp.bfloat16)
            outgoing[side, scene, 336:352, :] = upstream_ref[scene, column, border]
    pl.semaphore_wait(barrier, met)
    halos = []
    for side, other in enumerate((right, left)):
        copy = pltpu.make_async_remote_copy(
            src_ref=outgoing.at[side], dst_ref=near.at[side], send_sem=halo_send.at[side], recv_sem=halo_recv.at[side],
            device_id={"tile": other}, device_id_type=MESH,
        )
        copy.start()
        halos.append(copy)

    def keep1(moved, into):
        moved = moved.astype(jnp.bfloat16)
        for pair in range(5):
            into[:, pair * 128:pair * 128 + 128] = moved[pair * 64:pair * 64 + 64]

    def voxel_gate(row):
        return dot(order_ref[:, 0:64], jnp.broadcast_to(row, (128, 64)).astype(jnp.bfloat16), 1, 1)

    def coarse_gate(first):
        largest = None
        for a in range(2):
            for quarter in range(4):
                part = mk[first + a, quarter * 16:quarter * 16 + 16, :]
                largest = part if largest is None else jnp.maximum(largest, part)
        return largest

    for load in loads[3:]:
        load.wait()
    for step in range(3):
        taps = w1_ref[:, step * 576:step * 576 + 576]
        w1p[step] = jnp.concatenate([taps, jnp.zeros((64, 64), jnp.bfloat16)], axis=1)

    def local_planes(brick, carry):
        scene, column = lax.div(brick, 2), lax.rem(brick, 2)
        occupied = occupancy_ref[scene, column]
        for x in range(8):
            row = gate_row(occupied, x)
            keep1(dot(kept1_ref[...], blocks(features_ref[scene, column, x], row), 1, 1), xs.at[brick, x + 1])
            mk[brick * 8 + x] = voxel_gate(row)
        for x in range(4):
            gate2[brick * 4 + x] = coarse_gate(brick * 8 + 2 * x)
        return carry

    lax.fori_loop(0, 4, local_planes, 0)
    for tap in range(27):
        w2f[tap * 128:tap * 128 + 128, :] = w2_ref[:, (26 - tap) * 128:(26 - tap) * 128 + 128]

    def shares(from_row, to_row, valid):
        apart = from_row - to_row
        return [share * valid for share in (1.0 - apart * apart, 0.5 * apart * (apart + 1.0), 0.5 * apart * (apart - 1.0))]

    rows = [[jnp.full((1, 128), row_of(scene, column), jnp.float32) for column in range(2)] for scene in range(2)]
    has_left = (tile > 0).astype(jnp.float32)
    has_right = (tile < tiles_in_row - 1).astype(jnp.float32)

    def border1(plane, share, into):
        share = [part.astype(jnp.bfloat16) for part in share]
        moves = kept1_ref[...] * share[0] + after1_ref[...] * share[1] + before1_ref[...] * share[2]
        keep1(dot(moves, plane, 1, 1), into)

    share_of = {}
    for scene in range(2):
        share_of[scene, 1] = shares(rows[scene][1], rows[scene][0], 1.0)
        share_of[scene, 2] = shares(rows[scene][0], rows[scene][1], 1.0)
        border1(own_plane(scene * 2 + 1, 0), share_of[scene, 1], xs.at[scene * 2, 9])
        border1(own_plane(scene * 2, 7), share_of[scene, 2], xs.at[scene * 2 + 1, 0])

    def fine(source, first, count, gates, children, child_row, first_x, slopes):
        size = count * 64
        wide = dot(source[first:first + count + 2].reshape(size + 128, 640), w1p[...].reshape(192, 640), 1, 1)
        pre = wide[0:size, 0:64] + wide[64:size + 64, 64:128] + wide[128:size + 128, 128:192]
        mask = gates[:, :, 0:64].reshape(count * 64, 64)
        act, slope = gate_slope(pre)
        if slopes is not None:
            slopes[...] = (slope * mask).reshape(count, 64, 64)
        act = (act * mask).astype(jnp.bfloat16).reshape(count, 4, 16, 64)
        for index in range(count):
            x = first_x + index
            for half in range(2):
                pair = jnp.concatenate([act[index, 2 * half], act[index, 2 * half + 1]], axis=1)
                lanes = (x % 2 * 2 + half) * 128
                children[pl.ds(child_row + x // 2 * 16, 16), lanes:lanes + 128] = pair

    def inner_planes(scene, carry):
        for column in range(2):
            brick = scene * 2 + column
            first = 1 - column
            fine(
                xs.at[brick], first, 7, mk[pl.ds(brick * 8 + first, 7)], child, brick * 64, first,
                slope1.at[brick, pl.ds(first, 7)],
            )
        return carry

    lax.fori_loop(0, 2, inner_planes, 0)

    for copy in halos:
        copy.wait_recv()

    def near_planes(unit, carry):
        side, scene = lax.div(unit, 2), lax.rem(unit, 2)
        occupied = near[side, scene, 320:336, 0:64].astype(jnp.float32)
        after = (side == 0).astype(jnp.float32)
        for x in range(5):
            row = occupied[x + 3:x + 4] * after + occupied[x:x + 1] * (1.0 - after)
            moved = dot(kept1_ref[...], diagonal(near[side, scene, x * 64:x * 64 + 64, :]), 1, 1)
            keep1(moved, near_xs.at[unit, x + side])
            near_gate = voxel_gate(row)
            mk[32 + unit * 5 + x] = near_gate
        for x in range(2):
            gate2[16 + unit * 2 + x] = coarse_gate(32 + unit * 5 + 1 - side + 2 * x)
        return carry

    lax.fori_loop(0, 4, near_planes, 0)
    for scene in range(2):
        from_left = near[0, scene, 320:336, :].astype(jnp.float32)[8:9]
        from_right = near[1, scene, 320:336, :].astype(jnp.float32)[8:9]
        to_left = shares(from_left, rows[scene][0], has_left)
        to_right = shares(from_right, rows[scene][1], has_right)
        share_of[scene, 0], share_of[scene, 3] = to_left, to_right
        share_of[scene, 4] = [to_left[0], to_left[2], to_left[1]]
        share_of[scene, 5] = [to_right[0], to_right[2], to_right[1]]
        last = diagonal(near[0, scene, 256:320, :])
        border1(last, share_of[scene, 0], xs.at[scene * 2, 0])
        first = diagonal(near[1, scene, 0:64, :])
        border1(first, share_of[scene, 3], xs.at[scene * 2 + 1, 9])
        border1(own_plane(scene * 2, 0), share_of[scene, 4], near_xs.at[scene, 5])
        border1(own_plane(scene * 2 + 1, 7), share_of[scene, 5], near_xs.at[2 + scene, 0])

    for scene in range(2):
        brick = scene * 2
        fine(xs.at[brick], 0, 1, mk[brick * 8:brick * 8 + 1], child, brick * 64, 0, slope1.at[brick, 0:1])
        brick = scene * 2 + 1
        fine(xs.at[brick], 7, 1, mk[brick * 8 + 7:brick * 8 + 8], child, brick * 64, 7, slope1.at[brick, 7:8])

    for unit in range(4):
        first = 32 + unit * 5 + (1 if unit < 2 else 0)
        fine(near_xs.at[unit], 0, 4, mk[first:first + 4], child, 256 + unit * 32, 0, None)

    gate = gate2[...].reshape(384, 128)
    down_pre = dot(child[...], wd_ref[...], 1, 1)
    act, slope = gate_slope(down_pre)
    slope2[...] = slope[0:256] * gate[0:256]
    act2[...] = (act * gate).astype(jnp.bfloat16).reshape(24, 16, 128)

    def lanes_of(tap, step):
        first = (step * 9 + tap) * 128
        return slice(first, first + 128)

    def inner2(values, into):
        for brick in range(4):
            moved = dot(kept2_ref[:, 0:64], values[brick * 4:brick * 4 + 4].reshape(64, 128), 1, 0).astype(jnp.bfloat16)
            base = brick * 64
            for tap in range(9):
                here = moved[tap * 64:tap * 64 + 64]
                into[base + 16:base + 64, lanes_of(tap, 0)] = here[0:48]
                into[base:base + 64, lanes_of(tap, 1)] = here
                into[base:base + 48, lanes_of(tap, 2)] = here[16:64]

    def border2(values, beside, into):
        planes = []
        for scene in range(2):
            planes += [beside[0][scene], values[scene * 8 + 4], values[scene * 8 + 3], beside[1][scene]]
        moved = dot(edge2[...], jnp.concatenate(planes, axis=0), 1, 0).astype(jnp.bfloat16)
        for tap in range(9):
            for brick in range(4):
                first = tap * 128 + brick * 32
                base = brick * 64
                into[base:base + 16, lanes_of(tap, 0)] = moved[first:first + 16]
                into[base + 48:base + 64, lanes_of(tap, 2)] = moved[first + 16:first + 32]

    def near2():
        outer = [act2[16 + 4 * side:20 + 4 * side].reshape(64, 128) for side in range(2)]
        moved = [dot(kept2_ref[:, 0:64], part, 1, 0).astype(jnp.bfloat16) for part in outer]
        planes = [act2[scene * 8 + plane] for scene in range(2) for plane in (0, 7)]
        edges = dot(edge3[:, 0:64], jnp.concatenate(planes, axis=0), 1, 0).astype(jnp.bfloat16)
        for tap in range(9):
            for scene in range(2):
                first = tap * 64 + scene * 32
                base = 256 + scene * 16
                im2[base:base + 16, lanes_of(tap, 0)] = moved[0][first:first + 16]
                im2[base:base + 16, lanes_of(tap, 1)] = moved[0][first + 16:first + 32]
                im2[base:base + 16, lanes_of(tap, 2)] = edges[first:first + 16]
                im2[base + 32:base + 48, lanes_of(tap, 0)] = edges[first + 16:first + 32]
                im2[base + 32:base + 48, lanes_of(tap, 1)] = moved[1][first:first + 16]
                im2[base + 32:base + 48, lanes_of(tap, 2)] = moved[1][first + 16:first + 32]

    def edges_of(roles, count):
        lane = lax.broadcasted_iota(jnp.int32, (1, 128), 1) // 16
        shared = [jnp.zeros((1, 128), jnp.float32) for _ in range(3)]
        for index, role in enumerate(roles):
            own = (lane == index).astype(jnp.float32)
            shared = [so_far + own * part for so_far, part in zip(shared, share_of[role])]
        shared = [part.astype(jnp.bfloat16) for part in shared]
        same = lax.broadcasted_iota(jnp.int32, (count, 16, 128), 0) == lax.broadcasted_iota(jnp.int32, (count, 16, 128), 2) // 16
        same = same.astype(jnp.float32).astype(jnp.bfloat16).reshape(1, count, 16, 128)
        moves = kept8_ref[...] * shared[0] + after8_ref[...] * shared[1] + before8_ref[...] * shared[2]
        return (moves.reshape(9, 1, 16, 128) * same).reshape(9 * count * 16, 128)

    edge2[...] = edges_of([(scene, role) for scene in range(2) for role in range(4)], 8)
    edge3[...] = edges_of([(scene, role) for scene in range(2) for role in (4, 5)], 4)
    inner2(act2, im2)
    border2(act2, ([act2[17], act2[19]], [act2[20], act2[22]]), im2)
    near2()
    coarse_pre = dot(im2[...], w2_ref[...], 1, 1)
    act, slope = gate_slope(coarse_pre)
    section_ref[...] = (act[0:256] * gate[0:256]).astype(jnp.bfloat16)
    upstream = [upstream_ref[...].reshape(256, 128), near[:, :, 336:352, :].reshape(64, 128)]
    gates = [gate[0:256], gate[272:288], gate[304:320], gate[320:336], gate[352:368]]
    upstream = jnp.concatenate(upstream, axis=0).astype(jnp.float32) * jnp.concatenate(gates, axis=0)
    grad2[...] = (upstream * slope).astype(jnp.bfloat16).reshape(20, 16, 128)

    def keep_parts(values, first, width, lane_tile):
        values = values.astype(jnp.bfloat16)
        for block in range(values.shape[0] // 16):
            for column in range(values.shape[1] // 128):
                parts[first + block * width + lane_tile + column] = values[block * 16:block * 16 + 16, column * 128:column * 128 + 128]

    grad_rows = grad2[0:16].reshape(256, 128)
    for step in range(3):
        keep_parts(dot(grad_rows, im2[0:256, step * 1152:step * 1152 + 1152], 0, 0), 0, 27, step * 9)
    for chain in chains[:2]:
        chain.start(0)
    inner2(grad2, img)
    border2(grad2, ([grad2[16], grad2[17]], [grad2[18], grad2[19]]), img)
    down_back = dot(img[...], w2f[...], 1, 0)
    down_in = (down_back * slope2[...]).astype(jnp.bfloat16)
    keep_parts(dot(down_in, child[0:256], 0, 0), DOWN_AT, 4, 0)
    parts[DOWN_AT + 32:CONV1_AT] = jnp.zeros((CONV1_AT - DOWN_AT - 32, 16, 128), jnp.bfloat16)
    chains[2].start(0)

    def advance(some, stage):
        for chain in some:
            chain.finish(stage - 1)
            if stage < len(STAGES["x"]):
                chain.start(stage)

    advance(chains[:2], 1)

    fine_back = dot(down_in, wd_ref[...], 1, 0)
    for brick in range(4):
        for x in range(8):
            base = brick * 64 + x // 2 * 16
            first = x % 2 * 256
            back = [fine_back[base:base + 16, first + part * 64:first + part * 64 + 64] for part in range(4)]
            grad1[brick, x] = (jnp.concatenate(back, axis=0) * slope1[brick, x]).astype(jnp.bfloat16)
    advance(chains[2:3], 1)
    for step in range(3):
        term = None
        for brick in range(4):
            window = xs[brick, step:step + 8].reshape(512, 640)
            part = dot(grad1[brick].reshape(512, 64), window, 0, 0)
            term = part if term is None else term + part
        keep_parts(term, CONV1_AT, 15, step * 5)
    parts[CONV1_AT + 60:TILES] = jnp.zeros((TILES - CONV1_AT - 60, 16, 128), jnp.bfloat16)
    chains[-1].start(0)

    stages = [2, 2, 2, 1]
    for index in ARRIVALS:
        advance([chains[index]], stages[index])
        stages[index] += 1
    for copy in halos:
        copy.wait_send()
    for chain in chains:
        chain.close()


def unpack_kernel(scale, section_ref, total_ref, section_out, conv1_ref, down_ref, conv2_ref):
    section_out[...] = section_ref[...]
    for block in range(8):
        rows = slice(block * 16, block * 16 + 16)
        for column in range(27):
            conv2_ref[rows, column * 128:column * 128 + 128] = total_ref[block * 27 + column].astype(jnp.float32) * scale
        for column in range(4):
            down_ref[rows, column * 128:column * 128 + 128] = total_ref[DOWN_AT + block * 4 + column].astype(jnp.float32) * scale
    for block in range(4):
        rows = slice(block * 16, block * 16 + 16)
        taps = []
        for step in range(3):
            whole = [total_ref[CONV1_AT + block * 15 + step * 5 + pair].astype(jnp.float32) * scale for pair in range(5)]
            taps += whole[:4] + [whole[4][:, 0:64]]
        conv1_ref[rows, :] = jnp.concatenate(taps, axis=1)


def per_device(tiles_in_row, scale, features, occupancy, brick_slots, conv1_weight, down_weight, conv2_weight, upstream):
    tables, table_at = selections()
    bf16, f32 = jnp.bfloat16, jnp.float32
    vmem, dma = pltpu.VMEM, pltpu.SemaphoreType.DMA
    scratch = [
        vmem((2, 2, 8, 64, 64), bf16), vmem((2, 2, 8, 64), jnp.int32), vmem(tables.shape, bf16), vmem((64, 1728), bf16),
        vmem((128, 512), bf16), vmem((128, 3456), bf16), vmem((2, 2, 4, 16, 128), bf16), dma((7,)),
        vmem((2, 2, 352, 128), bf16), vmem((2, 2, 352, 128), bf16), dma((2,)), dma((2,)),
        vmem((TILES, 16, 128), bf16), vmem((4, 10, 64, 640), bf16), vmem((4, 6, 64, 640), bf16), vmem((3, 64, 640), bf16),
        vmem((3456, 128), bf16), vmem((52, 64, 128), f32), vmem((4, 8, 64, 64), f32), vmem((384, 512), bf16),
        vmem((4, 8, 64, 64), bf16), vmem((24, 16, 128), f32), vmem((256, 128), f32), vmem((24, 16, 128), bf16),
        vmem((1152, 128), bf16), vmem((576, 128), bf16), vmem((320, 3456), bf16), vmem((256, 3456), bf16),
        vmem((20, 16, 128), bf16),
    ]
    for order, first, tiles in CHAINS:
        landing, held = Chain.sizes(order, tiles)
        scratch += [vmem(size + (16, 128), bf16) for size in landing]
        scratch += [vmem((size, 16, 128), bf16) for size in held]
    scratch += [dma((len(CHAINS), 7, 7))] * 2
    whole = pl.BlockSpec(memory_space=vmem)
    section, total = pl.pallas_call(
        functools.partial(section_kernel, tiles_in_row, table_at),
        out_shape=(jax.ShapeDtypeStruct((256, 128), bf16), jax.ShapeDtypeStruct((TILES, 16, 128), bf16)),
        in_specs=[pl.BlockSpec(memory_space=pltpu.SMEM)] + [pl.BlockSpec(memory_space=pltpu.HBM)] * 7,
        out_specs=(whole, whole),
        scratch_shapes=scratch,
        compiler_params=pltpu.CompilerParams(collective_id=0, has_side_effects=True, vmem_limit_bytes=63 * 2**20),
    )(
        brick_slots, features, occupancy, jnp.asarray(tables), conv1_weight, down_weight, conv2_weight, upstream,
    )
    section, conv1, down, conv2 = pl.pallas_call(
        functools.partial(unpack_kernel, scale),
        out_shape=(
            jax.ShapeDtypeStruct((256, 128), bf16), jax.ShapeDtypeStruct((64, 1728), f32),
            jax.ShapeDtypeStruct((128, 512), f32), jax.ShapeDtypeStruct((128, 3456), f32),
        ),
        in_specs=[whole] * 2,
        out_specs=(whole,) * 4,
        compiler_params=pltpu.CompilerParams(vmem_limit_bytes=63 * 2**20),
    )(section, total)
    return section.reshape(upstream.shape), conv1, down, conv2


def solution(mesh):
    tiles_in_row, scenes = mesh.shape["tile"], mesh.shape["dp"] * 2
    scale = 1.0 / (scenes * tiles_in_row * 2)
    wide = P("dp", "tile", None, None, None)
    return jax.shard_map(
        functools.partial(per_device, tiles_in_row, scale),
        mesh=mesh,
        in_specs=(wide, P("dp", "tile", None, None), P("dp", "tile"), P(), P(), P(), wide),
        out_specs=(wide, P(), P(), P()),
        check_vma=False,
    )
```
